32 devices in a mesh: section: 4 (over x, core), seq: 4 (over z), head: 2 (over y).
Axes of the slice: x: 2, y: 2, z: 4, core: 2. Of those that a mesh axis runs over, the one named last changes fastest.
Arguments:
- queries: bfloat16 [4, 512, 1536], P('section', 'seq', 'head'), may hold values from -240 to 240
- grad_out: bfloat16 [4, 512, 1536], P('section', 'seq', 'head'), may hold values from -96 to 96
- keys: bfloat16 [4, 256, 768], P('section', 'seq', 'head'), may hold values from -6 to 6
- values: bfloat16 [4, 256, 768], P('section', 'seq', 'head'), may hold values from -6 to 6
- proj_query: bfloat16 [4, 5376, 1536], P('section', None, 'head'), may hold values from -0.15625 to 0.15625
- section_span: int32 [4], replicated, may hold values from 0 to 3, each once
- span_prefix: int32 [4], replicated, may hold values from 128 to 256, as said below
Outputs:
- grad_input: bfloat16 [4, 5376, 512], P('section', 'head', 'seq')
- grad_key: bfloat16 [4, 256, 768], P('section', 'seq', 'head')
- grad_value: bfloat16 [4, 256, 768], P('section', 'seq', 'head')
The draws below stay inside these ranges and needn't reach their ends.
Inputs may be any that keep to these rules, and one draw needn't show every extreme that they name: `span_prefix`: some entry equals 256 in every draw.
All inputs are finite; a program needn't handle non-finite values.
Results may differ from the reference program's by a relative error of at most 0.023.
Values may be sent and summed in bfloat16 or wider, within the bound.
No kernel may reach another device: no remote copies, remote signals or barrier semaphores. Data moves between devices by JAX's collectives and lax.ppermute only.
A program may use at most 64 MiB of HBM per device.

```python
import jax
import jax.numpy as jnp
from jax import lax

D = 5376
HD = 128
Q_DEV = 128
KV_HEADS = 6
QH = 12
ROWS = 512
PREFIX = 256
SECTIONS = 4
N_SEQ = 4


def draw_pair(key):
    base_q = jax.random.truncated_normal(jax.random.fold_in(key, 11), -6.0, 6.0, (SECTIONS, ROWS, QH * HD), jnp.float32)
    base_k = jax.random.truncated_normal(jax.random.fold_in(key, 12), -6.0, 6.0, (SECTIONS, PREFIX, KV_HEADS * HD), jnp.float32)
    return (base_q, base_k)


def draw_queries(key, part):
    return draw_pair(key)[0].astype(jnp.bfloat16)


def draw_keys(key, part):
    return draw_pair(key)[1].astype(jnp.bfloat16)


def draw_span_prefix(key, part):
    lengths = jax.random.randint(jax.random.fold_in(key, 21), (SECTIONS,), PREFIX // 2, PREFIX + 1)
    where_full = jax.random.randint(jax.random.fold_in(key, 22), (), 0, SECTIONS)
    return jnp.where(jnp.arange(SECTIONS) == where_full, PREFIX, lengths).astype(jnp.int32)


def block_scale(key, extent, pieces, low, high):
    loudness = 1.0
    for axis_at, shards_of in pieces:
        draws = jax.random.uniform(jax.random.fold_in(jax.random.fold_in(key, 6), axis_at), (shards_of,), jnp.float32, low / len(pieces), high / len(pieces))
        loudness = loudness * jnp.repeat(jnp.exp(draws), extent[axis_at] // shards_of).reshape((-1,) + (1,) * (len(extent) - 1 - axis_at))
    return loudness


def gaussian(key, shape, width, most, pieces=(), kind=jnp.bfloat16):
    entries = width * jax.random.normal(key, shape, jnp.float32)
    if pieces:
        entries = entries * block_scale(key, shape, pieces, -0.22, 0.18)
    return jnp.clip(entries, -most, most).astype(kind)


def setup_inputs(seed: int = 0) -> dict:
    key_list = jax.random.split(jax.random.key(seed), 8)
    return {
        "queries": draw_queries(jax.random.fold_in(key_list[7], 71), 0),
        "grad_out": gaussian(key_list[1], (SECTIONS, ROWS, QH * HD), 16.0, 96.0, ((0, 4), (1, 4), (2, 2))),
        "keys": draw_keys(jax.random.fold_in(key_list[7], 71), 0),
        "values": gaussian(key_list[3], (SECTIONS, PREFIX, KV_HEADS * HD), 1.0, 6.0, ((0, 4), (1, 4), (2, 2))),
        "proj_query": gaussian(key_list[4], (SECTIONS, D, QH * HD), (QH * HD) ** -0.5, 0.15625, ((0, 4), (2, 2))),
        "section_span": jax.random.permutation(key_list[5], SECTIONS).astype(jnp.int32),
        "span_prefix": draw_span_prefix(jax.random.fold_in(key_list[7], 71), 0),
    }


query_scale = 168.0 ** -0.5


def to_groups(matrix):
    count = matrix.shape[1] // (2 * HD)
    return matrix.reshape(matrix.shape[0], count, 2, HD).transpose(1, 2, 0, 3).reshape(count, 2 * matrix.shape[0], HD)


def from_groups(stacked):
    count = stacked.shape[0]
    rows_half = stacked.shape[1] // 2
    return stacked.reshape(count, 2, rows_half, HD).transpose(2, 0, 1, 3).reshape(rows_half, count * 2 * HD)


def kv_groups(matrix):
    return matrix.reshape(matrix.shape[0], matrix.shape[1] // HD, HD).transpose(1, 0, 2)


def kv_flat(stacked):
    return stacked.transpose(1, 0, 2).reshape(stacked.shape[1], stacked.shape[0] * HD)


def contract_rows(left, right):
    return lax.dot_general(left, right, (((0,), (0,)), ((), ())), preferred_element_type=jnp.float32)


def group_pass(q_group, d_group, k_group, v_group, live):
    scores = query_scale * jnp.dot(q_group, k_group.T, preferred_element_type=jnp.float32)
    scores = jnp.where(live[None, :], scores, jnp.float32(-1e30))
    top = jnp.max(scores, axis=1, keepdims=True)
    lse = top + jnp.log(jnp.sum(jnp.exp(scores - top), axis=1, keepdims=True))
    probs = jnp.where(live[None, :], jnp.exp(scores - lse), jnp.float32(0.0))
    probs_low = probs.astype(jnp.bfloat16)
    attn = jnp.dot(probs_low, v_group, preferred_element_type=jnp.float32)
    delta = jnp.sum(d_group.astype(jnp.float32) * attn, axis=1, keepdims=True)
    dprobs = jnp.dot(d_group, v_group.T, preferred_element_type=jnp.float32)
    dscores = (probs * (dprobs - delta)).astype(jnp.bfloat16)
    grad_q = (query_scale * jnp.dot(dscores, k_group, preferred_element_type=jnp.float32)).astype(jnp.bfloat16)
    grad_k = query_scale * contract_rows(dscores, q_group)
    grad_v = contract_rows(probs_low, d_group)
    return grad_q, grad_k, grad_v


def rounded(matrix):
    return lax.optimization_barrier(matrix.astype(jnp.bfloat16)).astype(jnp.float32)


def reference(queries, grad_out, keys, values, proj_query, section_span, span_prefix):
    incoming = jnp.roll(grad_out, -1, axis=0)

    def one_section(index):
        length = span_prefix[section_span[index]]
        live = jnp.arange(PREFIX, dtype=jnp.int32) < length
        k_groups = kv_groups(keys[index])
        v_groups = kv_groups(values[index])
        q_section = queries[index]
        d_section = incoming[index]

        def one_block(totals, block):
            start = (block * Q_DEV).astype(jnp.int32)
            q_groups = to_groups(lax.dynamic_slice_in_dim(q_section, start, Q_DEV, 0))
            d_groups = to_groups(lax.dynamic_slice_in_dim(d_section, start, Q_DEV, 0))

            def per_group(members):
                return group_pass(members[0], members[1], members[2], members[3], live)

            grad_q, grad_k, grad_v = lax.map(per_group, (q_groups, d_groups, k_groups, v_groups))
            key_sum = totals[0] + rounded(kv_flat(grad_k))
            value_sum = totals[1] + rounded(kv_flat(grad_v))
            return (key_sum, value_sum), from_groups(grad_q)

        zeros = jnp.zeros((PREFIX, KV_HEADS * HD), jnp.float32)
        totals, blocks = lax.scan(one_block, (zeros, zeros), jnp.arange(N_SEQ, dtype=jnp.int32))
        grad_query = blocks.reshape(ROWS, QH * HD)
        grad_input = lax.dot_general(proj_query[index], grad_query, (((1,), (1,)), ((), ())), preferred_element_type=jnp.float32)
        return grad_input.astype(jnp.bfloat16), totals[0].astype(jnp.bfloat16), totals[1].astype(jnp.bfloat16)

    grad_input, grad_key, grad_value = lax.map(one_section, jnp.arange(SECTIONS, dtype=jnp.int32))
    return grad_input, grad_key, grad_value
```

```python
import functools

import jax
import jax.numpy as jnp
from jax import lax
from jax.experimental import pallas as pl
from jax.experimental.pallas import tpu as pltpu
from jax.sharding import PartitionSpec as P

HD = 128
MOST_ROTATIONS = 4
VMEM_LIMIT = 48 * 1024 * 1024

query_scale = 168.0 ** (-0.5)


def shifted(block, axis, distance):
    devices = range(lax.axis_size(axis))
    route = [((i - distance) % len(devices), i) for i in devices]
    return lax.ppermute(block, axis, route)


def dot(left, right, left_dim, right_dim):
    return lax.dot_general(
        left, right, (((left_dim,), (right_dim,)), ((), ())), preferred_element_type=jnp.float32
    )


def attention_kernel(n_blocks, n_seq, n_head, parts, span, prefix, *refs):
    q_ref, d_ref = refs[:2]
    k_refs = refs[2 : 2 + n_blocks]
    v_refs = refs[2 + n_blocks : 2 + 2 * n_blocks]
    w_ref = refs[2 + 2 * n_blocks]
    outs = refs[3 + 2 * n_blocks :]
    grad_ref = outs[0]
    term_refs = outs[1 : 1 + n_blocks]
    n_parts = (n_head - 1) * parts
    part_refs = outs[1 + n_blocks : 1 + n_blocks + n_parts]
    w_held, w_sem = outs[1 + n_blocks + n_parts :]

    section = lax.axis_index("section")
    seq = lax.axis_index("seq")
    head = lax.axis_index("head")
    feats = w_ref.shape[1] // n_head

    copies = []
    for r in range(1, n_head):
        start = pl.multiple_of(lax.rem(head + r, n_head) * feats, 16)
        copy = pltpu.make_async_copy(
            w_ref.at[0, pl.ds(start, feats), :], w_held.at[r - 1], w_sem.at[r - 1]
        )
        copy.start()
        copies.append(copy)

    live = prefix[span[section]]
    held = k_refs[0].shape[1]
    spots = []
    for r in range(n_blocks):
        first = lax.rem(seq - r + n_seq, n_seq) * held if n_blocks > 1 else 0
        spots.append(first + lax.broadcasted_iota(jnp.int32, (held, 1), 0))
    alive = jnp.concatenate(spots, axis=0) < live

    groups = k_refs[0].shape[2] // HD
    rows = q_ref.shape[1]
    for g in range(groups):
        cols = slice(g * HD, (g + 1) * HD)
        two = [slice((2 * g + i) * HD, (2 * g + i + 1) * HD) for i in range(2)]
        q = jnp.concatenate([q_ref[0, :, c] for c in two], axis=0)
        d = jnp.concatenate([d_ref[0, :, c] for c in two], axis=0)
        k = jnp.concatenate([ref[0, :, cols] for ref in k_refs], axis=0)
        v = jnp.concatenate([ref[0, :, cols] for ref in v_refs], axis=0)
        scores = query_scale * dot(k, q, 1, 1)
        scores = jnp.where(alive, scores, jnp.float32(-1e30))
        top = jnp.max(scores, axis=0, keepdims=True)
        probs = jnp.exp(scores - top)
        probs = probs * (1.0 / jnp.sum(probs, axis=0, keepdims=True))
        probs_low = probs.astype(jnp.bfloat16)
        dprobs = dot(v, d, 1, 1)
        delta = jnp.sum(probs_low.astype(jnp.float32) * dprobs, axis=0, keepdims=True)
        dscores = (probs * (dprobs - delta)).astype(jnp.bfloat16)
        grad_q = (query_scale * dot(k, dscores, 0, 0)).astype(jnp.bfloat16)
        for i in range(2):
            grad_ref[two[i], :] = grad_q[:, i * rows : (i + 1) * rows]
        grad_k = (query_scale * dot(dscores, q, 1, 0)).astype(jnp.bfloat16)
        grad_v = dot(probs_low, d, 1, 0).astype(jnp.bfloat16)
        width = groups * HD
        for r in range(n_blocks):
            own = slice(r * held, (r + 1) * held)
            term_refs[r][:, cols] = grad_k[own]
            term_refs[r][:, width + g * HD : width + (g + 1) * HD] = grad_v[own]

    step = feats // parts
    for r in range(1, n_head):
        copies[r - 1].wait()
        for p in range(parts):
            block = w_held[r - 1, p * step : (p + 1) * step, :]
            part_refs[(r - 1) * parts + p][...] = dot(block, grad_ref[...], 1, 0).astype(
                jnp.bfloat16
            )


def own_kernel(n_head, grad_ref, w_ref, out_ref, w_held, w_sem):
    feats = w_ref.shape[1] // n_head
    start = pl.multiple_of(lax.axis_index("head") * feats, 16)
    copy = pltpu.make_async_copy(w_ref.at[0, pl.ds(start, feats), :], w_held, w_sem)
    copy.start()
    copy.wait()
    out_ref[...] = dot(w_held[...], grad_ref[...], 1, 0)


def input_sum_kernel(parts, own_ref, *refs):
    *arrived, out_ref = refs
    step = own_ref.shape[0] // parts
    for p in range(parts):
        at = slice(p * step, (p + 1) * step)
        total = own_ref[at, :]
        for ref in arrived[p::parts]:
            total = total + ref[...].astype(jnp.float32)
        out_ref[0, at, :] = total.astype(jnp.bfloat16)


def term_sum_kernel(*refs):
    *terms, key_ref, value_ref = refs
    total = terms[0][...].astype(jnp.float32)
    for ref in terms[1:]:
        total = total + ref[...].astype(jnp.float32)
    low = total.astype(jnp.bfloat16)
    half = low.shape[1] // 2
    key_ref[0] = low[:, :half]
    value_ref[0] = low[:, half:]


VMEM = pl.BlockSpec(memory_space=pltpu.VMEM)
SMEM = pl.BlockSpec(memory_space=pltpu.SMEM)
ANY = pl.BlockSpec(memory_space=pl.ANY)


def on_device(queries, grad_out, keys, values, proj_query, section_span, span_prefix):
    n_seq, n_head = lax.axis_size("seq"), lax.axis_size("head")
    rotate = n_seq <= MOST_ROTATIONS
    parts = 1
    low = jnp.bfloat16
    _, held, kv_width = keys.shape
    _, rows, width = queries.shape
    feats = proj_query.shape[1] // n_head

    incoming = shifted(grad_out, "section", -1)
    if rotate:
        key_blocks = [keys] + [shifted(keys, "seq", r) for r in range(1, n_seq)]
        value_blocks = [values] + [shifted(values, "seq", r) for r in range(1, n_seq)]
    else:
        key_blocks = [lax.all_gather(keys, "seq", axis=1, tiled=True)]
        value_blocks = [lax.all_gather(values, "seq", axis=1, tiled=True)]
    n_blocks = len(key_blocks)
    block_rows = key_blocks[0].shape[1]

    n_parts = (n_head - 1) * parts
    out = pl.pallas_call(
        functools.partial(attention_kernel, n_blocks, n_seq, n_head, parts),
        out_shape=[jax.ShapeDtypeStruct((width, rows), low)]
        + [jax.ShapeDtypeStruct((block_rows, 2 * kv_width), low)] * n_blocks
        + [jax.ShapeDtypeStruct((feats // parts, rows), low)] * n_parts,
        in_specs=[SMEM] * 2 + [VMEM] * (2 + 2 * n_blocks) + [ANY],
        out_specs=[VMEM] * (1 + n_blocks + n_parts),
        scratch_shapes=[
            pltpu.VMEM((max(n_head - 1, 1), feats, width), low),
            pltpu.SemaphoreType.DMA((max(n_head - 1, 1),)),
        ],
        compiler_params=pltpu.CompilerParams(vmem_limit_bytes=VMEM_LIMIT),
        name="attention",
    )(section_span, span_prefix, queries, incoming, *key_blocks, *value_blocks, proj_query)
    grad_query, terms, products = out[0], out[1 : 1 + n_blocks], out[1 + n_blocks :]

    arrived = [
        shifted(products[(r - 1) * parts + p], "head", r)
        for r in range(1, n_head)
        for p in range(parts)
    ]
    if rotate:
        all_terms = [terms[0]] + [shifted(terms[r], "seq", -r) for r in range(1, n_seq)]
    else:
        all_terms = [lax.psum_scatter(terms[0], "seq", scatter_dimension=0, tiled=True)]

    own = pl.pallas_call(
        functools.partial(own_kernel, n_head),
        out_shape=jax.ShapeDtypeStruct((feats, rows), jnp.float32),
        in_specs=[VMEM, ANY],
        out_specs=VMEM,
        scratch_shapes=[pltpu.VMEM((feats, width), low), pltpu.SemaphoreType.DMA(())],
        compiler_params=pltpu.CompilerParams(vmem_limit_bytes=VMEM_LIMIT),
        name="own_rows",
    )(grad_query, proj_query)

    kv_shape = jax.ShapeDtypeStruct((1, held, kv_width), low)
    grad_key, grad_value = pl.pallas_call(
        term_sum_kernel,
        out_shape=[kv_shape, kv_shape],
        in_specs=[VMEM] * len(all_terms),
        out_specs=[VMEM, VMEM],
        name="term_sum",
    )(*all_terms)
    grad_input = pl.pallas_call(
        functools.partial(input_sum_kernel, parts),
        out_shape=jax.ShapeDtypeStruct((1, feats, rows), low),
        in_specs=[VMEM] * (1 + len(arrived)),
        out_specs=VMEM,
        compiler_params=pltpu.CompilerParams(vmem_limit_bytes=VMEM_LIMIT),
        name="input_sum",
    )(own, *arrived)
    return (grad_input, grad_key, grad_value)


def solution(mesh):
    in_specs = (
        P("section", "seq", "head"),
        P("section", "seq", "head"),
        P("section", "seq", "head"),
        P("section", "seq", "head"),
        P("section", None, "head"),
        P(),
        P(),
    )
    out_specs = (
        P("section", "head", "seq"),
        P("section", "seq", "head"),
        P("section", "seq", "head"),
    )
    return jax.shard_map(
        on_device, mesh=mesh, in_specs=in_specs, out_specs=out_specs, check_vma=False
    )
```

```python
import functools
import math

import jax
import jax.numpy as jnp
from jax import lax
from jax.experimental import pallas as pl
from jax.experimental.pallas import tpu as pltpu
from jax.sharding import PartitionSpec as P

HD = 128
MOST_PARTNERS = 4
VMEM_LIMIT = 40 * 1024 * 1024

query_scale = 168.0 ** (-0.5)
exp2_scale = query_scale * math.log2(math.e)


def shifted(block, axis, distance):
    devices = range(lax.axis_size(axis))
    route = [((i - distance) % len(devices), i) for i in devices]
    return lax.ppermute(block, axis, route)


def swapped(block, axis, distance):
    return lax.ppermute(block, axis, [(i, i ^ distance) for i in range(lax.axis_size(axis))])


def dot(left, right, left_dim, right_dim):
    return lax.dot_general(
        left, right, (((left_dim,), (right_dim,)), ((), ())), preferred_element_type=jnp.float32
    )


def copied(pairs, sems):
    copies = [pltpu.make_async_copy(a, b, sems.at[i]) for i, (a, b) in enumerate(pairs)]
    for copy in copies:
        copy.start()
    for copy in copies:
        copy.wait()


def stage_kernel(n_head, span, prefix, q_ref, w_ref, limit_out, q_out, own_out, *refs):
    *other_outs, sems = refs
    feats = own_out.shape[0]
    head = lax.axis_index("head")
    pairs = [(q_ref.at[0], q_out)]
    for r, out in enumerate([own_out, *other_outs]):
        start = pl.multiple_of(lax.rem(head + r, n_head) * feats, 16)
        pairs.append((w_ref.at[0, pl.ds(start, feats), :], out))
    live = prefix[span[lax.axis_index("section")]]
    limit_out[...] = jnp.full(limit_out.shape, live, jnp.int32)
    copied(pairs, sems)


def attention_kernel(n_blocks, n_other, limit_ref, q_ref, d_ref, *refs):
    kv_refs = refs[:n_blocks]
    w_refs = refs[n_blocks : n_blocks + n_other]
    outs = refs[n_blocks + n_other :]
    grad_ref = outs[0]
    term_refs = outs[1 : 1 + n_blocks]
    part_refs = outs[1 + n_blocks :]

    held, both = kv_refs[0].shape
    width = both // 2
    seq = lax.axis_index("seq")
    spots = []
    for r in range(n_blocks):
        first = jnp.bitwise_xor(seq, r) * held if n_blocks > 1 else 0
        spots.append(first + lax.broadcasted_iota(jnp.int32, (held, 1), 0))
    alive = jnp.concatenate(spots, axis=0) < limit_ref[0:1, 0:1]

    groups = width // HD
    rows = q_ref.shape[0]
    for g in range(groups):
        two = [slice((2 * g + i) * HD, (2 * g + i + 1) * HD) for i in range(2)]
        k_cols = slice(g * HD, (g + 1) * HD)
        v_cols = slice(width + g * HD, width + (g + 1) * HD)
        q = jnp.concatenate([q_ref[:, c] for c in two], axis=0)
        d = jnp.concatenate([d_ref[0, :, c] for c in two], axis=0)
        k = jnp.concatenate([ref[:, k_cols] for ref in kv_refs], axis=0)
        v = jnp.concatenate([ref[:, v_cols] for ref in kv_refs], axis=0)
        scores = jnp.where(alive, dot(k, q, 1, 1), jnp.float32(-1e30))
        dprobs = dot(v, d, 1, 1)
        top = jnp.max(scores, axis=0, keepdims=True)
        probs = jnp.exp2((scores - top) * exp2_scale)
        probs = probs * (1.0 / jnp.sum(probs, axis=0, keepdims=True))
        probs_low = probs.astype(jnp.bfloat16)
        delta = jnp.sum(probs_low.astype(jnp.float32) * dprobs, axis=0, keepdims=True)
        dscores = (probs * (dprobs - delta)).astype(jnp.bfloat16)
        grad_q = (query_scale * dot(k, dscores, 0, 0)).astype(jnp.bfloat16)
        for i in range(2):
            grad_ref[two[i], :] = grad_q[:, i * rows : (i + 1) * rows]
        grad_k = (query_scale * dot(dscores, q, 1, 0)).astype(jnp.bfloat16)
        grad_v = dot(probs_low, d, 1, 0).astype(jnp.bfloat16)
        for r in range(n_blocks):
            own = slice(r * held, (r + 1) * held)
            term_refs[r][:, k_cols] = grad_k[own]
            term_refs[r][:, v_cols] = grad_v[own]

    for w_ref, part_ref in zip(w_refs, part_refs):
        part_ref[...] = dot(w_ref[...], grad_ref[...], 1, 0).astype(jnp.bfloat16)


def own_kernel(grad_ref, w_ref, out_ref):
    out_ref[...] = dot(w_ref[...], grad_ref[...], 1, 0)


def input_sum_kernel(own_ref, *refs):
    *arrived, out_ref = refs
    total = own_ref[...]
    for ref in arrived:
        total = total + ref[...].astype(jnp.float32)
    out_ref[0] = total.astype(jnp.bfloat16)


def term_sum_kernel(*refs):
    *terms, key_ref, value_ref = refs
    total = terms[0][...].astype(jnp.float32)
    for ref in terms[1:]:
        total = total + ref[...].astype(jnp.float32)
    low = total.astype(jnp.bfloat16)
    half = low.shape[1] // 2
    key_ref[0] = low[:, :half]
    value_ref[0] = low[:, half:]


VMEM = pl.BlockSpec(memory_space=pltpu.VMEM)
SMEM = pl.BlockSpec(memory_space=pltpu.SMEM)
HBM = pl.BlockSpec(memory_space=pltpu.HBM)


def kernel_call(body, name, out_shape, in_specs, scratch=(), limit=VMEM_LIMIT):
    return pl.pallas_call(
        body,
        out_shape=out_shape,
        in_specs=in_specs,
        out_specs=jax.tree.map(lambda _: VMEM, out_shape),
        scratch_shapes=list(scratch),
        compiler_params=pltpu.CompilerParams(vmem_limit_bytes=limit),
        name=name,
    )


def on_device(queries, grad_out, keys, values, proj_query, section_span, span_prefix):
    n_seq, n_head = lax.axis_size("seq"), lax.axis_size("head")
    n_other = n_head - 1
    direct = n_seq <= MOST_PARTNERS and n_seq & (n_seq - 1) == 0
    low = jnp.bfloat16
    _, held, kv_width = keys.shape
    _, rows, width = queries.shape
    feats = proj_query.shape[1] // n_head

    def shape(*dims, dtype=low):
        return jax.ShapeDtypeStruct(dims, dtype)

    joined = jnp.concatenate([keys[0], values[0]], axis=1)
    incoming = shifted(grad_out, "section", -1)
    if direct:
        blocks = [joined] + [swapped(joined, "seq", r) for r in range(1, n_seq)]
    else:
        blocks = [lax.all_gather(joined, "seq", axis=0, tiled=True)]
    n_blocks = len(blocks)

    limit, q, w_own, *w_other = kernel_call(
        functools.partial(stage_kernel, n_head),
        "stage",
        [shape(8, HD, dtype=jnp.int32), shape(rows, width)] + [shape(feats, width)] * n_head,
        [SMEM] * 2 + [HBM] * 2,
        [pltpu.SemaphoreType.DMA((1 + n_head,))],
    )(
        section_span,
        span_prefix,
        pltpu.with_memory_space_constraint(queries, pltpu.HBM),
        pltpu.with_memory_space_constraint(proj_query, pltpu.HBM),
    )

    out = kernel_call(
        functools.partial(attention_kernel, n_blocks, n_other),
        "attention",
        [shape(width, rows)]
        + [shape(*blocks[0].shape)] * n_blocks
        + [shape(feats, rows)] * n_other,
        [VMEM] * (3 + n_blocks + n_other),
    )(limit, q, incoming, *blocks, *w_other)
    grad_query, terms, products = out[0], out[1 : 1 + n_blocks], out[1 + n_blocks :]
    arrived = [shifted(part, "head", r + 1) for r, part in enumerate(products)]
    if direct:
        all_terms = [terms[0]] + [swapped(terms[r], "seq", r) for r in range(1, n_seq)]
    else:
        all_terms = [lax.psum_scatter(terms[0], "seq", scatter_dimension=0, tiled=True)]

    own = kernel_call(own_kernel, "own", shape(feats, rows, dtype=jnp.float32), [VMEM] * 2)(
        grad_query, w_own
    )
    grad_key, grad_value = kernel_call(
        term_sum_kernel, "term_sum", [shape(1, held, kv_width)] * 2, [VMEM] * len(all_terms)
    )(*all_terms)
    grad_input = kernel_call(
        input_sum_kernel, "input_sum", shape(1, feats, rows), [VMEM] * (1 + len(arrived))
    )(own, *arrived)
    return (grad_input, grad_key, grad_value)


def solution(mesh):
    in_specs = (
        P("section", "seq", "head"),
        P("section", "seq", "head"),
        P("section", "seq", "head"),
        P("section", "seq", "head"),
        P("section", None, "head"),
        P(),
        P(),
    )
    out_specs = (
        P("section", "head", "seq"),
        P("section", "seq", "head"),
        P("section", "seq", "head"),
    )
    return jax.shard_map(
        on_device, mesh=mesh, in_specs=in_specs, out_specs=out_specs, check_vma=False
    )
```

```python
import functools
import math

import jax
import jax.numpy as jnp
from jax import lax
from jax.experimental import pallas as pl
from jax.experimental.pallas import tpu as pltpu
from jax.sharding import PartitionSpec as P

HD = 128
MOST_PARTNERS = 4
VMEM_LIMIT = 40 * 1024 * 1024

query_scale = 168.0 ** (-0.5)
exp2_scale = query_scale * math.log2(math.e)


def shifted(block, axis, distance):
    devices = range(lax.axis_size(axis))
    route = [((i - distance) % len(devices), i) for i in devices]
    return lax.ppermute(block, axis, route)


def swapped(block, axis, distance):
    return lax.ppermute(block, axis, [(i, i ^ distance) for i in range(lax.axis_size(axis))])


def dot(left, right, left_dim, right_dim):
    return lax.dot_general(
        left, right, (((left_dim,), (right_dim,)), ((), ())), preferred_element_type=jnp.float32
    )


def in_hbm(x):
    return pltpu.with_memory_space_constraint(x, pltpu.HBM)


def stage_kernel(n_head, span_ref, prefix_ref, q_ref, w_ref, limit_out, q_out, *refs):
    *other_outs, span, prefix, sems, small_sems = refs
    feats = w_ref.shape[1] // n_head
    head = lax.axis_index("head")
    copies = []
    for r, out in enumerate(other_outs):
        start = pl.multiple_of(lax.rem(head + r + 1, n_head) * feats, 16)
        copies.append((w_ref.at[0, pl.ds(start, feats), :], out))
    copies.append((q_ref.at[0], q_out))
    copies = [pltpu.make_async_copy(a, b, sems.at[i]) for i, (a, b) in enumerate(copies)]
    small = [
        pltpu.make_async_copy(a, b, small_sems.at[i])
        for i, (a, b) in enumerate([(span_ref, span), (prefix_ref, prefix)])
    ]
    for copy in small + copies:
        copy.start()
    for copy in small:
        copy.wait()
    live = prefix[span[lax.axis_index("section")]]
    limit_out[...] = jnp.full(limit_out.shape, live, jnp.int32)
    for copy in copies:
        copy.wait()


def pair_of(ref, g, lead=()):
    cols = [slice((2 * g + i) * HD, (2 * g + i + 1) * HD) for i in range(2)]
    return jnp.concatenate([ref[lead + (slice(None), c)] for c in cols], axis=0)


def attention_kernel(n_blocks, n_other, limit_ref, q_ref, d_ref, *refs):
    kv_refs = refs[:n_blocks]
    w_refs = refs[n_blocks : n_blocks + n_other]
    grad_ref, probs_ref, dscores_ref, *part_refs = refs[n_blocks + n_other :]

    held, both = kv_refs[0].shape
    width = both // 2
    seq = lax.axis_index("seq")
    spots = []
    for r in range(n_blocks):
        first = jnp.bitwise_xor(seq, r) * held if n_blocks > 1 else 0
        spots.append(first + lax.broadcasted_iota(jnp.int32, (held, 1), 0))
    alive = jnp.concatenate(spots, axis=0) < limit_ref[0:1, 0:1]

    rows = q_ref.shape[0]
    for g in range(width // HD):
        k_cols = slice(g * HD, (g + 1) * HD)
        v_cols = slice(width + g * HD, width + (g + 1) * HD)
        q = pair_of(q_ref, g)
        d = pair_of(d_ref, g, (0,))
        k = jnp.concatenate([ref[:, k_cols] for ref in kv_refs], axis=0)
        v = jnp.concatenate([ref[:, v_cols] for ref in kv_refs], axis=0)
        scores = jnp.where(alive, dot(k, q, 1, 1), jnp.float32(-1e30))
        dprobs = dot(v, d, 1, 1)
        top = jnp.max(scores, axis=0, keepdims=True)
        probs = jnp.exp2((scores - top) * exp2_scale)
        probs = probs * (1.0 / jnp.sum(probs, axis=0, keepdims=True))
        probs_low = probs.astype(jnp.bfloat16)
        delta = jnp.sum(probs_low.astype(jnp.float32) * dprobs, axis=0, keepdims=True)
        dscores = (probs * (dprobs - delta)).astype(jnp.bfloat16)
        probs_ref[g] = probs_low
        dscores_ref[g] = dscores
        grad_q = (query_scale * dot(k, dscores, 0, 0)).astype(jnp.bfloat16)
        for i in range(2):
            spot = (2 * g + i) * HD
            grad_ref[spot : spot + HD, :] = grad_q[:, i * rows : (i + 1) * rows]

    for w_ref, part_ref in zip(w_refs, part_refs):
        part_ref[...] = dot(w_ref[...], grad_ref[...], 1, 0).astype(jnp.bfloat16)


def terms_kernel(probs_ref, dscores_ref, q_ref, d_ref, *term_refs):
    held, both = term_refs[0].shape
    width = both // 2
    for g in range(width // HD):
        grad_k = (query_scale * dot(dscores_ref[g], pair_of(q_ref, g), 1, 0)).astype(jnp.bfloat16)
        grad_v = dot(probs_ref[g], pair_of(d_ref, g, (0,)), 1, 0).astype(jnp.bfloat16)
        for r, ref in enumerate(term_refs):
            block = slice(r * held, (r + 1) * held)
            ref[:, g * HD : (g + 1) * HD] = grad_k[block]
            ref[:, width + g * HD : width + (g + 1) * HD] = grad_v[block]


def own_kernel(n_head, grad_ref, w_ref, out_ref, w_held, sem):
    feats = out_ref.shape[0]
    start = pl.multiple_of(lax.axis_index("head") * feats, 16)
    copy = pltpu.make_async_copy(w_ref.at[0, pl.ds(start, feats), :], w_held, sem)
    copy.start()
    copy.wait()
    out_ref[...] = dot(w_held[...], grad_ref[...], 1, 0)


def input_sum_kernel(own_ref, *refs):
    *arrived, out_ref = refs
    total = own_ref[...]
    for ref in arrived:
        total = total + ref[...].astype(jnp.float32)
    out_ref[0] = total.astype(jnp.bfloat16)


def term_sum_kernel(*refs):
    *terms, key_ref, value_ref = refs
    total = terms[0][...].astype(jnp.float32)
    for ref in terms[1:]:
        total = total + ref[...].astype(jnp.float32)
    low = total.astype(jnp.bfloat16)
    half = low.shape[1] // 2
    key_ref[0] = low[:, :half]
    value_ref[0] = low[:, half:]


VMEM = pl.BlockSpec(memory_space=pltpu.VMEM)
HBM = pl.BlockSpec(memory_space=pltpu.HBM)


def kernel_call(body, name, out_shape, in_specs, scratch=(), limit=VMEM_LIMIT):
    return pl.pallas_call(
        body,
        out_shape=out_shape,
        in_specs=in_specs,
        out_specs=jax.tree.map(lambda _: VMEM, out_shape),
        scratch_shapes=list(scratch),
        compiler_params=pltpu.CompilerParams(vmem_limit_bytes=limit),
        name=name,
    )


def on_device(queries, grad_out, keys, values, proj_query, section_span, span_prefix):
    n_seq, n_head = lax.axis_size("seq"), lax.axis_size("head")
    n_other = n_head - 1
    direct = n_seq <= MOST_PARTNERS and n_seq & (n_seq - 1) == 0
    low = jnp.bfloat16
    _, held, kv_width = keys.shape
    _, rows, width = queries.shape
    feats = proj_query.shape[1] // n_head

    def shape(*dims, dtype=low):
        return jax.ShapeDtypeStruct(dims, dtype)

    joined = jnp.concatenate([keys[0], values[0]], axis=1)
    incoming = shifted(grad_out, "section", -1)
    if direct:
        blocks = [joined] + [swapped(joined, "seq", r) for r in range(1, n_seq)]
    else:
        blocks = [lax.all_gather(joined, "seq", axis=0, tiled=True)]
    n_blocks = len(blocks)

    limit, q, *w_other = kernel_call(
        functools.partial(stage_kernel, n_head),
        "stage",
        [shape(8, HD, dtype=jnp.int32), shape(rows, width)] + [shape(feats, width)] * n_other,
        [HBM] * 4,
        [
            pltpu.SMEM(section_span.shape, jnp.int32),
            pltpu.SMEM(span_prefix.shape, jnp.int32),
            pltpu.SemaphoreType.DMA((1 + n_other,)),
            pltpu.SemaphoreType.DMA((2,)),
        ],
    )(*[in_hbm(x) for x in (section_span, span_prefix, queries, proj_query)])

    prefix = n_blocks * blocks[0].shape[0]
    weights = shape(kv_width // HD, prefix, 2 * rows)
    grad_query, probs, dscores, *products = kernel_call(
        functools.partial(attention_kernel, n_blocks, n_other),
        "attention",
        [shape(width, rows), weights, weights] + [shape(feats, rows)] * n_other,
        [VMEM] * (3 + n_blocks + n_other),
    )(limit, q, incoming, *blocks, *w_other)
    arrived = [shifted(part, "head", r + 1) for r, part in enumerate(products)]
    terms = kernel_call(
        terms_kernel, "terms", [shape(*blocks[0].shape)] * n_blocks, [VMEM] * 4
    )(probs, dscores, q, incoming)
    if direct:
        all_terms = [terms[0]] + [swapped(terms[r], "seq", r) for r in range(1, n_seq)]
    else:
        all_terms = [lax.psum_scatter(terms[0], "seq", scatter_dimension=0, tiled=True)]

    own = kernel_call(
        functools.partial(own_kernel, n_head),
        "own",
        shape(feats, rows, dtype=jnp.float32),
        [VMEM, HBM],
        [pltpu.VMEM((feats, width), low), pltpu.SemaphoreType.DMA(())],
    )(grad_query, in_hbm(proj_query))
    grad_key, grad_value = kernel_call(
        term_sum_kernel, "term_sum", [shape(1, held, kv_width)] * 2, [VMEM] * len(all_terms)
    )(*all_terms)
    grad_input = kernel_call(
        input_sum_kernel, "input_sum", shape(1, feats, rows), [VMEM] * (1 + len(arrived))
    )(own, *arrived)
    return (grad_input, grad_key, grad_value)


def solution(mesh):
    in_specs = (
        P("section", "seq", "head"),
        P("section", "seq", "head"),
        P("section", "seq", "head"),
        P("section", "seq", "head"),
        P("section", None, "head"),
        P(),
        P(),
    )
    out_specs = (
        P("section", "head", "seq"),
        P("section", "seq", "head"),
        P("section", "seq", "head"),
    )
    return jax.shard_map(
        on_device, mesh=mesh, in_specs=in_specs, out_specs=out_specs, check_vma=False
    )
```

```python
import functools
import math

import jax
import jax.numpy as jnp
from jax import lax
from jax.experimental import pallas as pl
from jax.experimental.pallas import tpu as pltpu
from jax.sharding import PartitionSpec as P

HD = 128
MOST_PARTNERS = 4
VMEM_LIMIT = 40 * 1024 * 1024

query_scale = 168.0 ** (-0.5)
exp2_scale = query_scale * math.log2(math.e)


def shifted(block, axis, distance):
    devices = range(lax.axis_size(axis))
    route = [((i - distance) % len(devices), i) for i in devices]
    return lax.ppermute(block, axis, route)


def swapped(block, axis, distance):
    return lax.ppermute(block, axis, [(i, i ^ distance) for i in range(lax.axis_size(axis))])


def dot(left, right, left_dim, right_dim):
    return lax.dot_general(
        left, right, (((left_dim,), (right_dim,)), ((), ())), preferred_element_type=jnp.float32
    )


def in_hbm(x):
    return pltpu.with_memory_space_constraint(x, pltpu.HBM)


def join_kernel(n_copies, key_ref, value_ref, grad_ref, *refs):
    *outs, sems = refs
    grad_outs = outs[n_copies:]
    width, rows = key_ref.shape[2], grad_outs[0].shape[0]
    pairs = []
    for out in outs[:n_copies]:
        pairs += [(key_ref.at[0], out.at[:, :width]), (value_ref.at[0], out.at[:, width:])]
    for i, out in enumerate(grad_outs):
        pairs.append((grad_ref.at[0, i * rows : (i + 1) * rows, :], out))
    copies = [pltpu.make_async_copy(a, b, sems.at[i]) for i, (a, b) in enumerate(pairs)]
    for copy in copies:
        copy.start()
    for copy in copies:
        copy.wait()


def stage_kernel(n_head, span_ref, prefix_ref, q_ref, w_ref, limit_out, q_out, *refs):
    *other_outs, span, prefix, sems, small_sems = refs
    feats = w_ref.shape[1] // n_head
    head = lax.axis_index("head")
    copies = []
    for r, out in enumerate(other_outs):
        start = pl.multiple_of(lax.rem(head + r + 1, n_head) * feats, 16)
        copies.append((w_ref.at[0, pl.ds(start, feats), :], out))
    copies.append((q_ref.at[0], q_out))
    copies = [pltpu.make_async_copy(a, b, sems.at[i]) for i, (a, b) in enumerate(copies)]
    small = [
        pltpu.make_async_copy(a, b, small_sems.at[i])
        for i, (a, b) in enumerate([(span_ref, span), (prefix_ref, prefix)])
    ]
    for copy in small + copies:
        copy.start()
    for copy in small:
        copy.wait()
    live = prefix[span[lax.axis_index("section")]]
    limit_out[...] = jnp.full(limit_out.shape, live, jnp.int32)
    for copy in copies:
        copy.wait()


def pair_of(refs, g):
    cols = [slice((2 * g + i) * HD, (2 * g + i + 1) * HD) for i in range(2)]
    return jnp.concatenate([ref[:, c] for c in cols for ref in refs], axis=0)


def attention_kernel(partners, n_other, limit_ref, q_ref, *refs):
    n_blocks = 1 + len(partners)
    kv_refs = refs[:n_blocks]
    d_low, d_high, *refs = refs[n_blocks:]
    w_refs = refs[:n_other]
    grad_ref, probs_ref, dscores_ref, *part_refs = refs[n_other:]

    held, both = kv_refs[0].shape
    width = both // 2
    seq = lax.axis_index("seq")
    spots = []
    for r in [0, *partners]:
        first = jnp.bitwise_xor(seq, r) * held if partners else 0
        spots.append(first + lax.broadcasted_iota(jnp.int32, (held, 1), 0))
    alive = jnp.concatenate(spots, axis=0) < limit_ref[0:1, 0:1]

    rows = q_ref.shape[0]
    for g in range(width // HD):
        k_cols = slice(g * HD, (g + 1) * HD)
        v_cols = slice(width + g * HD, width + (g + 1) * HD)
        q = pair_of((q_ref,), g)
        d = pair_of((d_low, d_high), g)
        k = jnp.concatenate([ref[:, k_cols] for ref in kv_refs], axis=0)
        v = jnp.concatenate([ref[:, v_cols] for ref in kv_refs], axis=0)
        scores = jnp.where(alive, dot(k, q, 1, 1), jnp.float32(-1e30))
        dprobs = dot(v, d, 1, 1)
        top = jnp.max(scores, axis=0, keepdims=True)
        probs = jnp.exp2((scores - top) * exp2_scale)
        probs = probs * (1.0 / jnp.sum(probs, axis=0, keepdims=True))
        probs_low = probs.astype(jnp.bfloat16)
        delta = jnp.sum(probs_low.astype(jnp.float32) * dprobs, axis=0, keepdims=True)
        dscores = (probs * (dprobs - delta)).astype(jnp.bfloat16)
        probs_ref[g] = probs_low
        dscores_ref[g] = dscores
        grad_q = (query_scale * dot(k, dscores, 0, 0)).astype(jnp.bfloat16)
        for i in range(2):
            spot = (2 * g + i) * HD
            grad_ref[spot : spot + HD, :] = grad_q[:, i * rows : (i + 1) * rows]

    for w_ref, part_ref in zip(w_refs, part_refs):
        part_ref[...] = dot(w_ref[...], grad_ref[...], 1, 0).astype(jnp.bfloat16)


def terms_kernel(probs_ref, dscores_ref, q_ref, d_low, d_high, *term_refs):
    held, both = term_refs[0].shape
    width = both // 2
    for g in range(width // HD):
        grad_k = (query_scale * dot(dscores_ref[g], pair_of((q_ref,), g), 1, 0)).astype(jnp.bfloat16)
        grad_v = dot(probs_ref[g], pair_of((d_low, d_high), g), 1, 0).astype(jnp.bfloat16)
        for r, ref in enumerate(term_refs):
            block = slice(r * held, (r + 1) * held)
            ref[:, g * HD : (g + 1) * HD] = grad_k[block]
            ref[:, width + g * HD : width + (g + 1) * HD] = grad_v[block]


def own_kernel(n_head, grad_ref, w_ref, out_ref, w_held, sem):
    feats = out_ref.shape[0]
    start = pl.multiple_of(lax.axis_index("head") * feats, 16)
    copy = pltpu.make_async_copy(w_ref.at[0, pl.ds(start, feats), :], w_held, sem)
    copy.start()
    copy.wait()
    out_ref[...] = dot(w_held[...], grad_ref[...], 1, 0)


def input_sum_kernel(own_ref, *refs):
    *arrived, out_ref = refs
    total = own_ref[...]
    for ref in arrived:
        total = total + ref[...].astype(jnp.float32)
    out_ref[0] = total.astype(jnp.bfloat16)


def term_sum_kernel(*refs):
    *terms, key_ref, value_ref = refs
    total = terms[0][...].astype(jnp.float32)
    for ref in terms[1:]:
        total = total + ref[...].astype(jnp.float32)
    low = total.astype(jnp.bfloat16)
    half = low.shape[1] // 2
    key_ref[0] = low[:, :half]
    value_ref[0] = low[:, half:]


VMEM = pl.BlockSpec(memory_space=pltpu.VMEM)
HBM = pl.BlockSpec(memory_space=pltpu.HBM)


def kernel_call(body, name, out_shape, in_specs, scratch=(), limit=VMEM_LIMIT):
    return pl.pallas_call(
        body,
        out_shape=out_shape,
        in_specs=in_specs,
        out_specs=jax.tree.map(lambda _: VMEM, out_shape),
        scratch_shapes=list(scratch),
        compiler_params=pltpu.CompilerParams(vmem_limit_bytes=limit),
        name=name,
    )


def on_device(queries, grad_out, keys, values, proj_query, section_span, span_prefix):
    n_seq, n_head = lax.axis_size("seq"), lax.axis_size("head")
    n_other = n_head - 1
    direct = n_seq <= MOST_PARTNERS and n_seq & (n_seq - 1) == 0
    low = jnp.bfloat16
    _, held, kv_width = keys.shape
    _, rows, width = queries.shape
    feats = proj_query.shape[1] // n_head

    def shape(*dims, dtype=low):
        return jax.ShapeDtypeStruct(dims, dtype)

    partners = sorted(range(1, n_seq), key=lambda r: -r.bit_length()) if direct else []
    n_copies = 1 + len(partners)
    *joined, grad_low, grad_high = kernel_call(
        functools.partial(join_kernel, n_copies),
        "join",
        [shape(held, 2 * kv_width)] * n_copies + [shape(rows // 2, width)] * 2,
        [HBM] * 3,
        [pltpu.SemaphoreType.DMA((2 * n_copies + 2,))],
    )(*[in_hbm(x) for x in (keys, values, grad_out)])
    if direct:
        blocks = joined[:1] + [swapped(x, "seq", r) for x, r in zip(joined[1:], partners)]
    else:
        blocks = [lax.all_gather(joined[0], "seq", axis=0, tiled=True)]
    n_blocks = len(blocks)
    incoming = [shifted(part, "section", -1) for part in (grad_low, grad_high)]

    limit, q, *w_other = kernel_call(
        functools.partial(stage_kernel, n_head),
        "stage",
        [shape(8, HD, dtype=jnp.int32), shape(rows, width)] + [shape(feats, width)] * n_other,
        [HBM] * 4,
        [
            pltpu.SMEM(section_span.shape, jnp.int32),
            pltpu.SMEM(span_prefix.shape, jnp.int32),
            pltpu.SemaphoreType.DMA((1 + n_other,)),
            pltpu.SemaphoreType.DMA((2,)),
        ],
    )(*[in_hbm(x) for x in (section_span, span_prefix, queries, proj_query)])

    prefix = n_blocks * blocks[0].shape[0]
    weights = shape(kv_width // HD, prefix, 2 * rows)
    grad_query, probs, dscores, *products = kernel_call(
        functools.partial(attention_kernel, partners, n_other),
        "attention",
        [shape(width, rows), weights, weights] + [shape(feats, rows)] * n_other,
        [VMEM] * (4 + n_blocks + n_other),
    )(limit, q, *blocks, *incoming, *w_other)
    arrived = [shifted(part, "head", r + 1) for r, part in enumerate(products)]
    terms = kernel_call(
        terms_kernel, "terms", [shape(*blocks[0].shape)] * n_blocks, [VMEM] * 5
    )(probs, dscores, q, *incoming)
    if direct:
        all_terms = [terms[0]] + [swapped(x, "seq", r) for x, r in zip(terms[1:], partners)]
    else:
        all_terms = [lax.psum_scatter(terms[0], "seq", scatter_dimension=0, tiled=True)]

    own = kernel_call(
        functools.partial(own_kernel, n_head),
        "own",
        shape(feats, rows, dtype=jnp.float32),
        [VMEM, HBM],
        [pltpu.VMEM((feats, width), low), pltpu.SemaphoreType.DMA(())],
    )(grad_query, in_hbm(proj_query))
    grad_key, grad_value = kernel_call(
        term_sum_kernel, "term_sum", [shape(1, held, kv_width)] * 2, [VMEM] * len(all_terms)
    )(*all_terms)
    grad_input = kernel_call(
        input_sum_kernel, "input_sum", shape(1, feats, rows), [VMEM] * (1 + len(arrived))
    )(own, *arrived)
    return (grad_input, grad_key, grad_value)


def solution(mesh):
    in_specs = (
        P("section", "seq", "head"),
        P("section", "seq", "head"),
        P("section", "seq", "head"),
        P("section", "seq", "head"),
        P("section", None, "head"),
        P(),
        P(),
    )
    out_specs = (
        P("section", "head", "seq"),
        P("section", "seq", "head"),
        P("section", "seq", "head"),
    )
    return jax.shard_map(
        on_device, mesh=mesh, in_specs=in_specs, out_specs=out_specs, check_vma=False
    )
```

```python
import functools
import math

import jax
import jax.numpy as jnp
from jax import lax
from jax.experimental import pallas as pl
from jax.experimental.pallas import tpu as pltpu
from jax.sharding import PartitionSpec as P

HD = 128
MOST_PARTNERS = 4
VMEM_LIMIT = 40 * 1024 * 1024

query_scale = 168.0 ** (-0.5)
exp2_scale = query_scale * math.log2(math.e)


def shifted(block, axis, distance):
    devices = range(lax.axis_size(axis))
    route = [((i - distance) % len(devices), i) for i in devices]
    return lax.ppermute(block, axis, route)


def swapped(block, axis, distance):
    return lax.ppermute(block, axis, [(i, i ^ distance) for i in range(lax.axis_size(axis))])


def dot(left, right, left_dim, right_dim):
    return lax.dot_general(
        left, right, (((left_dim,), (right_dim,)), ((), ())), preferred_element_type=jnp.float32
    )


def in_hbm(x):
    return pltpu.with_memory_space_constraint(x, pltpu.HBM)


def join_kernel(n_copies, key_ref, value_ref, grad_ref, *refs):
    *outs, grad_low, grad_high, sems = refs
    width, rows = key_ref.shape[2], grad_low.shape[0]
    pairs = [
        (key_ref.at[0], outs[0].at[:, :width]),
        (value_ref.at[0], outs[0].at[:, width:]),
        (grad_ref.at[0, :rows, :], grad_low),
        (grad_ref.at[0, rows:, :], grad_high),
    ]
    copies = [pltpu.make_async_copy(a, b, sems.at[i]) for i, (a, b) in enumerate(pairs)]
    for copy in copies:
        copy.start()
    for copy in copies[:2]:
        copy.wait()
    for out in outs[1:]:
        out[...] = outs[0][...]
    for copy in copies[2:]:
        copy.wait()


def stage_kernel(n_head, span_ref, prefix_ref, q_ref, w_ref, limit_out, q_out, *refs):
    *other_outs, span, prefix, sems, small_sems = refs
    feats = w_ref.shape[1] // n_head
    head = lax.axis_index("head")
    copies = []
    for r, out in enumerate(other_outs):
        start = pl.multiple_of(lax.rem(head + r + 1, n_head) * feats, 16)
        copies.append((w_ref.at[0, pl.ds(start, feats), :], out))
    copies.append((q_ref.at[0], q_out))
    copies = [pltpu.make_async_copy(a, b, sems.at[i]) for i, (a, b) in enumerate(copies)]
    small = [
        pltpu.make_async_copy(a, b, small_sems.at[i])
        for i, (a, b) in enumerate([(span_ref, span), (prefix_ref, prefix)])
    ]
    for copy in small + copies:
        copy.start()
    for copy in small:
        copy.wait()
    live = prefix[span[lax.axis_index("section")]]
    limit_out[...] = jnp.full(limit_out.shape, live, jnp.int32)
    for copy in copies:
        copy.wait()


def pair_of(refs, g):
    cols = [slice((2 * g + i) * HD, (2 * g + i + 1) * HD) for i in range(2)]
    return jnp.concatenate([ref[:, c] for c in cols for ref in refs], axis=0)


def attention_kernel(eager, late, n_other, limit_ref, q_ref, *refs):
    partners = [*eager, *late]
    pair_refs = refs[: 2 * len(eager)]
    refs = refs[2 * len(eager) :]
    kv_refs = refs[: 1 + len(late)]
    d_low, d_high, *refs = refs[1 + len(late) :]
    w_refs = refs[:n_other]
    grad_ref, probs_ref, dscores_ref, *part_refs = refs[n_other:]

    held, both = kv_refs[0].shape
    width = both // 2
    seq = lax.axis_index("seq")
    spots = []
    for r in [0, *partners]:
        first = jnp.bitwise_xor(seq, r) * held if partners else 0
        spots.append(first + lax.broadcasted_iota(jnp.int32, (held, 1), 0))
    alive = jnp.concatenate(spots, axis=0) < limit_ref[0:1, 0:1]

    rows = q_ref.shape[0]
    for g in range(width // HD):
        k_cols = slice(g * HD, (g + 1) * HD)
        v_cols = slice(width + g * HD, width + (g + 1) * HD)
        q = pair_of((q_ref,), g)
        d = pair_of((d_low, d_high), g)
        k = [ref[:, k_cols] for ref in kv_refs]
        v = [ref[:, v_cols] for ref in kv_refs]
        k[1:1] = [ref[0, :, k_cols] for ref in pair_refs[::2]]
        v[1:1] = [ref[0, :, k_cols] for ref in pair_refs[1::2]]
        k, v = jnp.concatenate(k, axis=0), jnp.concatenate(v, axis=0)
        scores = jnp.where(alive, dot(k, q, 1, 1), jnp.float32(-1e30))
        dprobs = dot(v, d, 1, 1)
        top = jnp.max(scores, axis=0, keepdims=True)
        probs = jnp.exp2((scores - top) * exp2_scale)
        probs = probs * (1.0 / jnp.sum(probs, axis=0, keepdims=True))
        probs_low = probs.astype(jnp.bfloat16)
        delta = jnp.sum(probs_low.astype(jnp.float32) * dprobs, axis=0, keepdims=True)
        dscores = (probs * (dprobs - delta)).astype(jnp.bfloat16)
        probs_ref[g] = probs_low
        dscores_ref[g] = dscores
        grad_q = (query_scale * dot(k, dscores, 0, 0)).astype(jnp.bfloat16)
        for i in range(2):
            spot = (2 * g + i) * HD
            grad_ref[spot : spot + HD, :] = grad_q[:, i * rows : (i + 1) * rows]

    for w_ref, part_ref in zip(w_refs, part_refs):
        block = w_ref[: part_ref.shape[0], :]
        part_ref[...] = dot(block, grad_ref[...], 1, 0).astype(jnp.bfloat16)


def rest_kernel(n_other, grad_ref, *refs):
    for w_ref, part_ref in zip(refs[:n_other], refs[n_other:]):
        block = w_ref[w_ref.shape[0] - part_ref.shape[0] :, :]
        part_ref[...] = dot(block, grad_ref[...], 1, 0).astype(jnp.bfloat16)


def terms_kernel(probs_ref, dscores_ref, q_ref, d_low, d_high, *term_refs):
    held, both = term_refs[0].shape
    width = both // 2
    for g in range(width // HD):
        grad_k = (query_scale * dot(dscores_ref[g], pair_of((q_ref,), g), 1, 0)).astype(jnp.bfloat16)
        grad_v = dot(probs_ref[g], pair_of((d_low, d_high), g), 1, 0).astype(jnp.bfloat16)
        for r, ref in enumerate(term_refs):
            block = slice(r * held, (r + 1) * held)
            ref[:, g * HD : (g + 1) * HD] = grad_k[block]
            ref[:, width + g * HD : width + (g + 1) * HD] = grad_v[block]


def own_kernel(n_head, grad_ref, w_ref, out_ref, w_held, sem):
    feats = out_ref.shape[0]
    start = pl.multiple_of(lax.axis_index("head") * feats, 16)
    copy = pltpu.make_async_copy(w_ref.at[0, pl.ds(start, feats), :], w_held, sem)
    copy.start()
    copy.wait()
    out_ref[...] = dot(w_held[...], grad_ref[...], 1, 0)


def input_sum_kernel(own_ref, *refs):
    *arrived, out_ref = refs
    half = len(arrived) // 2
    split = arrived[0].shape[0]
    for at, parts in (
        (slice(0, split), arrived[:half]),
        (slice(split, own_ref.shape[0]), arrived[half:]),
    ):
        total = own_ref[at, :]
        for ref in parts:
            total = total + ref[...].astype(jnp.float32)
        out_ref[0, at, :] = total.astype(jnp.bfloat16)


def term_sum_kernel(*refs):
    *terms, key_ref, value_ref = refs
    total = terms[0][...].astype(jnp.float32)
    for ref in terms[1:]:
        total = total + ref[...].astype(jnp.float32)
    low = total.astype(jnp.bfloat16)
    half = low.shape[1] // 2
    key_ref[0] = low[:, :half]
    value_ref[0] = low[:, half:]


VMEM = pl.BlockSpec(memory_space=pltpu.VMEM)
HBM = pl.BlockSpec(memory_space=pltpu.HBM)


def kernel_call(body, name, out_shape, in_specs, scratch=(), limit=VMEM_LIMIT):
    return pl.pallas_call(
        body,
        out_shape=out_shape,
        in_specs=in_specs,
        out_specs=jax.tree.map(lambda _: VMEM, out_shape),
        scratch_shapes=list(scratch),
        compiler_params=pltpu.CompilerParams(vmem_limit_bytes=limit),
        name=name,
    )


def on_device(queries, grad_out, keys, values, proj_query, section_span, span_prefix):
    n_seq, n_head = lax.axis_size("seq"), lax.axis_size("head")
    n_other = n_head - 1
    direct = n_seq <= MOST_PARTNERS and n_seq & (n_seq - 1) == 0
    low = jnp.bfloat16
    _, held, kv_width = keys.shape
    _, rows, width = queries.shape
    feats = proj_query.shape[1] // n_head

    def shape(*dims, dtype=low):
        return jax.ShapeDtypeStruct(dims, dtype)

    first = feats // 16 * 9 // 16 * 16
    partners = sorted(range(1, n_seq), key=lambda r: -r.bit_length()) if direct else []
    eager, late = partners[:1], partners[1:]
    n_copies = max(len(late), 1)
    *joined, grad_low, grad_high = kernel_call(
        functools.partial(join_kernel, n_copies),
        "join",
        [shape(held, 2 * kv_width)] * n_copies + [shape(rows // 2, width)] * 2,
        [HBM] * 3,
        [pltpu.SemaphoreType.DMA((4,))],
    )(*[in_hbm(x) for x in (keys, values, grad_out)])
    if direct:
        pairs = [swapped(x, "seq", r) for r in eager for x in (keys, values)]
        blocks = joined[-1:] + [swapped(x, "seq", r) for x, r in zip(joined, late)]
    else:
        pairs = []
        blocks = [lax.all_gather(joined[0], "seq", axis=0, tiled=True)]
    n_blocks = len(blocks) + len(eager)
    block_rows = blocks[0].shape[0]
    incoming = [shifted(part, "section", -1) for part in (grad_low, grad_high)]

    limit, q, *w_other = kernel_call(
        functools.partial(stage_kernel, n_head),
        "stage",
        [shape(8, HD, dtype=jnp.int32), shape(rows, width)] + [shape(feats, width)] * n_other,
        [HBM] * 4,
        [
            pltpu.SMEM(section_span.shape, jnp.int32),
            pltpu.SMEM(span_prefix.shape, jnp.int32),
            pltpu.SemaphoreType.DMA((1 + n_other,)),
            pltpu.SemaphoreType.DMA((2,)),
        ],
    )(*[in_hbm(x) for x in (section_span, span_prefix, queries, proj_query)])

    prefix = n_blocks * block_rows
    weights = shape(kv_width // HD, prefix, 2 * rows)
    grad_query, probs, dscores, *products = kernel_call(
        functools.partial(attention_kernel, eager, late, n_other),
        "attention",
        [shape(width, rows), weights, weights] + [shape(first, rows)] * n_other,
        [VMEM] * (4 + len(pairs) + len(blocks) + n_other),
    )(limit, q, *pairs, *blocks, *incoming, *w_other)
    rest = kernel_call(
        functools.partial(rest_kernel, n_other),
        "rest",
        [shape(feats - first, rows)] * n_other,
        [VMEM] * (1 + n_other),
    )(grad_query, *w_other)
    arrived = [shifted(p, "head", r + 1) for part in (products, rest) for r, p in enumerate(part)]
    terms = kernel_call(
        terms_kernel, "terms", [shape(block_rows, 2 * kv_width)] * n_blocks, [VMEM] * 5
    )(probs, dscores, q, *incoming)
    if direct:
        all_terms = [terms[0]] + [swapped(x, "seq", r) for x, r in zip(terms[1:], partners)]
    else:
        all_terms = [lax.psum_scatter(terms[0], "seq", scatter_dimension=0, tiled=True)]

    own = kernel_call(
        functools.partial(own_kernel, n_head),
        "own",
        shape(feats, rows, dtype=jnp.float32),
        [VMEM, HBM],
        [pltpu.VMEM((feats, width), low), pltpu.SemaphoreType.DMA(())],
    )(grad_query, in_hbm(proj_query))
    grad_key, grad_value = kernel_call(
        term_sum_kernel, "term_sum", [shape(1, held, kv_width)] * 2, [VMEM] * len(all_terms)
    )(*all_terms)
    grad_input = kernel_call(
        input_sum_kernel, "input_sum", shape(1, feats, rows), [VMEM] * (1 + len(arrived))
    )(own, *arrived)
    return (grad_input, grad_key, grad_value)


def solution(mesh):
    in_specs = (
        P("section", "seq", "head"),
        P("section", "seq", "head"),
        P("section", "seq", "head"),
        P("section", "seq", "head"),
        P("section", None, "head"),
        P(),
        P(),
    )
    out_specs = (
        P("section", "head", "seq"),
        P("section", "seq", "head"),
        P("section", "seq", "head"),
    )
    return jax.shard_map(
        on_device, mesh=mesh, in_specs=in_specs, out_specs=out_specs, check_vma=False
    )
```

```python
import functools
import math

import jax
import jax.numpy as jnp
from jax import lax
from jax.experimental import pallas as pl
from jax.experimental.pallas import tpu as pltpu
from jax.sharding import PartitionSpec as P

HD = 128
MOST_PARTNERS = 4
VMEM_LIMIT = 40 * 1024 * 1024

query_scale = 168.0 ** (-0.5)
exp2_scale = query_scale * math.log2(math.e)


def shifted(block, axis, distance):
    devices = range(lax.axis_size(axis))
    route = [((i - distance) % len(devices), i) for i in devices]
    return lax.ppermute(block, axis, route)


def swapped(block, axis, distance):
    return lax.ppermute(block, axis, [(i, i ^ distance) for i in range(lax.axis_size(axis))])


def dot(left, right, left_dim, right_dim):
    return lax.dot_general(
        left, right, (((left_dim,), (right_dim,)), ((), ())), preferred_element_type=jnp.float32
    )


def in_hbm(x):
    return pltpu.with_memory_space_constraint(x, pltpu.HBM)


def join_kernel(n_copies, key_ref, value_ref, grad_ref, *refs):
    *outs, grad_low, grad_high, sems = refs
    width, rows = key_ref.shape[2], grad_low.shape[0]
    pairs = [
        (key_ref.at[0], outs[0].at[:, :width]),
        (value_ref.at[0], outs[0].at[:, width:]),
        (grad_ref.at[0, :rows, :], grad_low),
        (grad_ref.at[0, rows:, :], grad_high),
    ]
    copies = [pltpu.make_async_copy(a, b, sems.at[i]) for i, (a, b) in enumerate(pairs)]
    for copy in copies:
        copy.start()
    for copy in copies[:2]:
        copy.wait()
    for out in outs[1:]:
        out[...] = outs[0][...]
    for copy in copies[2:]:
        copy.wait()


def stage_kernel(n_head, span_ref, prefix_ref, q_ref, w_ref, limit_out, q_out, *refs):
    *other_outs, span, prefix, sems, small_sems = refs
    feats = w_ref.shape[1] // n_head
    head = lax.axis_index("head")
    copies = []
    for r, out in enumerate(other_outs):
        start = pl.multiple_of(lax.rem(head + r + 1, n_head) * feats, 16)
        copies.append((w_ref.at[0, pl.ds(start, feats), :], out))
    copies.append((q_ref.at[0], q_out))
    copies = [pltpu.make_async_copy(a, b, sems.at[i]) for i, (a, b) in enumerate(copies)]
    small = [
        pltpu.make_async_copy(a, b, small_sems.at[i])
        for i, (a, b) in enumerate([(span_ref, span), (prefix_ref, prefix)])
    ]
    for copy in small + copies:
        copy.start()
    for copy in small:
        copy.wait()
    live = prefix[span[lax.axis_index("section")]]
    limit_out[...] = jnp.full(limit_out.shape, live, jnp.int32)
    for copy in copies:
        copy.wait()


def pair_of(refs, g):
    cols = [slice((2 * g + i) * HD, (2 * g + i + 1) * HD) for i in range(2)]
    return jnp.concatenate([ref[:, c] for c in cols for ref in refs], axis=0)


def attention_kernel(partners, n_other, limit_ref, q_ref, *refs):
    n_blocks = 1 + len(partners)
    kv_refs = refs[:n_blocks]
    d_low, d_high, *refs = refs[n_blocks:]
    w_refs = refs[:n_other]
    grad_ref, probs_ref, dscores_ref, *part_refs = refs[n_other:]

    held, both = kv_refs[0].shape
    width = both // 2
    seq = lax.axis_index("seq")
    spots = []
    for r in [0, *partners]:
        first = jnp.bitwise_xor(seq, r) * held if partners else 0
        spots.append(first + lax.broadcasted_iota(jnp.int32, (held, 1), 0))
    alive = jnp.concatenate(spots, axis=0) < limit_ref[0:1, 0:1]

    rows = q_ref.shape[0]
    for g in range(width // HD):
        k_cols = slice(g * HD, (g + 1) * HD)
        v_cols = slice(width + g * HD, width + (g + 1) * HD)
        q = pair_of((q_ref,), g)
        d = pair_of((d_low, d_high), g)
        k = jnp.concatenate([ref[:, k_cols] for ref in kv_refs], axis=0)
        v = jnp.concatenate([ref[:, v_cols] for ref in kv_refs], axis=0)
        scores = jnp.where(alive, dot(k, q, 1, 1), jnp.float32(-1e30))
        dprobs = dot(v, d, 1, 1)
        top = jnp.max(scores, axis=0, keepdims=True)
        probs = jnp.exp2((scores - top) * exp2_scale)
        probs = probs * (1.0 / jnp.sum(probs, axis=0, keepdims=True))
        probs_low = probs.astype(jnp.bfloat16)
        delta = jnp.sum(probs_low.astype(jnp.float32) * dprobs, axis=0, keepdims=True)
        dscores = (probs * (dprobs - delta)).astype(jnp.bfloat16)
        probs_ref[g] = probs_low
        dscores_ref[g] = dscores
        grad_q = (query_scale * dot(k, dscores, 0, 0)).astype(jnp.bfloat16)
        for i in range(2):
            spot = (2 * g + i) * HD
            grad_ref[spot : spot + HD, :] = grad_q[:, i * rows : (i + 1) * rows]

    for w_ref, part_ref in zip(w_refs, part_refs):
        block = w_ref[: part_ref.shape[0], :]
        part_ref[...] = dot(block, grad_ref[...], 1, 0).astype(jnp.bfloat16)


def rest_kernel(n_other, grad_ref, *refs):
    for w_ref, part_ref in zip(refs[:n_other], refs[n_other:]):
        block = w_ref[w_ref.shape[0] - part_ref.shape[0] :, :]
        part_ref[...] = dot(block, grad_ref[...], 1, 0).astype(jnp.bfloat16)


def terms_kernel(probs_ref, dscores_ref, q_ref, d_low, d_high, *term_refs):
    held, both = term_refs[0].shape
    width = both // 2
    for g in range(width // HD):
        grad_k = (query_scale * dot(dscores_ref[g], pair_of((q_ref,), g), 1, 0)).astype(jnp.bfloat16)
        grad_v = dot(probs_ref[g], pair_of((d_low, d_high), g), 1, 0).astype(jnp.bfloat16)
        for r, ref in enumerate(term_refs):
            block = slice(r * held, (r + 1) * held)
            ref[:, g * HD : (g + 1) * HD] = grad_k[block]
            ref[:, width + g * HD : width + (g + 1) * HD] = grad_v[block]


def own_kernel(n_head, grad_ref, w_ref, out_ref, w_held, sem):
    feats = out_ref.shape[0]
    start = pl.multiple_of(lax.axis_index("head") * feats, 16)
    copy = pltpu.make_async_copy(w_ref.at[0, pl.ds(start, feats), :], w_held, sem)
    copy.start()
    copy.wait()
    out_ref[...] = dot(w_held[...], grad_ref[...], 1, 0)


def input_sum_kernel(n_other, start, own_ref, *refs):
    arrived = refs[:n_other]
    *_, out_ref, held, sem = refs
    at = slice(start, start + held.shape[0])
    total = own_ref[at, :]
    for ref in arrived:
        total = total + ref[...].astype(jnp.float32)
    held[...] = total.astype(jnp.bfloat16)
    copy = pltpu.make_async_copy(held, out_ref.at[0, at, :], sem)
    copy.start()
    copy.wait()


def term_sum_kernel(*refs):
    *terms, key_ref, value_ref = refs
    total = terms[0][...].astype(jnp.float32)
    for ref in terms[1:]:
        total = total + ref[...].astype(jnp.float32)
    low = total.astype(jnp.bfloat16)
    half = low.shape[1] // 2
    key_ref[0] = low[:, :half]
    value_ref[0] = low[:, half:]


VMEM = pl.BlockSpec(memory_space=pltpu.VMEM)
HBM = pl.BlockSpec(memory_space=pltpu.HBM)


def kernel_call(body, name, out_shape, in_specs, scratch=(), limit=VMEM_LIMIT):
    return pl.pallas_call(
        body,
        out_shape=out_shape,
        in_specs=in_specs,
        out_specs=jax.tree.map(lambda _: VMEM, out_shape),
        scratch_shapes=list(scratch),
        compiler_params=pltpu.CompilerParams(vmem_limit_bytes=limit),
        name=name,
    )


def on_device(queries, grad_out, keys, values, proj_query, section_span, span_prefix):
    n_seq, n_head = lax.axis_size("seq"), lax.axis_size("head")
    n_other = n_head - 1
    direct = n_seq <= MOST_PARTNERS and n_seq & (n_seq - 1) == 0
    low = jnp.bfloat16
    _, held, kv_width = keys.shape
    _, rows, width = queries.shape
    feats = proj_query.shape[1] // n_head

    def shape(*dims, dtype=low):
        return jax.ShapeDtypeStruct(dims, dtype)

    first = feats // 16 * 9 // 16 * 16
    partners = sorted(range(1, n_seq), key=lambda r: -r.bit_length()) if direct else []
    n_copies = 1 + len(partners)
    *joined, grad_low, grad_high = kernel_call(
        functools.partial(join_kernel, n_copies),
        "join",
        [shape(held, 2 * kv_width)] * n_copies + [shape(rows // 2, width)] * 2,
        [HBM] * 3,
        [pltpu.SemaphoreType.DMA((4,))],
    )(*[in_hbm(x) for x in (keys, values, grad_out)])
    if direct:
        blocks = joined[-1:] + [swapped(x, "seq", r) for x, r in zip(joined, partners)]
    else:
        blocks = [lax.all_gather(joined[0], "seq", axis=0, tiled=True)]
    n_blocks, block_rows = len(blocks), blocks[0].shape[0]
    incoming = [shifted(part, "section", -1) for part in (grad_low, grad_high)]

    limit, q, *w_other = kernel_call(
        functools.partial(stage_kernel, n_head),
        "stage",
        [shape(8, HD, dtype=jnp.int32), shape(rows, width)] + [shape(feats, width)] * n_other,
        [HBM] * 4,
        [
            pltpu.SMEM(section_span.shape, jnp.int32),
            pltpu.SMEM(span_prefix.shape, jnp.int32),
            pltpu.SemaphoreType.DMA((1 + n_other,)),
            pltpu.SemaphoreType.DMA((2,)),
        ],
    )(*[in_hbm(x) for x in (section_span, span_prefix, queries, proj_query)])

    prefix = n_blocks * block_rows
    weights = shape(kv_width // HD, prefix, 2 * rows)
    grad_query, probs, dscores, *products = kernel_call(
        functools.partial(attention_kernel, partners, n_other),
        "attention",
        [shape(width, rows), weights, weights] + [shape(first, rows)] * n_other,
        [VMEM] * (4 + n_blocks + n_other),
    )(limit, q, *blocks, *incoming, *w_other)
    rest = kernel_call(
        functools.partial(rest_kernel, n_other),
        "rest",
        [shape(feats - first, rows)] * n_other,
        [VMEM] * (1 + n_other),
    )(grad_query, *w_other)
    arrived = [shifted(p, "head", r + 1) for part in (products, rest) for r, p in enumerate(part)]
    terms = kernel_call(
        terms_kernel, "terms", [shape(block_rows, 2 * kv_width)] * n_blocks, [VMEM] * 5
    )(probs, dscores, q, *incoming)
    if direct:
        all_terms = [terms[0]] + [swapped(x, "seq", r) for x, r in zip(terms[1:], partners)]
    else:
        all_terms = [lax.psum_scatter(terms[0], "seq", scatter_dimension=0, tiled=True)]

    own = kernel_call(
        functools.partial(own_kernel, n_head),
        "own",
        shape(feats, rows, dtype=jnp.float32),
        [VMEM, HBM],
        [pltpu.VMEM((feats, width), low), pltpu.SemaphoreType.DMA(())],
    )(grad_query, in_hbm(proj_query))
    grad_key, grad_value = kernel_call(
        term_sum_kernel, "term_sum", [shape(1, held, kv_width)] * 2, [VMEM] * len(all_terms)
    )(*all_terms)
    grad_input = []
    for start, part in ((0, arrived[:n_other]), (first, arrived[n_other:])):
        grad_input = [
            pl.pallas_call(
                functools.partial(input_sum_kernel, n_other, start),
                out_shape=shape(1, feats, rows),
                in_specs=[VMEM] * (1 + n_other) + [HBM] * len(grad_input),
                out_specs=HBM,
                scratch_shapes=[pltpu.VMEM(part[0].shape, low), pltpu.SemaphoreType.DMA(())],
                input_output_aliases={1 + n_other: 0} if grad_input else {},
                compiler_params=pltpu.CompilerParams(vmem_limit_bytes=VMEM_LIMIT),
                name="input_sum",
            )(own, *part, *grad_input)
        ]
    grad_input = grad_input[0]
    return (grad_input, grad_key, grad_value)


def solution(mesh):
    in_specs = (
        P("section", "seq", "head"),
        P("section", "seq", "head"),
        P("section", "seq", "head"),
        P("section", "seq", "head"),
        P("section", None, "head"),
        P(),
        P(),
    )
    out_specs = (
        P("section", "head", "seq"),
        P("section", "seq", "head"),
        P("section", "seq", "head"),
    )
    return jax.shard_map(
        on_device, mesh=mesh, in_specs=in_specs, out_specs=out_specs, check_vma=False
    )
```

```python
import functools
import math

import jax
import jax.numpy as jnp
from jax import lax
from jax.experimental import pallas as pl
from jax.experimental.pallas import tpu as pltpu
from jax.sharding import PartitionSpec as P

HD = 128
MOST_PARTNERS = 4
VMEM_LIMIT = 40 * 1024 * 1024

query_scale = 168.0 ** (-0.5)
exp2_scale = query_scale * math.log2(math.e)


def shifted(block, axis, distance):
    devices = range(lax.axis_size(axis))
    route = [((i - distance) % len(devices), i) for i in devices]
    return lax.ppermute(block, axis, route)


def swapped(block, axis, distance):
    return lax.ppermute(block, axis, [(i, i ^ distance) for i in range(lax.axis_size(axis))])


def dot(left, right, left_dim, right_dim):
    return lax.dot_general(
        left, right, (((left_dim,), (right_dim,)), ((), ())), preferred_element_type=jnp.float32
    )


def in_hbm(x):
    return pltpu.with_memory_space_constraint(x, pltpu.HBM)


def join_kernel(n_copies, key_ref, value_ref, grad_ref, out_ref, grad_low, grad_high, sems):
    width, rows = key_ref.shape[2], grad_low.shape[0]
    pairs = [
        (key_ref.at[0], out_ref.at[0, :, :width]),
        (value_ref.at[0], out_ref.at[0, :, width:]),
        (grad_ref.at[0, :rows, :], grad_low),
        (grad_ref.at[0, rows:, :], grad_high),
    ]
    copies = [pltpu.make_async_copy(a, b, sems.at[i]) for i, (a, b) in enumerate(pairs)]
    for copy in copies:
        copy.start()
    for copy in copies[:2]:
        copy.wait()
    for i in range(1, n_copies):
        out_ref[i] = out_ref[0]
    for copy in copies[2:]:
        copy.wait()


def stage_kernel(n_head, span_ref, prefix_ref, q_ref, w_ref, limit_out, q_out, *refs):
    *other_outs, span, prefix, sems, small_sems = refs
    feats = w_ref.shape[1] // n_head
    head = lax.axis_index("head")
    copies = []
    for r, out in enumerate(other_outs):
        start = pl.multiple_of(lax.rem(head + r + 1, n_head) * feats, 16)
        copies.append((w_ref.at[0, pl.ds(start, feats), :], out))
    copies.append((q_ref.at[0], q_out))
    copies = [pltpu.make_async_copy(a, b, sems.at[i]) for i, (a, b) in enumerate(copies)]
    small = [
        pltpu.make_async_copy(a, b, small_sems.at[i])
        for i, (a, b) in enumerate([(span_ref, span), (prefix_ref, prefix)])
    ]
    for copy in small + copies:
        copy.start()
    for copy in small:
        copy.wait()
    live = prefix[span[lax.axis_index("section")]]
    limit_out[...] = jnp.full(limit_out.shape, live, jnp.int32)
    for copy in copies:
        copy.wait()


def pair_of(refs, g):
    cols = [slice((2 * g + i) * HD, (2 * g + i + 1) * HD) for i in range(2)]
    return jnp.concatenate([ref[:, c] for c in cols for ref in refs], axis=0)


def attention_kernel(partners, n_other, limit_ref, q_ref, *refs):
    blocks_ref, d_low, d_high, *refs = refs
    seq = lax.axis_index("seq")
    order = [jnp.bitwise_xor(seq, r) for r in [0, *partners]] if partners else [0]
    kv_refs = [blocks_ref.at[i] for i in order]
    w_refs = refs[:n_other]
    grad_ref, probs_ref, dscores_ref, *part_refs = refs[n_other:]

    held, both = kv_refs[0].shape
    width = both // 2
    spots = [i * held + lax.broadcasted_iota(jnp.int32, (held, 1), 0) for i in order]
    alive = jnp.concatenate(spots, axis=0) < limit_ref[0:1, 0:1]

    rows = q_ref.shape[0]
    for g in range(width // HD):
        k_cols = slice(g * HD, (g + 1) * HD)
        v_cols = slice(width + g * HD, width + (g + 1) * HD)
        q = pair_of((q_ref,), g)
        d = pair_of((d_low, d_high), g)
        k = jnp.concatenate([ref[:, k_cols] for ref in kv_refs], axis=0)
        v = jnp.concatenate([ref[:, v_cols] for ref in kv_refs], axis=0)
        scores = jnp.where(alive, dot(k, q, 1, 1), jnp.float32(-1e30))
        dprobs = dot(v, d, 1, 1)
        top = jnp.max(scores, axis=0, keepdims=True)
        probs = jnp.exp2((scores - top) * exp2_scale)
        probs = probs * (1.0 / jnp.sum(probs, axis=0, keepdims=True))
        probs_low = probs.astype(jnp.bfloat16)
        delta = jnp.sum(probs_low.astype(jnp.float32) * dprobs, axis=0, keepdims=True)
        dscores = (probs * (dprobs - delta)).astype(jnp.bfloat16)
        probs_ref[g] = probs_low
        dscores_ref[g] = dscores
        grad_q = (query_scale * dot(k, dscores, 0, 0)).astype(jnp.bfloat16)
        for i in range(2):
            spot = (2 * g + i) * HD
            grad_ref[spot : spot + HD, :] = grad_q[:, i * rows : (i + 1) * rows]

    for w_ref, part_ref in zip(w_refs, part_refs):
        block = w_ref[: part_ref.shape[0], :]
        part_ref[...] = dot(block, grad_ref[...], 1, 0).astype(jnp.bfloat16)


def rest_kernel(n_other, grad_ref, *refs):
    for w_ref, part_ref in zip(refs[:n_other], refs[n_other:]):
        block = w_ref[w_ref.shape[0] - part_ref.shape[0] :, :]
        part_ref[...] = dot(block, grad_ref[...], 1, 0).astype(jnp.bfloat16)


def terms_kernel(probs_ref, dscores_ref, q_ref, d_low, d_high, *term_refs):
    held, both = term_refs[0].shape
    width = both // 2
    for g in range(width // HD):
        grad_k = (query_scale * dot(dscores_ref[g], pair_of((q_ref,), g), 1, 0)).astype(jnp.bfloat16)
        grad_v = dot(probs_ref[g], pair_of((d_low, d_high), g), 1, 0).astype(jnp.bfloat16)
        for r, ref in enumerate(term_refs):
            block = slice(r * held, (r + 1) * held)
            ref[:, g * HD : (g + 1) * HD] = grad_k[block]
            ref[:, width + g * HD : width + (g + 1) * HD] = grad_v[block]


def own_kernel(n_head, grad_ref, w_ref, out_ref, w_held, sem):
    feats = out_ref.shape[0]
    start = pl.multiple_of(lax.axis_index("head") * feats, 16)
    copy = pltpu.make_async_copy(w_ref.at[0, pl.ds(start, feats), :], w_held, sem)
    copy.start()
    copy.wait()
    out_ref[...] = dot(w_held[...], grad_ref[...], 1, 0)


def input_sum_kernel(n_other, start, own_ref, *refs):
    arrived = refs[:n_other]
    *_, out_ref, held, sem = refs
    at = slice(start, start + held.shape[0])
    total = own_ref[at, :]
    for ref in arrived:
        total = total + ref[...].astype(jnp.float32)
    held[...] = total.astype(jnp.bfloat16)
    copy = pltpu.make_async_copy(held, out_ref.at[0, at, :], sem)
    copy.start()
    copy.wait()


def term_sum_kernel(*refs):
    *terms, key_ref, value_ref = refs
    total = terms[0][...].astype(jnp.float32)
    for ref in terms[1:]:
        total = total + ref[...].astype(jnp.float32)
    low = total.astype(jnp.bfloat16)
    half = low.shape[1] // 2
    key_ref[0] = low[:, :half]
    value_ref[0] = low[:, half:]


VMEM = pl.BlockSpec(memory_space=pltpu.VMEM)
HBM = pl.BlockSpec(memory_space=pltpu.HBM)


def kernel_call(body, name, out_shape, in_specs, scratch=(), limit=VMEM_LIMIT):
    return pl.pallas_call(
        body,
        out_shape=out_shape,
        in_specs=in_specs,
        out_specs=jax.tree.map(lambda _: VMEM, out_shape),
        scratch_shapes=list(scratch),
        compiler_params=pltpu.CompilerParams(vmem_limit_bytes=limit),
        name=name,
    )


def on_device(queries, grad_out, keys, values, proj_query, section_span, span_prefix):
    n_seq, n_head = lax.axis_size("seq"), lax.axis_size("head")
    n_other = n_head - 1
    direct = n_seq <= MOST_PARTNERS and n_seq & (n_seq - 1) == 0
    low = jnp.bfloat16
    _, held, kv_width = keys.shape
    _, rows, width = queries.shape
    feats = proj_query.shape[1] // n_head

    def shape(*dims, dtype=low):
        return jax.ShapeDtypeStruct(dims, dtype)

    first = feats // 16 * 9 // 16 * 16
    partners = sorted(range(1, n_seq), key=lambda r: -r.bit_length()) if direct else []
    n_copies = 1 + len(partners)
    joined, grad_low, grad_high = kernel_call(
        functools.partial(join_kernel, n_copies),
        "join",
        [shape(n_copies, held, 2 * kv_width)] + [shape(rows // 2, width)] * 2,
        [HBM] * 3,
        [pltpu.SemaphoreType.DMA((4,))],
    )(*[in_hbm(x) for x in (keys, values, grad_out)])
    if direct:
        blocks = lax.all_to_all(joined, "seq", 0, 0)
    else:
        blocks = lax.all_gather(joined[0], "seq", axis=0, tiled=True)[None]
    n_blocks, block_rows = blocks.shape[:2]
    incoming = [shifted(part, "section", -1) for part in (grad_low, grad_high)]

    limit, q, *w_other = kernel_call(
        functools.partial(stage_kernel, n_head),
        "stage",
        [shape(8, HD, dtype=jnp.int32), shape(rows, width)] + [shape(feats, width)] * n_other,
        [HBM] * 4,
        [
            pltpu.SMEM(section_span.shape, jnp.int32),
            pltpu.SMEM(span_prefix.shape, jnp.int32),
            pltpu.SemaphoreType.DMA((1 + n_other,)),
            pltpu.SemaphoreType.DMA((2,)),
        ],
    )(*[in_hbm(x) for x in (section_span, span_prefix, queries, proj_query)])

    prefix = n_blocks * block_rows
    weights = shape(kv_width // HD, prefix, 2 * rows)
    grad_query, probs, dscores, *products = kernel_call(
        functools.partial(attention_kernel, partners, n_other),
        "attention",
        [shape(width, rows), weights, weights] + [shape(first, rows)] * n_other,
        [VMEM] * (5 + n_other),
    )(limit, q, blocks, *incoming, *w_other)
    rest = kernel_call(
        functools.partial(rest_kernel, n_other),
        "rest",
        [shape(feats - first, rows)] * n_other,
        [VMEM] * (1 + n_other),
    )(grad_query, *w_other)
    arrived = [shifted(p, "head", r + 1) for part in (products, rest) for r, p in enumerate(part)]
    terms = kernel_call(
        terms_kernel, "terms", [shape(block_rows, 2 * kv_width)] * n_blocks, [VMEM] * 5
    )(probs, dscores, q, *incoming)
    if direct:
        all_terms = [terms[0]] + [swapped(x, "seq", r) for x, r in zip(terms[1:], partners)]
    else:
        all_terms = [lax.psum_scatter(terms[0], "seq", scatter_dimension=0, tiled=True)]

    own = kernel_call(
        functools.partial(own_kernel, n_head),
        "own",
        shape(feats, rows, dtype=jnp.float32),
        [VMEM, HBM],
        [pltpu.VMEM((feats, width), low), pltpu.SemaphoreType.DMA(())],
    )(grad_query, in_hbm(proj_query))
    grad_key, grad_value = kernel_call(
        term_sum_kernel, "term_sum", [shape(1, held, kv_width)] * 2, [VMEM] * len(all_terms)
    )(*all_terms)
    grad_input = []
    for start, part in ((0, arrived[:n_other]), (first, arrived[n_other:])):
        grad_input = [
            pl.pallas_call(
                functools.partial(input_sum_kernel, n_other, start),
                out_shape=shape(1, feats, rows),
                in_specs=[VMEM] * (1 + n_other) + [HBM] * len(grad_input),
                out_specs=HBM,
                scratch_shapes=[pltpu.VMEM(part[0].shape, low), pltpu.SemaphoreType.DMA(())],
                input_output_aliases={1 + n_other: 0} if grad_input else {},
                compiler_params=pltpu.CompilerParams(vmem_limit_bytes=VMEM_LIMIT),
                name="input_sum",
            )(own, *part, *grad_input)
        ]
    grad_input = grad_input[0]
    return (grad_input, grad_key, grad_value)


def solution(mesh):
    in_specs = (
        P("section", "seq", "head"),
        P("section", "seq", "head"),
        P("section", "seq", "head"),
        P("section", "seq", "head"),
        P("section", None, "head"),
        P(),
        P(),
    )
    out_specs = (
        P("section", "head", "seq"),
        P("section", "seq", "head"),
        P("section", "seq", "head"),
    )
    return jax.shard_map(
        on_device, mesh=mesh, in_specs=in_specs, out_specs=out_specs, check_vma=False
    )
```

```python
import functools
import math

import jax
import jax.numpy as jnp
from jax import lax
from jax.experimental import pallas as pl
from jax.experimental.pallas import tpu as pltpu
from jax.sharding import PartitionSpec as P

HD = 128
MOST_PARTNERS = 4
VMEM_LIMIT = 40 * 1024 * 1024

query_scale = 168.0 ** (-0.5)
exp2_scale = query_scale * math.log2(math.e)


def shifted(block, axis, distance):
    devices = range(lax.axis_size(axis))
    route = [((i - distance) % len(devices), i) for i in devices]
    return lax.ppermute(block, axis, route)


def swapped(block, axis, distance):
    return lax.ppermute(block, axis, [(i, i ^ distance) for i in range(lax.axis_size(axis))])


def dot(left, right, left_dim, right_dim):
    return lax.dot_general(
        left, right, (((left_dim,), (right_dim,)), ((), ())), preferred_element_type=jnp.float32
    )


def in_hbm(x):
    return pltpu.with_memory_space_constraint(x, pltpu.HBM)


def fetch(copies, sems):
    copies = [pltpu.make_async_copy(a, b, sems.at[i]) for i, (a, b) in enumerate(copies)]
    for copy in copies:
        copy.start()
    return copies


def join_kernel(n_copies, span_ref, prefix_ref, key_ref, value_ref, grad_ref, q_ref, *refs):
    *outs, grad_low, grad_high, q_out, limit_out, span, prefix, sems = refs
    width, rows = key_ref.shape[2], grad_low.shape[0]
    copies = fetch(
        [
            (key_ref.at[0], outs[0].at[:, :width]),
            (value_ref.at[0], outs[0].at[:, width:]),
            (grad_ref.at[0, :rows, :], grad_low),
            (grad_ref.at[0, rows:, :], grad_high),
            (span_ref, span),
            (prefix_ref, prefix),
            (q_ref.at[0], q_out),
        ],
        sems,
    )
    for copy in copies[:2]:
        copy.wait()
    for out in outs[1:n_copies]:
        out[...] = outs[0][...]
    for copy in copies[2:]:
        copy.wait()
    live = prefix[span[lax.axis_index("section")]]
    limit_out[...] = jnp.full(limit_out.shape, live, jnp.int32)


def fetch_weights(n_head, skip, w_ref, w_held, sems):
    feats = w_ref.shape[1] // n_head
    head = lax.axis_index("head")
    copies = []
    for r in range(1, n_head):
        start = pl.multiple_of(lax.rem(head + r, n_head) * feats + skip, 16)
        copies.append((w_ref.at[0, pl.ds(start, w_held.shape[1]), :], w_held.at[r - 1]))
    return fetch(copies, sems)


def products(copies, grad_ref, w_held, part_refs):
    for i, (copy, part_ref) in enumerate(zip(copies, part_refs)):
        copy.wait()
        part_ref[...] = dot(w_held[i], grad_ref[...], 1, 0).astype(jnp.bfloat16)


def pair_of(refs, g):
    cols = [slice((2 * g + i) * HD, (2 * g + i + 1) * HD) for i in range(2)]
    return jnp.concatenate([ref[:, c] for c in cols for ref in refs], axis=0)


def attention_kernel(order, n_head, limit_ref, q_ref, *refs):
    kv_refs = refs[: len(order)]
    d_low, d_high, w_ref, *refs = refs[len(order) :]
    grad_ref, probs_ref, dscores_ref, *part_refs, w_held, sems = refs
    copies = fetch_weights(n_head, 0, w_ref, w_held, sems)

    held, both = kv_refs[0].shape
    width = both // 2
    seq = lax.axis_index("seq")
    spots = []
    for r in order:
        first = jnp.bitwise_xor(seq, r) * held if len(order) > 1 else 0
        spots.append(first + lax.broadcasted_iota(jnp.int32, (held, 1), 0))
    alive = jnp.concatenate(spots, axis=0) < limit_ref[0:1, 0:1]

    rows = q_ref.shape[0]
    for g in range(width // HD):
        k_cols = slice(g * HD, (g + 1) * HD)
        v_cols = slice(width + g * HD, width + (g + 1) * HD)
        q = pair_of((q_ref,), g)
        d = pair_of((d_low, d_high), g)
        k = jnp.concatenate([ref[:, k_cols] for ref in kv_refs], axis=0)
        v = jnp.concatenate([ref[:, v_cols] for ref in kv_refs], axis=0)
        scores = jnp.where(alive, dot(k, q, 1, 1), jnp.float32(-1e30))
        dprobs = dot(v, d, 1, 1)
        top = jnp.max(scores, axis=0, keepdims=True)
        probs = jnp.exp2((scores - top) * exp2_scale)
        probs = probs * (1.0 / jnp.sum(probs, axis=0, keepdims=True))
        probs_low = probs.astype(jnp.bfloat16)
        delta = jnp.sum(probs_low.astype(jnp.float32) * dprobs, axis=0, keepdims=True)
        dscores = (probs * (dprobs - delta)).astype(jnp.bfloat16)
        probs_ref[g] = probs_low
        dscores_ref[g] = dscores
        grad_q = (query_scale * dot(k, dscores, 0, 0)).astype(jnp.bfloat16)
        for i in range(2):
            spot = (2 * g + i) * HD
            grad_ref[spot : spot + HD, :] = grad_q[:, i * rows : (i + 1) * rows]

    products(copies, grad_ref, w_held, part_refs)


def rest_kernel(n_head, skip, grad_ref, w_ref, *refs):
    *part_refs, w_held, sems = refs
    copies = fetch_weights(n_head, skip, w_ref, w_held, sems)
    products(copies, grad_ref, w_held, part_refs)


def terms_kernel(probs_ref, dscores_ref, q_ref, d_low, d_high, *term_refs):
    held, both = term_refs[0].shape
    width = both // 2
    for g in range(width // HD):
        grad_k = (query_scale * dot(dscores_ref[g], pair_of((q_ref,), g), 1, 0)).astype(jnp.bfloat16)
        grad_v = dot(probs_ref[g], pair_of((d_low, d_high), g), 1, 0).astype(jnp.bfloat16)
        for r, ref in enumerate(term_refs):
            block = slice(r * held, (r + 1) * held)
            ref[:, g * HD : (g + 1) * HD] = grad_k[block]
            ref[:, width + g * HD : width + (g + 1) * HD] = grad_v[block]


def own_kernel(n_head, grad_ref, w_ref, out_ref, w_held, sem):
    feats = out_ref.shape[0]
    start = pl.multiple_of(lax.axis_index("head") * feats, 16)
    copy = pltpu.make_async_copy(w_ref.at[0, pl.ds(start, feats), :], w_held, sem)
    copy.start()
    copy.wait()
    out_ref[...] = dot(w_held[...], grad_ref[...], 1, 0)


def input_sum_kernel(n_other, start, own_ref, *refs):
    arrived = refs[:n_other]
    *_, out_ref, held, sem = refs
    at = slice(start, start + held.shape[0])
    total = own_ref[at, :]
    for ref in arrived:
        total = total + ref[...].astype(jnp.float32)
    held[...] = total.astype(jnp.bfloat16)
    copy = pltpu.make_async_copy(held, out_ref.at[0, at, :], sem)
    copy.start()
    copy.wait()


def term_sum_kernel(*refs):
    *terms, key_ref, value_ref = refs
    total = terms[0][...].astype(jnp.float32)
    for ref in terms[1:]:
        total = total + ref[...].astype(jnp.float32)
    low = total.astype(jnp.bfloat16)
    half = low.shape[1] // 2
    key_ref[0] = low[:, :half]
    value_ref[0] = low[:, half:]


VMEM = pl.BlockSpec(memory_space=pltpu.VMEM)
HBM = pl.BlockSpec(memory_space=pltpu.HBM)


def kernel_call(body, name, out_shape, in_specs, scratch=(), limit=VMEM_LIMIT):
    return pl.pallas_call(
        body,
        out_shape=out_shape,
        in_specs=in_specs,
        out_specs=jax.tree.map(lambda _: VMEM, out_shape),
        scratch_shapes=list(scratch),
        compiler_params=pltpu.CompilerParams(vmem_limit_bytes=limit),
        name=name,
    )


def on_device(queries, grad_out, keys, values, proj_query, section_span, span_prefix):
    n_seq, n_head = lax.axis_size("seq"), lax.axis_size("head")
    n_other = n_head - 1
    direct = n_seq <= MOST_PARTNERS and n_seq & (n_seq - 1) == 0
    low = jnp.bfloat16
    _, held, kv_width = keys.shape
    _, rows, width = queries.shape
    feats = proj_query.shape[1] // n_head

    def shape(*dims, dtype=low):
        return jax.ShapeDtypeStruct(dims, dtype)

    first = feats // 16 * 9 // 16 * 16
    bits = [1 << i for i in reversed(range(n_seq.bit_length() - 1))] if direct else []
    n_copies = max(len(bits), 1)
    scratch = [pltpu.SMEM(x.shape, x.dtype) for x in (section_span, span_prefix)]
    *joined, grad_low, grad_high, q, limit = kernel_call(
        functools.partial(join_kernel, n_copies),
        "join",
        [shape(held, 2 * kv_width)] * n_copies
        + [shape(rows // 2, width)] * 2
        + [shape(rows, width), shape(8, HD, dtype=jnp.int32)],
        [HBM] * 6,
        scratch + [pltpu.SemaphoreType.DMA((7,))],
    )(*[in_hbm(x) for x in (section_span, span_prefix, keys, values, grad_out, queries)])
    if direct:
        blocks = {0: joined[-1]}
        for bit, own in zip(bits, joined):
            sent = {r: own if r == 0 else block for r, block in blocks.items()}
            blocks |= {r ^ bit: swapped(block, "seq", bit) for r, block in sent.items()}
    else:
        blocks = {0: lax.all_gather(joined[0], "seq", axis=0, tiled=True)}
    order, blocks = list(blocks), list(blocks.values())
    n_blocks, block_rows = len(blocks), blocks[0].shape[0]
    incoming = [shifted(part, "section", -1) for part in (grad_low, grad_high)]

    weight_rows = in_hbm(proj_query)

    def held_rows(count):
        return [pltpu.VMEM((n_other, count, width), low), pltpu.SemaphoreType.DMA((n_other,))]

    prefix = n_blocks * block_rows
    weights = shape(kv_width // HD, prefix, 2 * rows)
    grad_query, probs, dscores, *products = kernel_call(
        functools.partial(attention_kernel, order, n_head),
        "attention",
        [shape(width, rows), weights, weights] + [shape(first, rows)] * n_other,
        [VMEM] * (4 + n_blocks) + [HBM],
        held_rows(first),
    )(limit, q, *blocks, *incoming, weight_rows)
    rest = kernel_call(
        functools.partial(rest_kernel, n_head, first),
        "rest",
        [shape(feats - first, rows)] * n_other,
        [VMEM, HBM],
        held_rows(feats - first),
    )(grad_query, weight_rows)
    arrived = [shifted(p, "head", r + 1) for part in (products, rest) for r, p in enumerate(part)]
    terms = kernel_call(
        terms_kernel, "terms", [shape(block_rows, 2 * kv_width)] * n_blocks, [VMEM] * 5
    )(probs, dscores, q, *incoming)
    if direct:
        all_terms = [terms[0]] + [swapped(x, "seq", r) for x, r in zip(terms[1:], order[1:])]
    else:
        all_terms = [lax.psum_scatter(terms[0], "seq", scatter_dimension=0, tiled=True)]

    own = kernel_call(
        functools.partial(own_kernel, n_head),
        "own",
        shape(feats, rows, dtype=jnp.float32),
        [VMEM, HBM],
        [pltpu.VMEM((feats, width), low), pltpu.SemaphoreType.DMA(())],
    )(grad_query, weight_rows)
    grad_key, grad_value = kernel_call(
        term_sum_kernel, "term_sum", [shape(1, held, kv_width)] * 2, [VMEM] * len(all_terms)
    )(*all_terms)
    grad_input = []
    for start, part in ((0, arrived[:n_other]), (first, arrived[n_other:])):
        grad_input = [
            pl.pallas_call(
                functools.partial(input_sum_kernel, n_other, start),
                out_shape=shape(1, feats, rows),
                in_specs=[VMEM] * (1 + n_other) + [HBM] * len(grad_input),
                out_specs=HBM,
                scratch_shapes=[pltpu.VMEM(part[0].shape, low), pltpu.SemaphoreType.DMA(())],
                input_output_aliases={1 + n_other: 0} if grad_input else {},
                compiler_params=pltpu.CompilerParams(vmem_limit_bytes=VMEM_LIMIT),
                name="input_sum",
            )(own, *part, *grad_input)
        ]
    grad_input = grad_input[0]
    return (grad_input, grad_key, grad_value)


def solution(mesh):
    in_specs = (
        P("section", "seq", "head"),
        P("section", "seq", "head"),
        P("section", "seq", "head"),
        P("section", "seq", "head"),
        P("section", None, "head"),
        P(),
        P(),
    )
    out_specs = (
        P("section", "head", "seq"),
        P("section", "seq", "head"),
        P("section", "seq", "head"),
    )
    return jax.shard_map(
        on_device, mesh=mesh, in_specs=in_specs, out_specs=out_specs, check_vma=False
    )
```

```python
import functools
import math

import jax
import jax.numpy as jnp
from jax import lax
from jax.experimental import pallas as pl
from jax.experimental.pallas import tpu as pltpu
from jax.sharding import PartitionSpec as P

HD = 128
MOST_PARTNERS = 4
VMEM_LIMIT = 40 * 1024 * 1024

query_scale = 168.0 ** (-0.5)
exp2_scale = query_scale * math.log2(math.e)


def shifted(block, axis, distance):
    devices = range(lax.axis_size(axis))
    route = [((i - distance) % len(devices), i) for i in devices]
    return lax.ppermute(block, axis, route)


def swapped(block, axis, distance):
    return lax.ppermute(block, axis, [(i, i ^ distance) for i in range(lax.axis_size(axis))])


def dot(left, right, left_dim, right_dim):
    return lax.dot_general(
        left, right, (((left_dim,), (right_dim,)), ((), ())), preferred_element_type=jnp.float32
    )


def in_hbm(x):
    return pltpu.with_memory_space_constraint(x, pltpu.HBM)


def join_kernel(n_copies, key_ref, value_ref, grad_ref, *refs):
    *outs, grad_low, grad_high, sems = refs
    width, rows = key_ref.shape[2], grad_low.shape[0]
    pairs = [
        (key_ref.at[0], outs[0].at[:, :width]),
        (value_ref.at[0], outs[0].at[:, width:]),
        (grad_ref.at[0, :rows, :], grad_low),
        (grad_ref.at[0, rows:, :], grad_high),
    ]
    copies = [pltpu.make_async_copy(a, b, sems.at[i]) for i, (a, b) in enumerate(pairs)]
    for copy in copies:
        copy.start()
    for copy in copies[:2]:
        copy.wait()
    for out in outs[1:]:
        out[...] = outs[0][...]
    for copy in copies[2:]:
        copy.wait()


def stage_kernel(n_head, span_ref, prefix_ref, q_ref, w_ref, limit_out, q_out, *refs):
    *other_outs, span, prefix, sems, small_sems = refs
    feats = w_ref.shape[1] // n_head
    head = lax.axis_index("head")
    copies = []
    for r, out in enumerate(other_outs):
        start = pl.multiple_of(lax.rem(head + r + 1, n_head) * feats, 16)
        copies.append((w_ref.at[0, pl.ds(start, feats), :], out))
    copies.append((q_ref.at[0], q_out))
    copies = [pltpu.make_async_copy(a, b, sems.at[i]) for i, (a, b) in enumerate(copies)]
    small = [
        pltpu.make_async_copy(a, b, small_sems.at[i])
        for i, (a, b) in enumerate([(span_ref, span), (prefix_ref, prefix)])
    ]
    for copy in small + copies:
        copy.start()
    for copy in small:
        copy.wait()
    live = prefix[span[lax.axis_index("section")]]
    limit_out[...] = jnp.full(limit_out.shape, live, jnp.int32)
    for copy in copies:
        copy.wait()


def pair_of(refs, g):
    cols = [slice((2 * g + i) * HD, (2 * g + i + 1) * HD) for i in range(2)]
    return jnp.concatenate([ref[:, c] for c in cols for ref in refs], axis=0)


def cols_of(g, start=0):
    return slice(start + g * HD, start + (g + 1) * HD)


def attention_kernel(partners, n_other, limit_ref, q_ref, *refs):
    n_blocks = 1 + len(partners)
    kv_refs = refs[:n_blocks]
    d_low, d_high, *refs = refs[n_blocks:]
    w_refs = refs[:n_other]
    grad_ref, probs_ref, dscores_ref, *part_refs = refs[n_other:]

    held, both = kv_refs[0].shape
    width = both // 2
    seq = lax.axis_index("seq")
    spots = []
    for r in [0, *partners]:
        first = jnp.bitwise_xor(seq, r) * held if partners else 0
        spots.append(first + lax.broadcasted_iota(jnp.int32, (held, 1), 0))
    alive = jnp.concatenate(spots, axis=0) < limit_ref[0:1, 0:1]

    rows = q_ref.shape[0]
    groups = range(width // HD)
    keys = [jnp.concatenate([ref[:, cols_of(g)] for ref in kv_refs], axis=0) for g in groups]
    scores = [dot(keys[g], pair_of((q_ref,), g), 1, 1) for g in groups]
    dprobs = []
    for g in groups:
        value = jnp.concatenate([ref[:, cols_of(g, width)] for ref in kv_refs], axis=0)
        dprobs.append(dot(value, pair_of((d_low, d_high), g), 1, 1))
    for g in groups:
        masked = jnp.where(alive, scores[g], jnp.float32(-1e30))
        top = jnp.max(masked, axis=0, keepdims=True)
        probs = jnp.exp2((masked - top) * exp2_scale)
        probs = probs * (1.0 / jnp.sum(probs, axis=0, keepdims=True))
        probs_low = probs.astype(jnp.bfloat16)
        delta = jnp.sum(probs_low.astype(jnp.float32) * dprobs[g], axis=0, keepdims=True)
        probs_ref[g] = probs_low
        dscores_ref[g] = (probs * (dprobs[g] - delta)).astype(jnp.bfloat16)
    for g in groups:
        grad_q = (query_scale * dot(keys[g], dscores_ref[g], 0, 0)).astype(jnp.bfloat16)
        for i in range(2):
            spot = (2 * g + i) * HD
            grad_ref[spot : spot + HD, :] = grad_q[:, i * rows : (i + 1) * rows]

    for w_ref, part_ref in zip(w_refs, part_refs):
        block = w_ref[: part_ref.shape[0], :]
        part_ref[...] = dot(block, grad_ref[...], 1, 0).astype(jnp.bfloat16)


def rest_kernel(n_other, grad_ref, *refs):
    for w_ref, part_ref in zip(refs[:n_other], refs[n_other:]):
        block = w_ref[w_ref.shape[0] - part_ref.shape[0] :, :]
        part_ref[...] = dot(block, grad_ref[...], 1, 0).astype(jnp.bfloat16)


def terms_kernel(probs_ref, dscores_ref, q_ref, d_low, d_high, *term_refs):
    held, both = term_refs[0].shape
    width = both // 2
    for g in range(width // HD):
        grad_k = (query_scale * dot(dscores_ref[g], pair_of((q_ref,), g), 1, 0)).astype(jnp.bfloat16)
        grad_v = dot(probs_ref[g], pair_of((d_low, d_high), g), 1, 0).astype(jnp.bfloat16)
        for r, ref in enumerate(term_refs):
            block = slice(r * held, (r + 1) * held)
            ref[:, g * HD : (g + 1) * HD] = grad_k[block]
            ref[:, width + g * HD : width + (g + 1) * HD] = grad_v[block]


def own_kernel(n_head, grad_ref, w_ref, out_ref, w_held, sem):
    feats = out_ref.shape[0]
    start = pl.multiple_of(lax.axis_index("head") * feats, 16)
    copy = pltpu.make_async_copy(w_ref.at[0, pl.ds(start, feats), :], w_held, sem)
    copy.start()
    copy.wait()
    out_ref[...] = dot(w_held[...], grad_ref[...], 1, 0)


def input_sum_kernel(n_other, start, own_ref, *refs):
    arrived = refs[:n_other]
    *_, out_ref, held, sem = refs
    at = slice(start, start + held.shape[0])
    total = own_ref[at, :]
    for ref in arrived:
        total = total + ref[...].astype(jnp.float32)
    held[...] = total.astype(jnp.bfloat16)
    copy = pltpu.make_async_copy(held, out_ref.at[0, at, :], sem)
    copy.start()
    copy.wait()


def term_sum_kernel(*refs):
    *terms, key_ref, value_ref = refs
    total = terms[0][...].astype(jnp.float32)
    for ref in terms[1:]:
        total = total + ref[...].astype(jnp.float32)
    low = total.astype(jnp.bfloat16)
    half = low.shape[1] // 2
    key_ref[0] = low[:, :half]
    value_ref[0] = low[:, half:]


VMEM = pl.BlockSpec(memory_space=pltpu.VMEM)
HBM = pl.BlockSpec(memory_space=pltpu.HBM)


def kernel_call(body, name, out_shape, in_specs, scratch=(), limit=VMEM_LIMIT):
    return pl.pallas_call(
        body,
        out_shape=out_shape,
        in_specs=in_specs,
        out_specs=jax.tree.map(lambda _: VMEM, out_shape),
        scratch_shapes=list(scratch),
        compiler_params=pltpu.CompilerParams(vmem_limit_bytes=limit),
        name=name,
    )


def on_device(queries, grad_out, keys, values, proj_query, section_span, span_prefix):
    n_seq, n_head = lax.axis_size("seq"), lax.axis_size("head")
    n_other = n_head - 1
    direct = n_seq <= MOST_PARTNERS and n_seq & (n_seq - 1) == 0
    low = jnp.bfloat16
    _, held, kv_width = keys.shape
    _, rows, width = queries.shape
    feats = proj_query.shape[1] // n_head

    def shape(*dims, dtype=low):
        return jax.ShapeDtypeStruct(dims, dtype)

    first = feats // 16 * 9 // 16 * 16
    partners = sorted(range(1, n_seq), key=lambda r: -r.bit_length()) if direct else []
    n_copies = 1 + len(partners)
    *joined, grad_low, grad_high = kernel_call(
        functools.partial(join_kernel, n_copies),
        "join",
        [shape(held, 2 * kv_width)] * n_copies + [shape(rows // 2, width)] * 2,
        [HBM] * 3,
        [pltpu.SemaphoreType.DMA((4,))],
    )(*[in_hbm(x) for x in (keys, values, grad_out)])
    if direct:
        blocks = joined[-1:] + [swapped(x, "seq", r) for x, r in zip(joined, partners)]
    else:
        blocks = [lax.all_gather(joined[0], "seq", axis=0, tiled=True)]
    n_blocks, block_rows = len(blocks), blocks[0].shape[0]
    incoming = [shifted(part, "section", -1) for part in (grad_low, grad_high)]

    limit, q, *w_other = kernel_call(
        functools.partial(stage_kernel, n_head),
        "stage",
        [shape(8, HD, dtype=jnp.int32), shape(rows, width)] + [shape(feats, width)] * n_other,
        [HBM] * 4,
        [
            pltpu.SMEM(section_span.shape, jnp.int32),
            pltpu.SMEM(span_prefix.shape, jnp.int32),
            pltpu.SemaphoreType.DMA((1 + n_other,)),
            pltpu.SemaphoreType.DMA((2,)),
        ],
    )(*[in_hbm(x) for x in (section_span, span_prefix, queries, proj_query)])

    prefix = n_blocks * block_rows
    weights = shape(kv_width // HD, prefix, 2 * rows)
    grad_query, probs, dscores, *products = kernel_call(
        functools.partial(attention_kernel, partners, n_other),
        "attention",
        [shape(width, rows), weights, weights] + [shape(first, rows)] * n_other,
        [VMEM] * (4 + n_blocks + n_other),
    )(limit, q, *blocks, *incoming, *w_other)
    rest = kernel_call(
        functools.partial(rest_kernel, n_other),
        "rest",
        [shape(feats - first, rows)] * n_other,
        [VMEM] * (1 + n_other),
    )(grad_query, *w_other)
    arrived = [shifted(p, "head", r + 1) for part in (products, rest) for r, p in enumerate(part)]
    terms = kernel_call(
        terms_kernel, "terms", [shape(block_rows, 2 * kv_width)] * n_blocks, [VMEM] * 5
    )(probs, dscores, q, *incoming)
    if direct:
        sent = sorted(zip(partners, terms[1:]), key=lambda pair: pair[0])
        all_terms = [terms[0]] + [swapped(x, "seq", r) for r, x in sent]
    else:
        all_terms = [lax.psum_scatter(terms[0], "seq", scatter_dimension=0, tiled=True)]

    own = kernel_call(
        functools.partial(own_kernel, n_head),
        "own",
        shape(feats, rows, dtype=jnp.float32),
        [VMEM, HBM],
        [pltpu.VMEM((feats, width), low), pltpu.SemaphoreType.DMA(())],
    )(grad_query, in_hbm(proj_query))
    grad_key, grad_value = kernel_call(
        term_sum_kernel, "term_sum", [shape(1, held, kv_width)] * 2, [VMEM] * len(all_terms)
    )(*all_terms)
    grad_input = []
    for start, part in ((0, arrived[:n_other]), (first, arrived[n_other:])):
        grad_input = [
            pl.pallas_call(
                functools.partial(input_sum_kernel, n_other, start),
                out_shape=shape(1, feats, rows),
                in_specs=[VMEM] * (1 + n_other) + [HBM] * len(grad_input),
                out_specs=HBM,
                scratch_shapes=[pltpu.VMEM(part[0].shape, low), pltpu.SemaphoreType.DMA(())],
                input_output_aliases={1 + n_other: 0} if grad_input else {},
                compiler_params=pltpu.CompilerParams(vmem_limit_bytes=VMEM_LIMIT),
                name="input_sum",
            )(own, *part, *grad_input)
        ]
    grad_input = grad_input[0]
    return (grad_input, grad_key, grad_value)


def solution(mesh):
    in_specs = (
        P("section", "seq", "head"),
        P("section", "seq", "head"),
        P("section", "seq", "head"),
        P("section", "seq", "head"),
        P("section", None, "head"),
        P(),
        P(),
    )
    out_specs = (
        P("section", "head", "seq"),
        P("section", "seq", "head"),
        P("section", "seq", "head"),
    )
    return jax.shard_map(
        on_device, mesh=mesh, in_specs=in_specs, out_specs=out_specs, check_vma=False
    )
```

```python
import functools
import math

import jax
import jax.numpy as jnp
from jax import lax
from jax.experimental import pallas as pl
from jax.experimental.pallas import tpu as pltpu
from jax.sharding import PartitionSpec as P

HD = 128
MOST_PARTNERS = 4
VMEM_LIMIT = 40 * 1024 * 1024

query_scale = 168.0 ** (-0.5)
exp2_scale = query_scale * math.log2(math.e)


def shifted(block, axis, distance):
    devices = range(lax.axis_size(axis))
    route = [((i - distance) % len(devices), i) for i in devices]
    return lax.ppermute(block, axis, route)


def swapped(block, axis, distance):
    return lax.ppermute(block, axis, [(i, i ^ distance) for i in range(lax.axis_size(axis))])


def dot(left, right, left_dim, right_dim):
    return lax.dot_general(
        left, right, (((left_dim,), (right_dim,)), ((), ())), preferred_element_type=jnp.float32
    )


def in_hbm(x):
    return pltpu.with_memory_space_constraint(x, pltpu.HBM)


def join_kernel(n_copies, key_ref, value_ref, grad_ref, *refs):
    *outs, grad_low, grad_high, sems = refs
    width, rows = key_ref.shape[2], grad_low.shape[0]
    pairs = [
        (key_ref.at[0], outs[0].at[:, :width]),
        (value_ref.at[0], outs[0].at[:, width:]),
        (grad_ref.at[0, :rows, :], grad_low),
        (grad_ref.at[0, rows:, :], grad_high),
    ]
    copies = [pltpu.make_async_copy(a, b, sems.at[i]) for i, (a, b) in enumerate(pairs)]
    for copy in copies:
        copy.start()
    for copy in copies[:2]:
        copy.wait()
    for out in outs[1:]:
        out[...] = outs[0][...]
    for copy in copies[2:]:
        copy.wait()


def stage_kernel(n_head, span_ref, prefix_ref, q_ref, w_ref, limit_out, q_out, *refs):
    *other_outs, span, prefix, sems, small_sems = refs
    feats = w_ref.shape[1] // n_head
    head = lax.axis_index("head")
    copies = []
    for r, out in enumerate(other_outs):
        start = pl.multiple_of(lax.rem(head + r + 1, n_head) * feats, 16)
        copies.append((w_ref.at[0, pl.ds(start, feats), :], out))
    copies.append((q_ref.at[0], q_out))
    copies = [pltpu.make_async_copy(a, b, sems.at[i]) for i, (a, b) in enumerate(copies)]
    small = [
        pltpu.make_async_copy(a, b, small_sems.at[i])
        for i, (a, b) in enumerate([(span_ref, span), (prefix_ref, prefix)])
    ]
    for copy in small + copies:
        copy.start()
    for copy in small:
        copy.wait()
    live = prefix[span[lax.axis_index("section")]]
    limit_out[...] = jnp.full(limit_out.shape, live, jnp.int32)
    for copy in copies:
        copy.wait()


def pair_of(refs, g):
    cols = [slice((2 * g + i) * HD, (2 * g + i + 1) * HD) for i in range(2)]
    return jnp.concatenate([ref[:, c] for c in cols for ref in refs], axis=0)


def cols_of(g, start=0):
    return slice(start + g * HD, start + (g + 1) * HD)


def attention_kernel(partners, n_other, limit_ref, q_ref, *refs):
    n_blocks = 1 + len(partners)
    kv_refs = refs[:n_blocks]
    d_low, d_high, *refs = refs[n_blocks:]
    w_refs = refs[:n_other]
    grad_ref, probs_ref, dscores_ref, *part_refs = refs[n_other:]

    held, both = kv_refs[0].shape
    width = both // 2
    seq = lax.axis_index("seq")
    spots = []
    for r in [0, *partners]:
        first = jnp.bitwise_xor(seq, r) * held if partners else 0
        spots.append(first + lax.broadcasted_iota(jnp.int32, (held, 1), 0))
    alive = jnp.concatenate(spots, axis=0) < limit_ref[0:1, 0:1]

    rows = q_ref.shape[0]
    groups = range(width // HD)
    keys = [jnp.concatenate([ref[:, cols_of(g)] for ref in kv_refs], axis=0) for g in groups]
    scores = [dot(keys[g], pair_of((q_ref,), g), 1, 1) for g in groups]
    dprobs = []
    for g in groups:
        value = jnp.concatenate([ref[:, cols_of(g, width)] for ref in kv_refs], axis=0)
        dprobs.append(dot(value, pair_of((d_low, d_high), g), 1, 1))
    for g in groups:
        masked = jnp.where(alive, scores[g], jnp.float32(-1e30))
        top = jnp.max(masked, axis=0, keepdims=True)
        probs = jnp.exp2((masked - top) * exp2_scale)
        probs = probs * (1.0 / jnp.sum(probs, axis=0, keepdims=True))
        probs_low = probs.astype(jnp.bfloat16)
        delta = jnp.sum(probs_low.astype(jnp.float32) * dprobs[g], axis=0, keepdims=True)
        probs_ref[g] = probs_low
        dscores_ref[g] = (probs * (dprobs[g] - delta)).astype(jnp.bfloat16)
    for g in groups:
        grad_q = (query_scale * dot(keys[g], dscores_ref[g], 0, 0)).astype(jnp.bfloat16)
        for i in range(2):
            spot = (2 * g + i) * HD
            grad_ref[spot : spot + HD, :] = grad_q[:, i * rows : (i + 1) * rows]

    for w_ref, part_ref in zip(w_refs, part_refs):
        block = w_ref[: part_ref.shape[0], :]
        part_ref[...] = dot(block, grad_ref[...], 1, 0).astype(jnp.bfloat16)


def rest_kernel(n_other, grad_ref, *refs):
    for w_ref, part_ref in zip(refs[:n_other], refs[n_other:]):
        block = w_ref[w_ref.shape[0] - part_ref.shape[0] :, :]
        part_ref[...] = dot(block, grad_ref[...], 1, 0).astype(jnp.bfloat16)


def terms_kernel(probs_ref, dscores_ref, q_ref, d_low, d_high, *term_refs):
    held, both = term_refs[0].shape
    width = both // 2
    for g in range(width // HD):
        grad_k = (query_scale * dot(dscores_ref[g], pair_of((q_ref,), g), 1, 0)).astype(jnp.bfloat16)
        grad_v = dot(probs_ref[g], pair_of((d_low, d_high), g), 1, 0).astype(jnp.bfloat16)
        for r, ref in enumerate(term_refs):
            block = slice(r * held, (r + 1) * held)
            ref[:, g * HD : (g + 1) * HD] = grad_k[block]
            ref[:, width + g * HD : width + (g + 1) * HD] = grad_v[block]


def own_kernel(n_head, grad_ref, w_ref, out_ref, w_held, sem):
    feats = out_ref.shape[0]
    start = pl.multiple_of(lax.axis_index("head") * feats, 16)
    copy = pltpu.make_async_copy(w_ref.at[0, pl.ds(start, feats), :], w_held, sem)
    copy.start()
    copy.wait()
    out_ref[...] = dot(w_held[...], grad_ref[...], 1, 0)


def input_sum_kernel(n_other, start, own_ref, *refs):
    arrived = refs[:n_other]
    *_, out_ref, held, sem = refs
    at = slice(start, start + held.shape[0])
    total = own_ref[at, :]
    for ref in arrived:
        total = total + ref[...].astype(jnp.float32)
    held[...] = total.astype(jnp.bfloat16)
    copy = pltpu.make_async_copy(held, out_ref.at[0, at, :], sem)
    copy.start()
    copy.wait()


def term_sum_kernel(*refs):
    *terms, key_ref, value_ref = refs
    total = terms[0][...].astype(jnp.float32)
    for ref in terms[1:]:
        total = total + ref[...].astype(jnp.float32)
    low = total.astype(jnp.bfloat16)
    half = low.shape[1] // 2
    key_ref[0] = low[:, :half]
    value_ref[0] = low[:, half:]


VMEM = pl.BlockSpec(memory_space=pltpu.VMEM)
HBM = pl.BlockSpec(memory_space=pltpu.HBM)


def kernel_call(body, name, out_shape, in_specs, scratch=(), limit=VMEM_LIMIT):
    return pl.pallas_call(
        body,
        out_shape=out_shape,
        in_specs=in_specs,
        out_specs=jax.tree.map(lambda _: VMEM, out_shape),
        scratch_shapes=list(scratch),
        compiler_params=pltpu.CompilerParams(vmem_limit_bytes=limit),
        name=name,
    )


def on_device(queries, grad_out, keys, values, proj_query, section_span, span_prefix):
    n_seq, n_head = lax.axis_size("seq"), lax.axis_size("head")
    n_other = n_head - 1
    direct = n_seq <= MOST_PARTNERS and n_seq & (n_seq - 1) == 0
    low = jnp.bfloat16
    _, held, kv_width = keys.shape
    _, rows, width = queries.shape
    feats = proj_query.shape[1] // n_head

    def shape(*dims, dtype=low):
        return jax.ShapeDtypeStruct(dims, dtype)

    first = feats // 16 * 9 // 16 * 16
    partners = list(range(n_seq - 1, 0, -1)) if direct else []
    n_copies = 1 + len(partners)
    *joined, grad_low, grad_high = kernel_call(
        functools.partial(join_kernel, n_copies),
        "join",
        [shape(held, 2 * kv_width)] * n_copies + [shape(rows // 2, width)] * 2,
        [HBM] * 3,
        [pltpu.SemaphoreType.DMA((4,))],
    )(*[in_hbm(x) for x in (keys, values, grad_out)])
    if direct:
        blocks = joined[-1:] + [swapped(x, "seq", r) for x, r in zip(joined, partners)]
    else:
        blocks = [lax.all_gather(joined[0], "seq", axis=0, tiled=True)]
    n_blocks, block_rows = len(blocks), blocks[0].shape[0]
    incoming = [shifted(part, "section", -1) for part in (grad_low, grad_high)]

    limit, q, *w_other = kernel_call(
        functools.partial(stage_kernel, n_head),
        "stage",
        [shape(8, HD, dtype=jnp.int32), shape(rows, width)] + [shape(feats, width)] * n_other,
        [HBM] * 4,
        [
            pltpu.SMEM(section_span.shape, jnp.int32),
            pltpu.SMEM(span_prefix.shape, jnp.int32),
            pltpu.SemaphoreType.DMA((1 + n_other,)),
            pltpu.SemaphoreType.DMA((2,)),
        ],
    )(*[in_hbm(x) for x in (section_span, span_prefix, queries, proj_query)])

    prefix = n_blocks * block_rows
    weights = shape(kv_width // HD, prefix, 2 * rows)
    grad_query, probs, dscores, *products = kernel_call(
        functools.partial(attention_kernel, partners, n_other),
        "attention",
        [shape(width, rows), weights, weights] + [shape(first, rows)] * n_other,
        [VMEM] * (4 + n_blocks + n_other),
    )(limit, q, *blocks, *incoming, *w_other)
    rest = kernel_call(
        functools.partial(rest_kernel, n_other),
        "rest",
        [shape(feats - first, rows)] * n_other,
        [VMEM] * (1 + n_other),
    )(grad_query, *w_other)
    arrived = [shifted(p, "head", r + 1) for part in (products, rest) for r, p in enumerate(part)]
    terms = kernel_call(
        terms_kernel, "terms", [shape(block_rows, 2 * kv_width)] * n_blocks, [VMEM] * 5
    )(probs, dscores, q, *incoming)
    if direct:
        sent = sorted(zip(partners, terms[1:]), key=lambda pair: pair[0])
        all_terms = [terms[0]] + [swapped(x, "seq", r) for r, x in sent]
    else:
        all_terms = [lax.psum_scatter(terms[0], "seq", scatter_dimension=0, tiled=True)]

    own = kernel_call(
        functools.partial(own_kernel, n_head),
        "own",
        shape(feats, rows, dtype=jnp.float32),
        [VMEM, HBM],
        [pltpu.VMEM((feats, width), low), pltpu.SemaphoreType.DMA(())],
    )(grad_query, in_hbm(proj_query))
    grad_key, grad_value = kernel_call(
        term_sum_kernel, "term_sum", [shape(1, held, kv_width)] * 2, [VMEM] * len(all_terms)
    )(*all_terms)
    grad_input = []
    for start, part in ((0, arrived[:n_other]), (first, arrived[n_other:])):
        grad_input = [
            pl.pallas_call(
                functools.partial(input_sum_kernel, n_other, start),
                out_shape=shape(1, feats, rows),
                in_specs=[VMEM] * (1 + n_other) + [HBM] * len(grad_input),
                out_specs=HBM,
                scratch_shapes=[pltpu.VMEM(part[0].shape, low), pltpu.SemaphoreType.DMA(())],
                input_output_aliases={1 + n_other: 0} if grad_input else {},
                compiler_params=pltpu.CompilerParams(vmem_limit_bytes=VMEM_LIMIT),
                name="input_sum",
            )(own, *part, *grad_input)
        ]
    grad_input = grad_input[0]
    return (grad_input, grad_key, grad_value)


def solution(mesh):
    in_specs = (
        P("section", "seq", "head"),
        P("section", "seq", "head"),
        P("section", "seq", "head"),
        P("section", "seq", "head"),
        P("section", None, "head"),
        P(),
        P(),
    )
    out_specs = (
        P("section", "head", "seq"),
        P("section", "seq", "head"),
        P("section", "seq", "head"),
    )
    return jax.shard_map(
        on_device, mesh=mesh, in_specs=in_specs, out_specs=out_specs, check_vma=False
    )
```

```python
import functools
import math

import jax
import jax.numpy as jnp
from jax import lax
from jax.experimental import pallas as pl
from jax.experimental.pallas import tpu as pltpu
from jax.sharding import PartitionSpec as P

HD = 128
MOST_PARTNERS = 4
VMEM_LIMIT = 40 * 1024 * 1024

query_scale = 168.0 ** (-0.5)
exp2_scale = query_scale * math.log2(math.e)


def shifted(block, axis, distance):
    devices = range(lax.axis_size(axis))
    route = [((i - distance) % len(devices), i) for i in devices]
    return lax.ppermute(block, axis, route)


def swapped(block, axis, distance):
    return lax.ppermute(block, axis, [(i, i ^ distance) for i in range(lax.axis_size(axis))])


def dot(left, right, left_dim, right_dim):
    return lax.dot_general(
        left, right, (((left_dim,), (right_dim,)), ((), ())), preferred_element_type=jnp.float32
    )


def in_hbm(x):
    return pltpu.with_memory_space_constraint(x, pltpu.HBM)


def join_kernel(n_copies, key_ref, value_ref, grad_ref, *refs):
    *outs, grad_low, grad_high, sems = refs
    width, rows = key_ref.shape[2], grad_low.shape[0]
    pairs = [
        (key_ref.at[0], outs[0].at[:, :width]),
        (value_ref.at[0], outs[0].at[:, width:]),
        (grad_ref.at[0, :rows, :], grad_low),
        (grad_ref.at[0, rows:, :], grad_high),
    ]
    copies = [pltpu.make_async_copy(a, b, sems.at[i]) for i, (a, b) in enumerate(pairs)]
    for copy in copies:
        copy.start()
    for copy in copies[:2]:
        copy.wait()
    for out in outs[1:]:
        out[...] = outs[0][...]
    for copy in copies[2:]:
        copy.wait()


def stage_kernel(n_head, span_ref, prefix_ref, q_ref, w_ref, limit_out, q_out, *refs):
    *other_outs, span, prefix, sems, small_sems = refs
    feats = w_ref.shape[1] // n_head
    head = lax.axis_index("head")
    copies = []
    for r, out in enumerate(other_outs):
        start = pl.multiple_of(lax.rem(head + r + 1, n_head) * feats, 16)
        copies.append((w_ref.at[0, pl.ds(start, feats), :], out))
    copies.append((q_ref.at[0], q_out))
    copies = [pltpu.make_async_copy(a, b, sems.at[i]) for i, (a, b) in enumerate(copies)]
    small = [
        pltpu.make_async_copy(a, b, small_sems.at[i])
        for i, (a, b) in enumerate([(span_ref, span), (prefix_ref, prefix)])
    ]
    for copy in small + copies:
        copy.start()
    for copy in small:
        copy.wait()
    live = prefix[span[lax.axis_index("section")]]
    limit_out[...] = jnp.full(limit_out.shape, live, jnp.int32)
    for copy in copies:
        copy.wait()


def pair_of(refs, g):
    cols = [slice((2 * g + i) * HD, (2 * g + i + 1) * HD) for i in range(2)]
    return jnp.concatenate([ref[:, c] for c in cols for ref in refs], axis=0)


def cols_of(g, start=0):
    return slice(start + g * HD, start + (g + 1) * HD)


def attention_kernel(partners, n_other, limit_ref, q_ref, *refs):
    n_blocks = 1 + len(partners)
    kv_refs = refs[:n_blocks]
    d_low, d_high, *refs = refs[n_blocks:]
    w_refs = refs[:n_other]
    grad_ref, probs_ref, dscores_ref, *part_refs = refs[n_other:]

    held, both = kv_refs[0].shape
    width = both // 2
    seq = lax.axis_index("seq")
    spots = []
    for r in [0, *partners]:
        first = jnp.bitwise_xor(seq, r) * held if partners else 0
        spots.append(first + lax.broadcasted_iota(jnp.int32, (held, 1), 0))
    alive = jnp.concatenate(spots, axis=0) < limit_ref[0:1, 0:1]

    rows = q_ref.shape[0]
    groups = range(width // HD)
    keys = [jnp.concatenate([ref[:, cols_of(g)] for ref in kv_refs], axis=0) for g in groups]
    scores = [dot(keys[g], pair_of((q_ref,), g), 1, 1) for g in groups]
    dprobs = []
    for g in groups:
        value = jnp.concatenate([ref[:, cols_of(g, width)] for ref in kv_refs], axis=0)
        dprobs.append(dot(value, pair_of((d_low, d_high), g), 1, 1))
    for g in groups:
        masked = jnp.where(alive, scores[g], jnp.float32(-1e30))
        top = jnp.max(masked, axis=0, keepdims=True)
        probs = jnp.exp2((masked - top) * exp2_scale)
        probs = probs * (1.0 / jnp.sum(probs, axis=0, keepdims=True))
        probs_low = probs.astype(jnp.bfloat16)
        delta = jnp.sum(probs_low.astype(jnp.float32) * dprobs[g], axis=0, keepdims=True)
        probs_ref[g] = probs_low
        dscores_ref[g] = (probs * (dprobs[g] - delta)).astype(jnp.bfloat16)
    for g in groups:
        grad_q = (query_scale * dot(keys[g], dscores_ref[g], 0, 0)).astype(jnp.bfloat16)
        for i in range(2):
            spot = (2 * g + i) * HD
            grad_ref[spot : spot + HD, :] = grad_q[:, i * rows : (i + 1) * rows]

    for w_ref, part_ref in zip(w_refs, part_refs):
        block = w_ref[: part_ref.shape[0], :]
        part_ref[...] = dot(block, grad_ref[...], 1, 0).astype(jnp.bfloat16)


def rest_kernel(n_other, grad_ref, *refs):
    for w_ref, part_ref in zip(refs[:n_other], refs[n_other:]):
        block = w_ref[w_ref.shape[0] - part_ref.shape[0] :, :]
        part_ref[...] = dot(block, grad_ref[...], 1, 0).astype(jnp.bfloat16)


def terms_kernel(probs_ref, dscores_ref, q_ref, d_low, d_high, *term_refs):
    held, both = term_refs[0].shape
    width = both // 2
    for g in range(width // HD):
        grad_k = (query_scale * dot(dscores_ref[g], pair_of((q_ref,), g), 1, 0)).astype(jnp.bfloat16)
        grad_v = dot(probs_ref[g], pair_of((d_low, d_high), g), 1, 0).astype(jnp.bfloat16)
        for r, ref in enumerate(term_refs):
            block = slice(r * held, (r + 1) * held)
            ref[:, g * HD : (g + 1) * HD] = grad_k[block]
            ref[:, width + g * HD : width + (g + 1) * HD] = grad_v[block]


def own_kernel(n_head, grad_ref, w_ref, out_ref, w_held, sem):
    feats = out_ref.shape[0]
    start = pl.multiple_of(lax.axis_index("head") * feats, 16)
    copy = pltpu.make_async_copy(w_ref.at[0, pl.ds(start, feats), :], w_held, sem)
    copy.start()
    copy.wait()
    out_ref[...] = dot(w_held[...], grad_ref[...], 1, 0)


def input_sum_kernel(n_other, start, own_ref, *refs):
    arrived = refs[:n_other]
    *_, out_ref, held, sem = refs
    at = slice(start, start + held.shape[0])
    total = own_ref[at, :]
    for ref in arrived:
        total = total + ref[...].astype(jnp.float32)
    held[...] = total.astype(jnp.bfloat16)
    copy = pltpu.make_async_copy(held, out_ref.at[0, at, :], sem)
    copy.start()
    copy.wait()


def term_sum_kernel(*refs):
    *terms, key_ref, value_ref = refs
    total = terms[0][...].astype(jnp.float32)
    for ref in terms[1:]:
        total = total + ref[...].astype(jnp.float32)
    low = total.astype(jnp.bfloat16)
    half = low.shape[1] // 2
    key_ref[0] = low[:, :half]
    value_ref[0] = low[:, half:]


VMEM = pl.BlockSpec(memory_space=pltpu.VMEM)
HBM = pl.BlockSpec(memory_space=pltpu.HBM)


def kernel_call(body, name, out_shape, in_specs, scratch=(), limit=VMEM_LIMIT):
    return pl.pallas_call(
        body,
        out_shape=out_shape,
        in_specs=in_specs,
        out_specs=jax.tree.map(lambda _: VMEM, out_shape),
        scratch_shapes=list(scratch),
        compiler_params=pltpu.CompilerParams(vmem_limit_bytes=limit),
        name=name,
    )


def on_device(queries, grad_out, keys, values, proj_query, section_span, span_prefix):
    n_seq, n_head = lax.axis_size("seq"), lax.axis_size("head")
    n_other = n_head - 1
    direct = n_seq <= MOST_PARTNERS and n_seq & (n_seq - 1) == 0
    low = jnp.bfloat16
    _, held, kv_width = keys.shape
    _, rows, width = queries.shape
    feats = proj_query.shape[1] // n_head

    def shape(*dims, dtype=low):
        return jax.ShapeDtypeStruct(dims, dtype)

    first = feats // 16 * 9 // 16 * 16
    partners = list(range(1, n_seq)) if direct else []
    n_copies = 1 + len(partners)
    *joined, grad_low, grad_high = kernel_call(
        functools.partial(join_kernel, n_copies),
        "join",
        [shape(held, 2 * kv_width)] * n_copies + [shape(rows // 2, width)] * 2,
        [HBM] * 3,
        [pltpu.SemaphoreType.DMA((4,))],
    )(*[in_hbm(x) for x in (keys, values, grad_out)])
    if direct:
        blocks = joined[-1:] + [swapped(x, "seq", r) for x, r in zip(joined, partners)]
    else:
        blocks = [lax.all_gather(joined[0], "seq", axis=0, tiled=True)]
    n_blocks, block_rows = len(blocks), blocks[0].shape[0]
    incoming = [shifted(part, "section", -1) for part in (grad_low, grad_high)]

    limit, q, *w_other = kernel_call(
        functools.partial(stage_kernel, n_head),
        "stage",
        [shape(8, HD, dtype=jnp.int32), shape(rows, width)] + [shape(feats, width)] * n_other,
        [HBM] * 4,
        [
            pltpu.SMEM(section_span.shape, jnp.int32),
            pltpu.SMEM(span_prefix.shape, jnp.int32),
            pltpu.SemaphoreType.DMA((1 + n_other,)),
            pltpu.SemaphoreType.DMA((2,)),
        ],
    )(*[in_hbm(x) for x in (section_span, span_prefix, queries, proj_query)])

    prefix = n_blocks * block_rows
    weights = shape(kv_width // HD, prefix, 2 * rows)
    grad_query, probs, dscores, *products = kernel_call(
        functools.partial(attention_kernel, partners, n_other),
        "attention",
        [shape(width, rows), weights, weights] + [shape(first, rows)] * n_other,
        [VMEM] * (4 + n_blocks + n_other),
    )(limit, q, *blocks, *incoming, *w_other)
    rest = kernel_call(
        functools.partial(rest_kernel, n_other),
        "rest",
        [shape(feats - first, rows)] * n_other,
        [VMEM] * (1 + n_other),
    )(grad_query, *w_other)
    arrived = [shifted(p, "head", r + 1) for part in (products, rest) for r, p in enumerate(part)]
    terms = kernel_call(
        terms_kernel, "terms", [shape(block_rows, 2 * kv_width)] * n_blocks, [VMEM] * 5
    )(probs, dscores, q, *incoming)
    if direct:
        sent = sorted(zip(partners, terms[1:]), key=lambda pair: pair[0])
        all_terms = [terms[0]] + [swapped(x, "seq", r) for r, x in sent]
    else:
        all_terms = [lax.psum_scatter(terms[0], "seq", scatter_dimension=0, tiled=True)]

    own = kernel_call(
        functools.partial(own_kernel, n_head),
        "own",
        shape(feats, rows, dtype=jnp.float32),
        [VMEM, HBM],
        [pltpu.VMEM((feats, width), low), pltpu.SemaphoreType.DMA(())],
    )(grad_query, in_hbm(proj_query))
    grad_key, grad_value = kernel_call(
        term_sum_kernel, "term_sum", [shape(1, held, kv_width)] * 2, [VMEM] * len(all_terms)
    )(*all_terms)
    grad_input = []
    for start, part in ((0, arrived[:n_other]), (first, arrived[n_other:])):
        grad_input = [
            pl.pallas_call(
                functools.partial(input_sum_kernel, n_other, start),
                out_shape=shape(1, feats, rows),
                in_specs=[VMEM] * (1 + n_other) + [HBM] * len(grad_input),
                out_specs=HBM,
                scratch_shapes=[pltpu.VMEM(part[0].shape, low), pltpu.SemaphoreType.DMA(())],
                input_output_aliases={1 + n_other: 0} if grad_input else {},
                compiler_params=pltpu.CompilerParams(vmem_limit_bytes=VMEM_LIMIT),
                name="input_sum",
            )(own, *part, *grad_input)
        ]
    grad_input = grad_input[0]
    return (grad_input, grad_key, grad_value)


def solution(mesh):
    in_specs = (
        P("section", "seq", "head"),
        P("section", "seq", "head"),
        P("section", "seq", "head"),
        P("section", "seq", "head"),
        P("section", None, "head"),
        P(),
        P(),
    )
    out_specs = (
        P("section", "head", "seq"),
        P("section", "seq", "head"),
        P("section", "seq", "head"),
    )
    return jax.shard_map(
        on_device, mesh=mesh, in_specs=in_specs, out_specs=out_specs, check_vma=False
    )
```

```python
import functools
import math

import jax
import jax.numpy as jnp
from jax import lax
from jax.experimental import pallas as pl
from jax.experimental.pallas import tpu as pltpu
from jax.sharding import PartitionSpec as P

HD = 128
MOST_PARTNERS = 4
VMEM_LIMIT = 40 * 1024 * 1024

query_scale = 168.0 ** (-0.5)
exp2_scale = query_scale * math.log2(math.e)


def shifted(block, axis, distance):
    devices = range(lax.axis_size(axis))
    route = [((i - distance) % len(devices), i) for i in devices]
    return lax.ppermute(block, axis, route)


def swapped(block, axis, distance):
    return lax.ppermute(block, axis, [(i, i ^ distance) for i in range(lax.axis_size(axis))])


def dot(left, right, left_dim, right_dim):
    return lax.dot_general(
        left, right, (((left_dim,), (right_dim,)), ((), ())), preferred_element_type=jnp.float32
    )


def in_hbm(x):
    return pltpu.with_memory_space_constraint(x, pltpu.HBM)


def join_kernel(n_copies, key_ref, value_ref, grad_ref, *refs):
    *outs, grad_low, grad_high, sems = refs
    width, rows = key_ref.shape[2], grad_low.shape[0]
    pairs = [
        (key_ref.at[0], outs[0].at[:, :width]),
        (value_ref.at[0], outs[0].at[:, width:]),
        (grad_ref.at[0, :rows, :], grad_low),
        (grad_ref.at[0, rows:, :], grad_high),
    ]
    copies = [pltpu.make_async_copy(a, b, sems.at[i]) for i, (a, b) in enumerate(pairs)]
    for copy in copies:
        copy.start()
    for copy in copies[:2]:
        copy.wait()
    for out in outs[1:]:
        out[...] = outs[0][...]
    for copy in copies[2:]:
        copy.wait()


def stage_kernel(n_head, span_ref, prefix_ref, q_ref, w_ref, limit_out, q_out, *refs):
    *other_outs, span, prefix, sems, small_sems = refs
    feats = w_ref.shape[1] // n_head
    head = lax.axis_index("head")
    copies = []
    for r, out in enumerate(other_outs):
        start = pl.multiple_of(lax.rem(head + r + 1, n_head) * feats, 16)
        copies.append((w_ref.at[0, pl.ds(start, feats), :], out))
    copies.append((q_ref.at[0], q_out))
    copies = [pltpu.make_async_copy(a, b, sems.at[i]) for i, (a, b) in enumerate(copies)]
    small = [
        pltpu.make_async_copy(a, b, small_sems.at[i])
        for i, (a, b) in enumerate([(span_ref, span), (prefix_ref, prefix)])
    ]
    for copy in small + copies:
        copy.start()
    for copy in small:
        copy.wait()
    live = prefix[span[lax.axis_index("section")]]
    limit_out[...] = jnp.full(limit_out.shape, live, jnp.int32)
    for copy in copies:
        copy.wait()


def pair_of(refs, g):
    cols = [slice((2 * g + i) * HD, (2 * g + i + 1) * HD) for i in range(2)]
    return jnp.concatenate([ref[:, c] for c in cols for ref in refs], axis=0)


def cols_of(g, start=0):
    return slice(start + g * HD, start + (g + 1) * HD)


def attention_kernel(partners, n_other, limit_ref, q_ref, *refs):
    n_blocks = 1 + len(partners)
    kv_refs = refs[:n_blocks]
    d_low, d_high, *refs = refs[n_blocks:]
    w_refs = refs[:n_other]
    grad_ref, probs_ref, dscores_ref, *part_refs = refs[n_other:]

    held, both = kv_refs[0].shape
    width = both // 2
    seq = lax.axis_index("seq")
    spots = []
    for r in [0, *partners]:
        first = jnp.bitwise_xor(seq, r) * held if partners else 0
        spots.append(first + lax.broadcasted_iota(jnp.int32, (held, 1), 0))
    alive = jnp.concatenate(spots, axis=0) < limit_ref[0:1, 0:1]

    rows = q_ref.shape[0]
    groups = range(width // HD)
    keys = [jnp.concatenate([ref[:, cols_of(g)] for ref in kv_refs], axis=0) for g in groups]
    scores = [dot(keys[g], pair_of((q_ref,), g), 1, 1) for g in groups]
    dprobs = []
    for g in groups:
        value = jnp.concatenate([ref[:, cols_of(g, width)] for ref in kv_refs], axis=0)
        dprobs.append(dot(value, pair_of((d_low, d_high), g), 1, 1))
    for g in groups:
        masked = jnp.where(alive, scores[g], jnp.float32(-1e30))
        top = jnp.max(masked, axis=0, keepdims=True)
        probs = jnp.exp2((masked - top) * exp2_scale)
        probs = probs * (1.0 / jnp.sum(probs, axis=0, keepdims=True))
        probs_low = probs.astype(jnp.bfloat16)
        delta = jnp.sum(probs_low.astype(jnp.float32) * dprobs[g], axis=0, keepdims=True)
        probs_ref[g] = probs_low
        dscores_ref[g] = (probs * (dprobs[g] - delta)).astype(jnp.bfloat16)
    for g in groups:
        grad_q = (query_scale * dot(keys[g], dscores_ref[g], 0, 0)).astype(jnp.bfloat16)
        for i in range(2):
            spot = (2 * g + i) * HD
            grad_ref[spot : spot + HD, :] = grad_q[:, i * rows : (i + 1) * rows]

    for w_ref, part_ref in zip(w_refs, part_refs):
        block = w_ref[: part_ref.shape[0], :]
        part_ref[...] = dot(block, grad_ref[...], 1, 0).astype(jnp.bfloat16)


def rest_kernel(n_other, grad_ref, *refs):
    for w_ref, part_ref in zip(refs[:n_other], refs[n_other:]):
        block = w_ref[w_ref.shape[0] - part_ref.shape[0] :, :]
        part_ref[...] = dot(block, grad_ref[...], 1, 0).astype(jnp.bfloat16)


def terms_kernel(probs_ref, dscores_ref, q_ref, d_low, d_high, *term_refs):
    held, both = term_refs[0].shape
    width = both // 2
    for g in range(width // HD):
        grad_k = (query_scale * dot(dscores_ref[g], pair_of((q_ref,), g), 1, 0)).astype(jnp.bfloat16)
        grad_v = dot(probs_ref[g], pair_of((d_low, d_high), g), 1, 0).astype(jnp.bfloat16)
        for r, ref in enumerate(term_refs):
            block = slice(r * held, (r + 1) * held)
            ref[:, g * HD : (g + 1) * HD] = grad_k[block]
            ref[:, width + g * HD : width + (g + 1) * HD] = grad_v[block]


def own_kernel(n_head, grad_ref, w_ref, out_ref, w_held, sem):
    feats = out_ref.shape[0]
    start = pl.multiple_of(lax.axis_index("head") * feats, 16)
    copy = pltpu.make_async_copy(w_ref.at[0, pl.ds(start, feats), :], w_held, sem)
    copy.start()
    copy.wait()
    out_ref[...] = dot(w_held[...], grad_ref[...], 1, 0)


def input_sum_kernel(n_other, start, own_ref, *refs):
    arrived = refs[:n_other]
    *_, out_ref, held, sem = refs
    at = slice(start, start + held.shape[0])
    total = own_ref[at, :]
    for ref in arrived:
        total = total + ref[...].astype(jnp.float32)
    held[...] = total.astype(jnp.bfloat16)
    copy = pltpu.make_async_copy(held, out_ref.at[0, at, :], sem)
    copy.start()
    copy.wait()


def term_sum_kernel(*refs):
    *terms, key_ref, value_ref = refs
    total = terms[0][...].astype(jnp.float32)
    for ref in terms[1:]:
        total = total + ref[...].astype(jnp.float32)
    low = total.astype(jnp.bfloat16)
    half = low.shape[1] // 2
    key_ref[0] = low[:, :half]
    value_ref[0] = low[:, half:]


VMEM = pl.BlockSpec(memory_space=pltpu.VMEM)
HBM = pl.BlockSpec(memory_space=pltpu.HBM)


def kernel_call(body, name, out_shape, in_specs, scratch=(), limit=VMEM_LIMIT):
    return pl.pallas_call(
        body,
        out_shape=out_shape,
        in_specs=in_specs,
        out_specs=jax.tree.map(lambda _: VMEM, out_shape),
        scratch_shapes=list(scratch),
        compiler_params=pltpu.CompilerParams(vmem_limit_bytes=limit),
        name=name,
    )


def on_device(queries, grad_out, keys, values, proj_query, section_span, span_prefix):
    n_seq, n_head = lax.axis_size("seq"), lax.axis_size("head")
    n_other = n_head - 1
    direct = n_seq <= MOST_PARTNERS and n_seq & (n_seq - 1) == 0
    low = jnp.bfloat16
    _, held, kv_width = keys.shape
    _, rows, width = queries.shape
    feats = proj_query.shape[1] // n_head

    def shape(*dims, dtype=low):
        return jax.ShapeDtypeStruct(dims, dtype)

    first = feats // 16 * 9 // 16 * 16
    partners = sorted(range(1, n_seq), key=lambda r: (r.bit_count(), -r)) if direct else []
    n_copies = 1 + len(partners)
    *joined, grad_low, grad_high = kernel_call(
        functools.partial(join_kernel, n_copies),
        "join",
        [shape(held, 2 * kv_width)] * n_copies + [shape(rows // 2, width)] * 2,
        [HBM] * 3,
        [pltpu.SemaphoreType.DMA((4,))],
    )(*[in_hbm(x) for x in (keys, values, grad_out)])
    if direct:
        blocks = joined[-1:] + [swapped(x, "seq", r) for x, r in zip(joined, partners)]
    else:
        blocks = [lax.all_gather(joined[0], "seq", axis=0, tiled=True)]
    n_blocks, block_rows = len(blocks), blocks[0].shape[0]
    incoming = [shifted(part, "section", -1) for part in (grad_low, grad_high)]

    limit, q, *w_other = kernel_call(
        functools.partial(stage_kernel, n_head),
        "stage",
        [shape(8, HD, dtype=jnp.int32), shape(rows, width)] + [shape(feats, width)] * n_other,
        [HBM] * 4,
        [
            pltpu.SMEM(section_span.shape, jnp.int32),
            pltpu.SMEM(span_prefix.shape, jnp.int32),
            pltpu.SemaphoreType.DMA((1 + n_other,)),
            pltpu.SemaphoreType.DMA((2,)),
        ],
    )(*[in_hbm(x) for x in (section_span, span_prefix, queries, proj_query)])

    prefix = n_blocks * block_rows
    weights = shape(kv_width // HD, prefix, 2 * rows)
    grad_query, probs, dscores, *products = kernel_call(
        functools.partial(attention_kernel, partners, n_other),
        "attention",
        [shape(width, rows), weights, weights] + [shape(first, rows)] * n_other,
        [VMEM] * (4 + n_blocks + n_other),
    )(limit, q, *blocks, *incoming, *w_other)
    rest = kernel_call(
        functools.partial(rest_kernel, n_other),
        "rest",
        [shape(feats - first, rows)] * n_other,
        [VMEM] * (1 + n_other),
    )(grad_query, *w_other)
    arrived = [shifted(p, "head", r + 1) for part in (products, rest) for r, p in enumerate(part)]
    terms = kernel_call(
        terms_kernel, "terms", [shape(block_rows, 2 * kv_width)] * n_blocks, [VMEM] * 5
    )(probs, dscores, q, *incoming)
    if direct:
        sent = sorted(zip(partners, terms[1:]), key=lambda pair: pair[0])
        all_terms = [terms[0]] + [swapped(x, "seq", r) for r, x in sent]
    else:
        all_terms = [lax.psum_scatter(terms[0], "seq", scatter_dimension=0, tiled=True)]

    own = kernel_call(
        functools.partial(own_kernel, n_head),
        "own",
        shape(feats, rows, dtype=jnp.float32),
        [VMEM, HBM],
        [pltpu.VMEM((feats, width), low), pltpu.SemaphoreType.DMA(())],
    )(grad_query, in_hbm(proj_query))
    grad_key, grad_value = kernel_call(
        term_sum_kernel, "term_sum", [shape(1, held, kv_width)] * 2, [VMEM] * len(all_terms)
    )(*all_terms)
    grad_input = []
    for start, part in ((0, arrived[:n_other]), (first, arrived[n_other:])):
        grad_input = [
            pl.pallas_call(
                functools.partial(input_sum_kernel, n_other, start),
                out_shape=shape(1, feats, rows),
                in_specs=[VMEM] * (1 + n_other) + [HBM] * len(grad_input),
                out_specs=HBM,
                scratch_shapes=[pltpu.VMEM(part[0].shape, low), pltpu.SemaphoreType.DMA(())],
                input_output_aliases={1 + n_other: 0} if grad_input else {},
                compiler_params=pltpu.CompilerParams(vmem_limit_bytes=VMEM_LIMIT),
                name="input_sum",
            )(own, *part, *grad_input)
        ]
    grad_input = grad_input[0]
    return (grad_input, grad_key, grad_value)


def solution(mesh):
    in_specs = (
        P("section", "seq", "head"),
        P("section", "seq", "head"),
        P("section", "seq", "head"),
        P("section", "seq", "head"),
        P("section", None, "head"),
        P(),
        P(),
    )
    out_specs = (
        P("section", "head", "seq"),
        P("section", "seq", "head"),
        P("section", "seq", "head"),
    )
    return jax.shard_map(
        on_device, mesh=mesh, in_specs=in_specs, out_specs=out_specs, check_vma=False
    )
```

```python
import functools
import math

import jax
import jax.numpy as jnp
from jax import lax
from jax.experimental import pallas as pl
from jax.experimental.pallas import tpu as pltpu
from jax.sharding import PartitionSpec as P

HD = 128
MOST_PARTNERS = 4
VMEM_LIMIT = 40 * 1024 * 1024

query_scale = 168.0 ** (-0.5)
exp2_scale = query_scale * math.log2(math.e)


def shifted(block, axis, distance):
    devices = range(lax.axis_size(axis))
    route = [((i - distance) % len(devices), i) for i in devices]
    return lax.ppermute(block, axis, route)


def swapped(block, axis, distance):
    return lax.ppermute(block, axis, [(i, i ^ distance) for i in range(lax.axis_size(axis))])


def dot(left, right, left_dim, right_dim):
    return lax.dot_general(
        left, right, (((left_dim,), (right_dim,)), ((), ())), preferred_element_type=jnp.float32
    )


def in_hbm(x):
    return pltpu.with_memory_space_constraint(x, pltpu.HBM)


def join_kernel(n_copies, key_ref, value_ref, grad_ref, *refs):
    *outs, grad_low, grad_high, sems = refs
    width, rows = key_ref.shape[2], grad_low.shape[0]
    pairs = [
        (key_ref.at[0], outs[0].at[:, :width]),
        (value_ref.at[0], outs[0].at[:, width:]),
        (grad_ref.at[0, :rows, :], grad_low),
        (grad_ref.at[0, rows:, :], grad_high),
    ]
    copies = [pltpu.make_async_copy(a, b, sems.at[i]) for i, (a, b) in enumerate(pairs)]
    for copy in copies:
        copy.start()
    for copy in copies[:2]:
        copy.wait()
    for out in outs[1:]:
        out[...] = outs[0][...]
    for copy in copies[2:]:
        copy.wait()


def stage_kernel(n_head, span_ref, prefix_ref, q_ref, w_ref, limit_out, q_out, *refs):
    *other_outs, span, prefix, sems, small_sems = refs
    feats = w_ref.shape[1] // n_head
    head = lax.axis_index("head")
    copies = []
    for r, out in enumerate(other_outs):
        start = pl.multiple_of(lax.rem(head + r + 1, n_head) * feats, 16)
        copies.append((w_ref.at[0, pl.ds(start, feats), :], out))
    copies.append((q_ref.at[0], q_out))
    copies = [pltpu.make_async_copy(a, b, sems.at[i]) for i, (a, b) in enumerate(copies)]
    small = [
        pltpu.make_async_copy(a, b, small_sems.at[i])
        for i, (a, b) in enumerate([(span_ref, span), (prefix_ref, prefix)])
    ]
    for copy in small + copies:
        copy.start()
    for copy in small:
        copy.wait()
    live = prefix[span[lax.axis_index("section")]]
    limit_out[...] = jnp.full(limit_out.shape, live, jnp.int32)
    for copy in copies:
        copy.wait()


def pair_of(refs, g):
    cols = [slice((2 * g + i) * HD, (2 * g + i + 1) * HD) for i in range(2)]
    return jnp.concatenate([ref[:, c] for c in cols for ref in refs], axis=0)


def cols_of(g, start=0):
    return slice(start + g * HD, start + (g + 1) * HD)


def attention_kernel(partners, n_other, limit_ref, q_ref, *refs):
    n_blocks = 1 + len(partners)
    kv_refs = refs[:n_blocks]
    d_low, d_high, *refs = refs[n_blocks:]
    w_refs = refs[:n_other]
    grad_ref, probs_ref, dscores_ref, *part_refs = refs[n_other:]

    held, both = kv_refs[0].shape
    width = both // 2
    seq = lax.axis_index("seq")
    spots = []
    for r in [0, *partners]:
        first = jnp.bitwise_xor(seq, r) * held if partners else 0
        spots.append(first + lax.broadcasted_iota(jnp.int32, (held, 1), 0))
    alive = jnp.concatenate(spots, axis=0) < limit_ref[0:1, 0:1]

    rows = q_ref.shape[0]
    groups = range(width // HD)
    keys = [jnp.concatenate([ref[:, cols_of(g)] for ref in kv_refs], axis=0) for g in groups]
    scores = [dot(keys[g], pair_of((q_ref,), g), 1, 1) for g in groups]
    dprobs = []
    for g in groups:
        value = jnp.concatenate([ref[:, cols_of(g, width)] for ref in kv_refs], axis=0)
        dprobs.append(dot(value, pair_of((d_low, d_high), g), 1, 1))
    for g in groups:
        masked = jnp.where(alive, scores[g], jnp.float32(-1e30))
        top = jnp.max(masked, axis=0, keepdims=True)
        probs = jnp.exp2((masked - top) * exp2_scale)
        probs = probs * (1.0 / jnp.sum(probs, axis=0, keepdims=True))
        probs_low = probs.astype(jnp.bfloat16)
        delta = jnp.sum(probs_low.astype(jnp.float32) * dprobs[g], axis=0, keepdims=True)
        probs_ref[g] = probs_low
        dscores_ref[g] = (probs * (dprobs[g] - delta)).astype(jnp.bfloat16)
    for g in groups:
        grad_q = (query_scale * dot(keys[g], dscores_ref[g], 0, 0)).astype(jnp.bfloat16)
        for i in range(2):
            spot = (2 * g + i) * HD
            grad_ref[spot : spot + HD, :] = grad_q[:, i * rows : (i + 1) * rows]

    for w_ref, part_ref in zip(w_refs, part_refs):
        block = w_ref[: part_ref.shape[0], :]
        part_ref[...] = dot(block, grad_ref[...], 1, 0).astype(jnp.bfloat16)


def rest_kernel(n_other, grad_ref, *refs):
    for w_ref, part_ref in zip(refs[:n_other], refs[n_other:]):
        block = w_ref[w_ref.shape[0] - part_ref.shape[0] :, :]
        part_ref[...] = dot(block, grad_ref[...], 1, 0).astype(jnp.bfloat16)


def terms_kernel(probs_ref, dscores_ref, q_ref, d_low, d_high, *term_refs):
    held, both = term_refs[0].shape
    width = both // 2
    for g in range(width // HD):
        grad_k = (query_scale * dot(dscores_ref[g], pair_of((q_ref,), g), 1, 0)).astype(jnp.bfloat16)
        grad_v = dot(probs_ref[g], pair_of((d_low, d_high), g), 1, 0).astype(jnp.bfloat16)
        for r, ref in enumerate(term_refs):
            block = slice(r * held, (r + 1) * held)
            ref[:, g * HD : (g + 1) * HD] = grad_k[block]
            ref[:, width + g * HD : width + (g + 1) * HD] = grad_v[block]


def own_kernel(n_head, grad_ref, w_ref, out_ref, w_held, sem):
    feats = out_ref.shape[0]
    start = pl.multiple_of(lax.axis_index("head") * feats, 16)
    copy = pltpu.make_async_copy(w_ref.at[0, pl.ds(start, feats), :], w_held, sem)
    copy.start()
    copy.wait()
    out_ref[...] = dot(w_held[...], grad_ref[...], 1, 0)


def input_sum_kernel(n_other, start, own_ref, *refs):
    arrived = refs[:n_other]
    *_, out_ref, held, sem = refs
    at = slice(start, start + held.shape[0])
    total = own_ref[at, :]
    for ref in arrived:
        total = total + ref[...].astype(jnp.float32)
    held[...] = total.astype(jnp.bfloat16)
    copy = pltpu.make_async_copy(held, out_ref.at[0, at, :], sem)
    copy.start()
    copy.wait()


def term_sum_kernel(*refs):
    *terms, key_ref, value_ref = refs
    total = terms[0][...].astype(jnp.float32)
    for ref in terms[1:]:
        total = total + ref[...].astype(jnp.float32)
    low = total.astype(jnp.bfloat16)
    half = low.shape[1] // 2
    key_ref[0] = low[:, :half]
    value_ref[0] = low[:, half:]


VMEM = pl.BlockSpec(memory_space=pltpu.VMEM)
HBM = pl.BlockSpec(memory_space=pltpu.HBM)


def kernel_call(body, name, out_shape, in_specs, scratch=(), limit=VMEM_LIMIT):
    return pl.pallas_call(
        body,
        out_shape=out_shape,
        in_specs=in_specs,
        out_specs=jax.tree.map(lambda _: VMEM, out_shape),
        scratch_shapes=list(scratch),
        compiler_params=pltpu.CompilerParams(vmem_limit_bytes=limit),
        name=name,
    )


def on_device(queries, grad_out, keys, values, proj_query, section_span, span_prefix):
    n_seq, n_head = lax.axis_size("seq"), lax.axis_size("head")
    n_other = n_head - 1
    direct = n_seq <= MOST_PARTNERS and n_seq & (n_seq - 1) == 0
    low = jnp.bfloat16
    _, held, kv_width = keys.shape
    _, rows, width = queries.shape
    feats = proj_query.shape[1] // n_head

    def shape(*dims, dtype=low):
        return jax.ShapeDtypeStruct(dims, dtype)

    first = feats // 16 * 9 // 16 * 16
    partners = sorted(range(1, n_seq), key=lambda r: (r.bit_count(), -r)) if direct else []
    n_copies = 1 + len(partners)
    *joined, grad_low, grad_high = kernel_call(
        functools.partial(join_kernel, n_copies),
        "join",
        [shape(held, 2 * kv_width)] * n_copies + [shape(rows // 2, width)] * 2,
        [HBM] * 3,
        [pltpu.SemaphoreType.DMA((4,))],
    )(*[in_hbm(x) for x in (keys, values, grad_out)])
    if direct:
        blocks = joined[-1:] + [swapped(x, "seq", r) for x, r in zip(joined, partners)]
    else:
        blocks = [lax.all_gather(joined[0], "seq", axis=0, tiled=True)]
    n_blocks, block_rows = len(blocks), blocks[0].shape[0]
    incoming = [shifted(part, "section", -1) for part in (grad_low, grad_high)]

    limit, q, *w_other = kernel_call(
        functools.partial(stage_kernel, n_head),
        "stage",
        [shape(8, HD, dtype=jnp.int32), shape(rows, width)] + [shape(feats, width)] * n_other,
        [HBM] * 4,
        [
            pltpu.SMEM(section_span.shape, jnp.int32),
            pltpu.SMEM(span_prefix.shape, jnp.int32),
            pltpu.SemaphoreType.DMA((1 + n_other,)),
            pltpu.SemaphoreType.DMA((2,)),
        ],
    )(*[in_hbm(x) for x in (section_span, span_prefix, queries, proj_query)])

    prefix = n_blocks * block_rows
    weights = shape(kv_width // HD, prefix, 2 * rows)
    grad_query, probs, dscores, *products = kernel_call(
        functools.partial(attention_kernel, partners, n_other),
        "attention",
        [shape(width, rows), weights, weights] + [shape(first, rows)] * n_other,
        [VMEM] * (4 + n_blocks + n_other),
    )(limit, q, *blocks, *incoming, *w_other)
    rest = kernel_call(
        functools.partial(rest_kernel, n_other),
        "rest",
        [shape(feats - first, rows)] * n_other,
        [VMEM] * (1 + n_other),
    )(grad_query, *w_other)
    arrived = [shifted(p, "head", r + 1) for part in (products, rest) for r, p in enumerate(part)]
    terms = kernel_call(
        terms_kernel, "terms", [shape(block_rows, 2 * kv_width)] * n_blocks, [VMEM] * 5
    )(probs, dscores, q, *incoming)
    if direct:
        sent = dict(zip(partners, terms[1:]))
        came = {}
        for r, after in ((2, 0), (1, 0), (3, 1)):
            if r in sent:
                block = sent[r]
                if after in came:
                    block, came[after] = lax.optimization_barrier((block, came[after]))
                came[r] = swapped(block, "seq", r)
        all_terms = [terms[0], *came.values()]
    else:
        all_terms = [lax.psum_scatter(terms[0], "seq", scatter_dimension=0, tiled=True)]

    own = kernel_call(
        functools.partial(own_kernel, n_head),
        "own",
        shape(feats, rows, dtype=jnp.float32),
        [VMEM, HBM],
        [pltpu.VMEM((feats, width), low), pltpu.SemaphoreType.DMA(())],
    )(grad_query, in_hbm(proj_query))
    grad_key, grad_value = kernel_call(
        term_sum_kernel, "term_sum", [shape(1, held, kv_width)] * 2, [VMEM] * len(all_terms)
    )(*all_terms)
    grad_input = []
    for start, part in ((0, arrived[:n_other]), (first, arrived[n_other:])):
        grad_input = [
            pl.pallas_call(
                functools.partial(input_sum_kernel, n_other, start),
                out_shape=shape(1, feats, rows),
                in_specs=[VMEM] * (1 + n_other) + [HBM] * len(grad_input),
                out_specs=HBM,
                scratch_shapes=[pltpu.VMEM(part[0].shape, low), pltpu.SemaphoreType.DMA(())],
                input_output_aliases={1 + n_other: 0} if grad_input else {},
                compiler_params=pltpu.CompilerParams(vmem_limit_bytes=VMEM_LIMIT),
                name="input_sum",
            )(own, *part, *grad_input)
        ]
    grad_input = grad_input[0]
    return (grad_input, grad_key, grad_value)


def solution(mesh):
    in_specs = (
        P("section", "seq", "head"),
        P("section", "seq", "head"),
        P("section", "seq", "head"),
        P("section", "seq", "head"),
        P("section", None, "head"),
        P(),
        P(),
    )
    out_specs = (
        P("section", "head", "seq"),
        P("section", "seq", "head"),
        P("section", "seq", "head"),
    )
    return jax.shard_map(
        on_device, mesh=mesh, in_specs=in_specs, out_specs=out_specs, check_vma=False
    )
```

```python
import functools
import math

import jax
import jax.numpy as jnp
from jax import lax
from jax.experimental import pallas as pl
from jax.experimental.pallas import tpu as pltpu
from jax.sharding import PartitionSpec as P

HD = 128
MOST_PARTNERS = 4
VMEM_LIMIT = 40 * 1024 * 1024

query_scale = 168.0 ** (-0.5)
exp2_scale = query_scale * math.log2(math.e)


def shifted(block, axis, distance):
    devices = range(lax.axis_size(axis))
    route = [((i - distance) % len(devices), i) for i in devices]
    return lax.ppermute(block, axis, route)


def swapped(block, axis, distance):
    return lax.ppermute(block, axis, [(i, i ^ distance) for i in range(lax.axis_size(axis))])


def dot(left, right, left_dim, right_dim):
    return lax.dot_general(
        left, right, (((left_dim,), (right_dim,)), ((), ())), preferred_element_type=jnp.float32
    )


def in_hbm(x):
    return pltpu.with_memory_space_constraint(x, pltpu.HBM)


def join_kernel(n_copies, key_ref, value_ref, grad_ref, *refs):
    *outs, grad_low, grad_high, sems = refs
    width, rows = key_ref.shape[2], grad_low.shape[0]
    pairs = [
        (key_ref.at[0], outs[0].at[:, :width]),
        (value_ref.at[0], outs[0].at[:, width:]),
        (grad_ref.at[0, :rows, :], grad_low),
        (grad_ref.at[0, rows:, :], grad_high),
    ]
    copies = [pltpu.make_async_copy(a, b, sems.at[i]) for i, (a, b) in enumerate(pairs)]
    for copy in copies:
        copy.start()
    for copy in copies[:2]:
        copy.wait()
    for out in outs[1:]:
        out[...] = outs[0][...]
    for copy in copies[2:]:
        copy.wait()


def stage_kernel(n_head, span_ref, prefix_ref, q_ref, w_ref, limit_out, q_out, *refs):
    *other_outs, span, prefix, sems, small_sems = refs
    feats = w_ref.shape[1] // n_head
    head = lax.axis_index("head")
    copies = []
    for r, out in enumerate(other_outs):
        start = pl.multiple_of(lax.rem(head + r + 1, n_head) * feats, 16)
        copies.append((w_ref.at[0, pl.ds(start, feats), :], out))
    copies.append((q_ref.at[0], q_out))
    copies = [pltpu.make_async_copy(a, b, sems.at[i]) for i, (a, b) in enumerate(copies)]
    small = [
        pltpu.make_async_copy(a, b, small_sems.at[i])
        for i, (a, b) in enumerate([(span_ref, span), (prefix_ref, prefix)])
    ]
    for copy in small + copies:
        copy.start()
    for copy in small:
        copy.wait()
    live = prefix[span[lax.axis_index("section")]]
    limit_out[...] = jnp.full(limit_out.shape, live, jnp.int32)
    for copy in copies:
        copy.wait()


def pair_of(refs, g):
    cols = [slice((2 * g + i) * HD, (2 * g + i + 1) * HD) for i in range(2)]
    return jnp.concatenate([ref[:, c] for c in cols for ref in refs], axis=0)


def cols_of(g, start=0):
    return slice(start + g * HD, start + (g + 1) * HD)


def attention_kernel(partners, n_other, limit_ref, q_ref, *refs):
    n_blocks = 1 + len(partners)
    kv_refs = refs[:n_blocks]
    d_low, d_high, *refs = refs[n_blocks:]
    w_refs = refs[:n_other]
    grad_ref, probs_ref, dscores_ref, *part_refs = refs[n_other:]

    held, both = kv_refs[0].shape
    width = both // 2
    seq = lax.axis_index("seq")
    spots = []
    for r in [0, *partners]:
        first = jnp.bitwise_xor(seq, r) * held if partners else 0
        spots.append(first + lax.broadcasted_iota(jnp.int32, (held, 1), 0))
    alive = jnp.concatenate(spots, axis=0) < limit_ref[0:1, 0:1]

    rows = q_ref.shape[0]
    groups = range(width // HD)
    keys = [jnp.concatenate([ref[:, cols_of(g)] for ref in kv_refs], axis=0) for g in groups]
    scores = [dot(keys[g], pair_of((q_ref,), g), 1, 1) for g in groups]
    dprobs = []
    for g in groups:
        value = jnp.concatenate([ref[:, cols_of(g, width)] for ref in kv_refs], axis=0)
        dprobs.append(dot(value, pair_of((d_low, d_high), g), 1, 1))
    for g in groups:
        masked = jnp.where(alive, scores[g], jnp.float32(-1e30))
        top = jnp.max(masked, axis=0, keepdims=True)
        probs = jnp.exp2((masked - top) * exp2_scale)
        probs = probs * (1.0 / jnp.sum(probs, axis=0, keepdims=True))
        probs_low = probs.astype(jnp.bfloat16)
        delta = jnp.sum(probs_low.astype(jnp.float32) * dprobs[g], axis=0, keepdims=True)
        probs_ref[g] = probs_low
        dscores_ref[g] = (probs * (dprobs[g] - delta)).astype(jnp.bfloat16)
    for g in groups:
        grad_q = (query_scale * dot(keys[g], dscores_ref[g], 0, 0)).astype(jnp.bfloat16)
        for i in range(2):
            spot = (2 * g + i) * HD
            grad_ref[spot : spot + HD, :] = grad_q[:, i * rows : (i + 1) * rows]

    for w_ref, part_ref in zip(w_refs, part_refs):
        block = w_ref[: part_ref.shape[0], :]
        part_ref[...] = dot(block, grad_ref[...], 1, 0).astype(jnp.bfloat16)


def rest_kernel(n_other, grad_ref, *refs):
    for w_ref, part_ref in zip(refs[:n_other], refs[n_other:]):
        block = w_ref[w_ref.shape[0] - part_ref.shape[0] :, :]
        part_ref[...] = dot(block, grad_ref[...], 1, 0).astype(jnp.bfloat16)


def terms_kernel(probs_ref, dscores_ref, q_ref, d_low, d_high, *term_refs):
    held, both = term_refs[0].shape
    width = both // 2
    for g in range(width // HD):
        grad_k = (query_scale * dot(dscores_ref[g], pair_of((q_ref,), g), 1, 0)).astype(jnp.bfloat16)
        grad_v = dot(probs_ref[g], pair_of((d_low, d_high), g), 1, 0).astype(jnp.bfloat16)
        for r, ref in enumerate(term_refs):
            block = slice(r * held, (r + 1) * held)
            ref[:, g * HD : (g + 1) * HD] = grad_k[block]
            ref[:, width + g * HD : width + (g + 1) * HD] = grad_v[block]


def own_kernel(n_head, grad_ref, w_ref, out_ref, w_held, sem):
    feats = out_ref.shape[0]
    start = pl.multiple_of(lax.axis_index("head") * feats, 16)
    copy = pltpu.make_async_copy(w_ref.at[0, pl.ds(start, feats), :], w_held, sem)
    copy.start()
    copy.wait()
    out_ref[...] = dot(w_held[...], grad_ref[...], 1, 0)


def input_sum_kernel(n_other, start, own_ref, *refs):
    arrived = refs[:n_other]
    *_, out_ref, held, sem = refs
    at = slice(start, start + held.shape[0])
    total = own_ref[at, :]
    for ref in arrived:
        total = total + ref[...].astype(jnp.float32)
    held[...] = total.astype(jnp.bfloat16)
    copy = pltpu.make_async_copy(held, out_ref.at[0, at, :], sem)
    copy.start()
    copy.wait()


def term_sum_kernel(*refs):
    *terms, key_ref, value_ref = refs
    total = terms[0][...].astype(jnp.float32)
    for ref in terms[1:]:
        total = total + ref[...].astype(jnp.float32)
    low = total.astype(jnp.bfloat16)
    half = low.shape[1] // 2
    key_ref[0] = low[:, :half]
    value_ref[0] = low[:, half:]


VMEM = pl.BlockSpec(memory_space=pltpu.VMEM)
HBM = pl.BlockSpec(memory_space=pltpu.HBM)


def kernel_call(body, name, out_shape, in_specs, scratch=(), limit=VMEM_LIMIT):
    return pl.pallas_call(
        body,
        out_shape=out_shape,
        in_specs=in_specs,
        out_specs=jax.tree.map(lambda _: VMEM, out_shape),
        scratch_shapes=list(scratch),
        compiler_params=pltpu.CompilerParams(vmem_limit_bytes=limit),
        name=name,
    )


def on_device(queries, grad_out, keys, values, proj_query, section_span, span_prefix):
    n_seq, n_head = lax.axis_size("seq"), lax.axis_size("head")
    n_other = n_head - 1
    direct = n_seq <= MOST_PARTNERS and n_seq & (n_seq - 1) == 0
    low = jnp.bfloat16
    _, held, kv_width = keys.shape
    _, rows, width = queries.shape
    feats = proj_query.shape[1] // n_head

    def shape(*dims, dtype=low):
        return jax.ShapeDtypeStruct(dims, dtype)

    first = feats // 16 * 9 // 16 * 16
    partners = sorted(range(1, n_seq), key=lambda r: -(r % 2)) if direct else []
    n_copies = 1 + len(partners)
    *joined, grad_low, grad_high = kernel_call(
        functools.partial(join_kernel, n_copies),
        "join",
        [shape(held, 2 * kv_width)] * n_copies + [shape(rows // 2, width)] * 2,
        [HBM] * 3,
        [pltpu.SemaphoreType.DMA((4,))],
    )(*[in_hbm(x) for x in (keys, values, grad_out)])
    if direct:
        blocks = joined[-1:] + [swapped(x, "seq", r) for x, r in zip(joined, partners)]
    else:
        blocks = [lax.all_gather(joined[0], "seq", axis=0, tiled=True)]
    n_blocks, block_rows = len(blocks), blocks[0].shape[0]
    incoming = [shifted(part, "section", -1) for part in (grad_low, grad_high)]

    limit, q, *w_other = kernel_call(
        functools.partial(stage_kernel, n_head),
        "stage",
        [shape(8, HD, dtype=jnp.int32), shape(rows, width)] + [shape(feats, width)] * n_other,
        [HBM] * 4,
        [
            pltpu.SMEM(section_span.shape, jnp.int32),
            pltpu.SMEM(span_prefix.shape, jnp.int32),
            pltpu.SemaphoreType.DMA((1 + n_other,)),
            pltpu.SemaphoreType.DMA((2,)),
        ],
    )(*[in_hbm(x) for x in (section_span, span_prefix, queries, proj_query)])

    prefix = n_blocks * block_rows
    weights = shape(kv_width // HD, prefix, 2 * rows)
    grad_query, probs, dscores, *products = kernel_call(
        functools.partial(attention_kernel, partners, n_other),
        "attention",
        [shape(width, rows), weights, weights] + [shape(first, rows)] * n_other,
        [VMEM] * (4 + n_blocks + n_other),
    )(limit, q, *blocks, *incoming, *w_other)
    rest = kernel_call(
        functools.partial(rest_kernel, n_other),
        "rest",
        [shape(feats - first, rows)] * n_other,
        [VMEM] * (1 + n_other),
    )(grad_query, *w_other)
    arrived = [shifted(p, "head", r + 1) for part in (products, rest) for r, p in enumerate(part)]
    terms = kernel_call(
        terms_kernel, "terms", [shape(block_rows, 2 * kv_width)] * n_blocks, [VMEM] * 5
    )(probs, dscores, q, *incoming)
    if direct:
        sent = sorted(zip(partners, terms[1:]), key=lambda pair: pair[0])
        all_terms = [terms[0]] + [swapped(x, "seq", r) for r, x in sent]
    else:
        all_terms = [lax.psum_scatter(terms[0], "seq", scatter_dimension=0, tiled=True)]

    own = kernel_call(
        functools.partial(own_kernel, n_head),
        "own",
        shape(feats, rows, dtype=jnp.float32),
        [VMEM, HBM],
        [pltpu.VMEM((feats, width), low), pltpu.SemaphoreType.DMA(())],
    )(grad_query, in_hbm(proj_query))
    grad_key, grad_value = kernel_call(
        term_sum_kernel, "term_sum", [shape(1, held, kv_width)] * 2, [VMEM] * len(all_terms)
    )(*all_terms)
    grad_input = []
    for start, part in ((0, arrived[:n_other]), (first, arrived[n_other:])):
        grad_input = [
            pl.pallas_call(
                functools.partial(input_sum_kernel, n_other, start),
                out_shape=shape(1, feats, rows),
                in_specs=[VMEM] * (1 + n_other) + [HBM] * len(grad_input),
                out_specs=HBM,
                scratch_shapes=[pltpu.VMEM(part[0].shape, low), pltpu.SemaphoreType.DMA(())],
                input_output_aliases={1 + n_other: 0} if grad_input else {},
                compiler_params=pltpu.CompilerParams(vmem_limit_bytes=VMEM_LIMIT),
                name="input_sum",
            )(own, *part, *grad_input)
        ]
    grad_input = grad_input[0]
    return (grad_input, grad_key, grad_value)


def solution(mesh):
    in_specs = (
        P("section", "seq", "head"),
        P("section", "seq", "head"),
        P("section", "seq", "head"),
        P("section", "seq", "head"),
        P("section", None, "head"),
        P(),
        P(),
    )
    out_specs = (
        P("section", "head", "seq"),
        P("section", "seq", "head"),
        P("section", "seq", "head"),
    )
    return jax.shard_map(
        on_device, mesh=mesh, in_specs=in_specs, out_specs=out_specs, check_vma=False
    )
```

```python
import functools
import math

import jax
import jax.numpy as jnp
from jax import lax
from jax.experimental import pallas as pl
from jax.experimental.pallas import tpu as pltpu
from jax.sharding import PartitionSpec as P

HD = 128
MOST_PARTNERS = 4
VMEM_LIMIT = 40 * 1024 * 1024

query_scale = 168.0 ** (-0.5)
exp2_scale = query_scale * math.log2(math.e)


def shifted(block, axis, distance):
    devices = range(lax.axis_size(axis))
    route = [((i - distance) % len(devices), i) for i in devices]
    return lax.ppermute(block, axis, route)


def swapped(block, axis, distance):
    return lax.ppermute(block, axis, [(i, i ^ distance) for i in range(lax.axis_size(axis))])


def dot(left, right, left_dim, right_dim):
    return lax.dot_general(
        left, right, (((left_dim,), (right_dim,)), ((), ())), preferred_element_type=jnp.float32
    )


def in_hbm(x):
    return pltpu.with_memory_space_constraint(x, pltpu.HBM)


def join_kernel(n_copies, key_ref, value_ref, grad_ref, *refs):
    *outs, grad_low, grad_high, sems = refs
    width, rows = key_ref.shape[2], grad_low.shape[0]
    pairs = [
        (key_ref.at[0], outs[0].at[:, :width]),
        (value_ref.at[0], outs[0].at[:, width:]),
        (grad_ref.at[0, :rows, :], grad_low),
        (grad_ref.at[0, rows:, :], grad_high),
    ]
    copies = [pltpu.make_async_copy(a, b, sems.at[i]) for i, (a, b) in enumerate(pairs)]
    for copy in copies:
        copy.start()
    for copy in copies[:2]:
        copy.wait()
    for out in outs[1:]:
        out[...] = outs[0][...]
    for copy in copies[2:]:
        copy.wait()


def stage_kernel(n_head, span_ref, prefix_ref, q_ref, w_ref, limit_out, q_out, *refs):
    *other_outs, span, prefix, sems, small_sems = refs
    feats = w_ref.shape[1] // n_head
    head = lax.axis_index("head")
    copies = []
    for r, out in enumerate(other_outs):
        start = pl.multiple_of(lax.rem(head + r + 1, n_head) * feats, 16)
        copies.append((w_ref.at[0, pl.ds(start, feats), :], out))
    copies.append((q_ref.at[0], q_out))
    copies = [pltpu.make_async_copy(a, b, sems.at[i]) for i, (a, b) in enumerate(copies)]
    small = [
        pltpu.make_async_copy(a, b, small_sems.at[i])
        for i, (a, b) in enumerate([(span_ref, span), (prefix_ref, prefix)])
    ]
    for copy in small + copies:
        copy.start()
    for copy in small:
        copy.wait()
    live = prefix[span[lax.axis_index("section")]]
    limit_out[...] = jnp.full(limit_out.shape, live, jnp.int32)
    for copy in copies:
        copy.wait()


def pair_of(refs, g):
    cols = [slice((2 * g + i) * HD, (2 * g + i + 1) * HD) for i in range(2)]
    return jnp.concatenate([ref[:, c] for c in cols for ref in refs], axis=0)


def cols_of(g, start=0):
    return slice(start + g * HD, start + (g + 1) * HD)


def attention_kernel(partners, counts, n_other, limit_ref, q_ref, *refs):
    key_refs, value_refs = [], []
    for count in counts:
        if count == 2:
            key_refs.append(lambda g, ref=refs[0]: ref[0, :, cols_of(g)])
            value_refs.append(lambda g, ref=refs[1]: ref[0, :, cols_of(g)])
        else:
            width = refs[0].shape[1] // 2
            key_refs.append(lambda g, ref=refs[0]: ref[:, cols_of(g)])
            value_refs.append(lambda g, ref=refs[0]: ref[:, cols_of(g, width)])
        refs = refs[count:]
    d_low, d_high, *refs = refs
    w_refs = refs[:n_other]
    grad_ref, probs_ref, dscores_ref, *part_refs = refs[n_other:]

    held = probs_ref.shape[1] // len(counts)
    seq = lax.axis_index("seq")
    spots = []
    for r in [0, *partners]:
        first = jnp.bitwise_xor(seq, r) * held if partners else 0
        spots.append(first + lax.broadcasted_iota(jnp.int32, (held, 1), 0))
    alive = jnp.concatenate(spots, axis=0) < limit_ref[0:1, 0:1]

    rows = q_ref.shape[0]
    groups = range(probs_ref.shape[0])
    keys = [jnp.concatenate([read(g) for read in key_refs], axis=0) for g in groups]
    scores = [dot(keys[g], pair_of((q_ref,), g), 1, 1) for g in groups]
    dprobs = []
    for g in groups:
        value = jnp.concatenate([read(g) for read in value_refs], axis=0)
        dprobs.append(dot(value, pair_of((d_low, d_high), g), 1, 1))
    for g in groups:
        masked = jnp.where(alive, scores[g], jnp.float32(-1e30))
        top = jnp.max(masked, axis=0, keepdims=True)
        probs = jnp.exp2((masked - top) * exp2_scale)
        probs = probs * (1.0 / jnp.sum(probs, axis=0, keepdims=True))
        probs_low = probs.astype(jnp.bfloat16)
        delta = jnp.sum(probs_low.astype(jnp.float32) * dprobs[g], axis=0, keepdims=True)
        probs_ref[g] = probs_low
        dscores_ref[g] = (probs * (dprobs[g] - delta)).astype(jnp.bfloat16)
    for g in groups:
        grad_q = (query_scale * dot(keys[g], dscores_ref[g], 0, 0)).astype(jnp.bfloat16)
        for i in range(2):
            spot = (2 * g + i) * HD
            grad_ref[spot : spot + HD, :] = grad_q[:, i * rows : (i + 1) * rows]

    for w_ref, part_ref in zip(w_refs, part_refs):
        block = w_ref[: part_ref.shape[0], :]
        part_ref[...] = dot(block, grad_ref[...], 1, 0).astype(jnp.bfloat16)


def rest_kernel(n_other, grad_ref, *refs):
    for w_ref, part_ref in zip(refs[:n_other], refs[n_other:]):
        block = w_ref[w_ref.shape[0] - part_ref.shape[0] :, :]
        part_ref[...] = dot(block, grad_ref[...], 1, 0).astype(jnp.bfloat16)


def terms_kernel(probs_ref, dscores_ref, q_ref, d_low, d_high, *term_refs):
    held, both = term_refs[0].shape
    width = both // 2
    for g in range(width // HD):
        grad_k = (query_scale * dot(dscores_ref[g], pair_of((q_ref,), g), 1, 0)).astype(jnp.bfloat16)
        grad_v = dot(probs_ref[g], pair_of((d_low, d_high), g), 1, 0).astype(jnp.bfloat16)
        for r, ref in enumerate(term_refs):
            block = slice(r * held, (r + 1) * held)
            ref[:, g * HD : (g + 1) * HD] = grad_k[block]
            ref[:, width + g * HD : width + (g + 1) * HD] = grad_v[block]


def own_kernel(n_head, grad_ref, w_ref, out_ref, w_held, sem):
    feats = out_ref.shape[0]
    start = pl.multiple_of(lax.axis_index("head") * feats, 16)
    copy = pltpu.make_async_copy(w_ref.at[0, pl.ds(start, feats), :], w_held, sem)
    copy.start()
    copy.wait()
    out_ref[...] = dot(w_held[...], grad_ref[...], 1, 0)


def input_sum_kernel(n_other, start, own_ref, *refs):
    arrived = refs[:n_other]
    *_, out_ref, held, sem = refs
    at = slice(start, start + held.shape[0])
    total = own_ref[at, :]
    for ref in arrived:
        total = total + ref[...].astype(jnp.float32)
    held[...] = total.astype(jnp.bfloat16)
    copy = pltpu.make_async_copy(held, out_ref.at[0, at, :], sem)
    copy.start()
    copy.wait()


def term_sum_kernel(*refs):
    *terms, key_ref, value_ref = refs
    total = terms[0][...].astype(jnp.float32)
    for ref in terms[1:]:
        total = total + ref[...].astype(jnp.float32)
    low = total.astype(jnp.bfloat16)
    half = low.shape[1] // 2
    key_ref[0] = low[:, :half]
    value_ref[0] = low[:, half:]


VMEM = pl.BlockSpec(memory_space=pltpu.VMEM)
HBM = pl.BlockSpec(memory_space=pltpu.HBM)


def kernel_call(body, name, out_shape, in_specs, scratch=(), limit=VMEM_LIMIT):
    return pl.pallas_call(
        body,
        out_shape=out_shape,
        in_specs=in_specs,
        out_specs=jax.tree.map(lambda _: VMEM, out_shape),
        scratch_shapes=list(scratch),
        compiler_params=pltpu.CompilerParams(vmem_limit_bytes=limit),
        name=name,
    )


def on_device(queries, grad_out, keys, values, proj_query, section_span, span_prefix):
    n_seq, n_head = lax.axis_size("seq"), lax.axis_size("head")
    n_other = n_head - 1
    direct = n_seq <= MOST_PARTNERS and n_seq & (n_seq - 1) == 0
    low = jnp.bfloat16
    _, held, kv_width = keys.shape
    _, rows, width = queries.shape
    feats = proj_query.shape[1] // n_head

    def shape(*dims, dtype=low):
        return jax.ShapeDtypeStruct(dims, dtype)

    first = feats // 16 * 9 // 16 * 16
    partners = sorted(range(1, n_seq), key=lambda r: -r.bit_length()) if direct else []
    plain = {1} & set(partners)
    joint = [r for r in partners if r not in plain]
    n_copies = 1 + len(joint)
    *joined, grad_low, grad_high = kernel_call(
        functools.partial(join_kernel, n_copies),
        "join",
        [shape(held, 2 * kv_width)] * n_copies + [shape(rows // 2, width)] * 2,
        [HBM] * 3,
        [pltpu.SemaphoreType.DMA((4,))],
    )(*[in_hbm(x) for x in (keys, values, grad_out)])
    if direct:
        buffers = dict(zip(joint, joined))
        blocks = [(joined[-1],)] + [
            tuple(swapped(x, "seq", r) for x in ([keys, values] if r in plain else [buffers[r]]))
            for r in partners
        ]
    else:
        blocks = [(lax.all_gather(joined[0], "seq", axis=0, tiled=True),)]
    n_blocks, block_rows = len(blocks), blocks[0][0].shape[0]
    counts = [len(block) for block in blocks]
    blocks = [x for block in blocks for x in block]
    incoming = [shifted(part, "section", -1) for part in (grad_low, grad_high)]

    limit, q, *w_other = kernel_call(
        functools.partial(stage_kernel, n_head),
        "stage",
        [shape(8, HD, dtype=jnp.int32), shape(rows, width)] + [shape(feats, width)] * n_other,
        [HBM] * 4,
        [
            pltpu.SMEM(section_span.shape, jnp.int32),
            pltpu.SMEM(span_prefix.shape, jnp.int32),
            pltpu.SemaphoreType.DMA((1 + n_other,)),
            pltpu.SemaphoreType.DMA((2,)),
        ],
    )(*[in_hbm(x) for x in (section_span, span_prefix, queries, proj_query)])

    prefix = n_blocks * block_rows
    weights = shape(kv_width // HD, prefix, 2 * rows)
    grad_query, probs, dscores, *products = kernel_call(
        functools.partial(attention_kernel, partners, counts, n_other),
        "attention",
        [shape(width, rows), weights, weights] + [shape(first, rows)] * n_other,
        [VMEM] * (4 + len(blocks) + n_other),
    )(limit, q, *blocks, *incoming, *w_other)
    rest = kernel_call(
        functools.partial(rest_kernel, n_other),
        "rest",
        [shape(feats - first, rows)] * n_other,
        [VMEM] * (1 + n_other),
    )(grad_query, *w_other)
    arrived = [shifted(p, "head", r + 1) for part in (products, rest) for r, p in enumerate(part)]
    terms = kernel_call(
        terms_kernel, "terms", [shape(block_rows, 2 * kv_width)] * n_blocks, [VMEM] * 5
    )(probs, dscores, q, *incoming)
    if direct:
        sent = sorted(zip(partners, terms[1:]), key=lambda pair: pair[0])
        all_terms = [terms[0]] + [swapped(x, "seq", r) for r, x in sent]
    else:
        all_terms = [lax.psum_scatter(terms[0], "seq", scatter_dimension=0, tiled=True)]

    own = kernel_call(
        functools.partial(own_kernel, n_head),
        "own",
        shape(feats, rows, dtype=jnp.float32),
        [VMEM, HBM],
        [pltpu.VMEM((feats, width), low), pltpu.SemaphoreType.DMA(())],
    )(grad_query, in_hbm(proj_query))
    grad_key, grad_value = kernel_call(
        term_sum_kernel, "term_sum", [shape(1, held, kv_width)] * 2, [VMEM] * len(all_terms)
    )(*all_terms)
    grad_input = []
    for start, part in ((0, arrived[:n_other]), (first, arrived[n_other:])):
        grad_input = [
            pl.pallas_call(
                functools.partial(input_sum_kernel, n_other, start),
                out_shape=shape(1, feats, rows),
                in_specs=[VMEM] * (1 + n_other) + [HBM] * len(grad_input),
                out_specs=HBM,
                scratch_shapes=[pltpu.VMEM(part[0].shape, low), pltpu.SemaphoreType.DMA(())],
                input_output_aliases={1 + n_other: 0} if grad_input else {},
                compiler_params=pltpu.CompilerParams(vmem_limit_bytes=VMEM_LIMIT),
                name="input_sum",
            )(own, *part, *grad_input)
        ]
    grad_input = grad_input[0]
    return (grad_input, grad_key, grad_value)


def solution(mesh):
    in_specs = (
        P("section", "seq", "head"),
        P("section", "seq", "head"),
        P("section", "seq", "head"),
        P("section", "seq", "head"),
        P("section", None, "head"),
        P(),
        P(),
    )
    out_specs = (
        P("section", "head", "seq"),
        P("section", "seq", "head"),
        P("section", "seq", "head"),
    )
    return jax.shard_map(
        on_device, mesh=mesh, in_specs=in_specs, out_specs=out_specs, check_vma=False
    )
```

```python
import functools
import math

import jax
import jax.numpy as jnp
from jax import lax
from jax.experimental import pallas as pl
from jax.experimental.pallas import tpu as pltpu
from jax.sharding import PartitionSpec as P

HD = 128
MOST_PARTNERS = 4
VMEM_LIMIT = 40 * 1024 * 1024

query_scale = 168.0 ** (-0.5)
exp2_scale = query_scale * math.log2(math.e)


def shifted(block, axis, distance):
    devices = range(lax.axis_size(axis))
    route = [((i - distance) % len(devices), i) for i in devices]
    return lax.ppermute(block, axis, route)


def swapped(block, axis, distance):
    return lax.ppermute(block, axis, [(i, i ^ distance) for i in range(lax.axis_size(axis))])


def dot(left, right, left_dim, right_dim):
    return lax.dot_general(
        left, right, (((left_dim,), (right_dim,)), ((), ())), preferred_element_type=jnp.float32
    )


def in_hbm(x):
    return pltpu.with_memory_space_constraint(x, pltpu.HBM)


def join_kernel(n_copies, key_ref, value_ref, grad_ref, *refs):
    *outs, grad_low, grad_high, sems = refs
    width, rows = key_ref.shape[2], grad_low.shape[0]
    pairs = [
        (key_ref.at[0], outs[0].at[:, :width]),
        (value_ref.at[0], outs[0].at[:, width:]),
        (grad_ref.at[0, :rows, :], grad_low),
        (grad_ref.at[0, rows:, :], grad_high),
    ]
    copies = [pltpu.make_async_copy(a, b, sems.at[i]) for i, (a, b) in enumerate(pairs)]
    for copy in copies:
        copy.start()
    for copy in copies[:2]:
        copy.wait()
    for out in outs[1:]:
        out[...] = outs[0][...]
    for copy in copies[2:]:
        copy.wait()


def stage_kernel(n_head, span_ref, prefix_ref, q_ref, w_ref, limit_out, q_out, *refs):
    *other_outs, span, prefix, sems, small_sems = refs
    feats = w_ref.shape[1] // n_head
    head = lax.axis_index("head")
    copies = []
    for r, out in enumerate(other_outs):
        start = pl.multiple_of(lax.rem(head + r + 1, n_head) * feats, 16)
        copies.append((w_ref.at[0, pl.ds(start, feats), :], out))
    copies.append((q_ref.at[0], q_out))
    copies = [pltpu.make_async_copy(a, b, sems.at[i]) for i, (a, b) in enumerate(copies)]
    small = [
        pltpu.make_async_copy(a, b, small_sems.at[i])
        for i, (a, b) in enumerate([(span_ref, span), (prefix_ref, prefix)])
    ]
    for copy in small + copies:
        copy.start()
    for copy in small:
        copy.wait()
    live = prefix[span[lax.axis_index("section")]]
    limit_out[...] = jnp.full(limit_out.shape, live, jnp.int32)
    for copy in copies:
        copy.wait()


def pair_of(refs, g):
    cols = [slice((2 * g + i) * HD, (2 * g + i + 1) * HD) for i in range(2)]
    return jnp.concatenate([ref[:, c] for c in cols for ref in refs], axis=0)


def cols_of(g, start=0):
    return slice(start + g * HD, start + (g + 1) * HD)


def attention_kernel(partners, counts, n_other, limit_ref, q_ref, *refs):
    key_refs, value_refs = [], []
    for count in counts:
        if count == 2:
            key_refs.append(lambda g, ref=refs[0]: ref[0, :, cols_of(g)])
            value_refs.append(lambda g, ref=refs[1]: ref[0, :, cols_of(g)])
        else:
            width = refs[0].shape[1] // 2
            key_refs.append(lambda g, ref=refs[0]: ref[:, cols_of(g)])
            value_refs.append(lambda g, ref=refs[0]: ref[:, cols_of(g, width)])
        refs = refs[count:]
    d_low, d_high, *refs = refs
    w_refs = refs[:n_other]
    grad_ref, probs_ref, dscores_ref, *part_refs = refs[n_other:]

    held = probs_ref.shape[1] // len(counts)
    seq = lax.axis_index("seq")
    spots = []
    for r in [0, *partners]:
        first = jnp.bitwise_xor(seq, r) * held if partners else 0
        spots.append(first + lax.broadcasted_iota(jnp.int32, (held, 1), 0))
    alive = jnp.concatenate(spots, axis=0) < limit_ref[0:1, 0:1]

    rows = q_ref.shape[0]
    groups = range(probs_ref.shape[0])
    keys = [jnp.concatenate([read(g) for read in key_refs], axis=0) for g in groups]
    scores = [dot(keys[g], pair_of((q_ref,), g), 1, 1) for g in groups]
    dprobs = []
    for g in groups:
        value = jnp.concatenate([read(g) for read in value_refs], axis=0)
        dprobs.append(dot(value, pair_of((d_low, d_high), g), 1, 1))
    for g in groups:
        masked = jnp.where(alive, scores[g], jnp.float32(-1e30))
        top = jnp.max(masked, axis=0, keepdims=True)
        probs = jnp.exp2((masked - top) * exp2_scale)
        probs = probs * (1.0 / jnp.sum(probs, axis=0, keepdims=True))
        probs_low = probs.astype(jnp.bfloat16)
        delta = jnp.sum(probs_low.astype(jnp.float32) * dprobs[g], axis=0, keepdims=True)
        probs_ref[g] = probs_low
        dscores_ref[g] = (probs * (dprobs[g] - delta)).astype(jnp.bfloat16)
    for g in groups:
        grad_q = (query_scale * dot(keys[g], dscores_ref[g], 0, 0)).astype(jnp.bfloat16)
        for i in range(2):
            spot = (2 * g + i) * HD
            grad_ref[spot : spot + HD, :] = grad_q[:, i * rows : (i + 1) * rows]

    for w_ref, part_ref in zip(w_refs, part_refs):
        block = w_ref[: part_ref.shape[0], :]
        part_ref[...] = dot(block, grad_ref[...], 1, 0).astype(jnp.bfloat16)


def rest_kernel(n_other, grad_ref, *refs):
    for w_ref, part_ref in zip(refs[:n_other], refs[n_other:]):
        block = w_ref[w_ref.shape[0] - part_ref.shape[0] :, :]
        part_ref[...] = dot(block, grad_ref[...], 1, 0).astype(jnp.bfloat16)


def terms_kernel(probs_ref, dscores_ref, q_ref, d_low, d_high, *term_refs):
    held, both = term_refs[0].shape
    width = both // 2
    for g in range(width // HD):
        grad_k = (query_scale * dot(dscores_ref[g], pair_of((q_ref,), g), 1, 0)).astype(jnp.bfloat16)
        grad_v = dot(probs_ref[g], pair_of((d_low, d_high), g), 1, 0).astype(jnp.bfloat16)
        for r, ref in enumerate(term_refs):
            block = slice(r * held, (r + 1) * held)
            ref[:, g * HD : (g + 1) * HD] = grad_k[block]
            ref[:, width + g * HD : width + (g + 1) * HD] = grad_v[block]


def own_kernel(n_head, grad_ref, w_ref, out_ref, w_held, sem):
    feats = out_ref.shape[0]
    start = pl.multiple_of(lax.axis_index("head") * feats, 16)
    copy = pltpu.make_async_copy(w_ref.at[0, pl.ds(start, feats), :], w_held, sem)
    copy.start()
    copy.wait()
    out_ref[...] = dot(w_held[...], grad_ref[...], 1, 0)


def input_sum_kernel(n_other, start, own_ref, *refs):
    arrived = refs[:n_other]
    *_, out_ref, held, sem = refs
    at = slice(start, start + held.shape[0])
    total = own_ref[at, :]
    for ref in arrived:
        total = total + ref[...].astype(jnp.float32)
    held[...] = total.astype(jnp.bfloat16)
    copy = pltpu.make_async_copy(held, out_ref.at[0, at, :], sem)
    copy.start()
    copy.wait()


def term_sum_kernel(*refs):
    *terms, key_ref, value_ref = refs
    total = terms[0][...].astype(jnp.float32)
    for ref in terms[1:]:
        total = total + ref[...].astype(jnp.float32)
    low = total.astype(jnp.bfloat16)
    half = low.shape[1] // 2
    key_ref[0] = low[:, :half]
    value_ref[0] = low[:, half:]


VMEM = pl.BlockSpec(memory_space=pltpu.VMEM)
HBM = pl.BlockSpec(memory_space=pltpu.HBM)


def kernel_call(body, name, out_shape, in_specs, scratch=(), limit=VMEM_LIMIT):
    return pl.pallas_call(
        body,
        out_shape=out_shape,
        in_specs=in_specs,
        out_specs=jax.tree.map(lambda _: VMEM, out_shape),
        scratch_shapes=list(scratch),
        compiler_params=pltpu.CompilerParams(vmem_limit_bytes=limit),
        name=name,
    )


def on_device(queries, grad_out, keys, values, proj_query, section_span, span_prefix):
    n_seq, n_head = lax.axis_size("seq"), lax.axis_size("head")
    n_other = n_head - 1
    direct = n_seq <= MOST_PARTNERS and n_seq & (n_seq - 1) == 0
    low = jnp.bfloat16
    _, held, kv_width = keys.shape
    _, rows, width = queries.shape
    feats = proj_query.shape[1] // n_head

    def shape(*dims, dtype=low):
        return jax.ShapeDtypeStruct(dims, dtype)

    first = feats // 16 * 9 // 16 * 16
    partners = sorted(range(1, n_seq), key=lambda r: -r.bit_length()) if direct else []
    plain = {2} & set(partners)
    joint = [r for r in partners if r not in plain]
    n_copies = 1 + len(joint)
    *joined, grad_low, grad_high = kernel_call(
        functools.partial(join_kernel, n_copies),
        "join",
        [shape(held, 2 * kv_width)] * n_copies + [shape(rows // 2, width)] * 2,
        [HBM] * 3,
        [pltpu.SemaphoreType.DMA((4,))],
    )(*[in_hbm(x) for x in (keys, values, grad_out)])
    if direct:
        far = {r: [swapped(x, "seq", r) for x in (keys, values)] for r in sorted(plain)}
        buffers = dict(zip(joint, joined))
        if far:
            last = joint[:0]
            late = [buffers[r] for r in last]
            came = far[min(far)]
            came[0], came[1], grad_low, grad_high, *late = lax.optimization_barrier(
                (*came, grad_low, grad_high, *late)
            )
            buffers |= dict(zip(last, late))
        blocks = [(joined[-1],)] + [
            tuple(far[r]) if r in far else (swapped(buffers[r], "seq", r),) for r in partners
        ]
    else:
        blocks = [(lax.all_gather(joined[0], "seq", axis=0, tiled=True),)]
    n_blocks, block_rows = len(blocks), blocks[0][0].shape[0]
    counts = [len(block) for block in blocks]
    blocks = [x for block in blocks for x in block]
    incoming = [shifted(part, "section", -1) for part in (grad_low, grad_high)]

    limit, q, *w_other = kernel_call(
        functools.partial(stage_kernel, n_head),
        "stage",
        [shape(8, HD, dtype=jnp.int32), shape(rows, width)] + [shape(feats, width)] * n_other,
        [HBM] * 4,
        [
            pltpu.SMEM(section_span.shape, jnp.int32),
            pltpu.SMEM(span_prefix.shape, jnp.int32),
            pltpu.SemaphoreType.DMA((1 + n_other,)),
            pltpu.SemaphoreType.DMA((2,)),
        ],
    )(*[in_hbm(x) for x in (section_span, span_prefix, queries, proj_query)])

    prefix = n_blocks * block_rows
    weights = shape(kv_width // HD, prefix, 2 * rows)
    grad_query, probs, dscores, *products = kernel_call(
        functools.partial(attention_kernel, partners, counts, n_other),
        "attention",
        [shape(width, rows), weights, weights] + [shape(first, rows)] * n_other,
        [VMEM] * (4 + len(blocks) + n_other),
    )(limit, q, *blocks, *incoming, *w_other)
    rest = kernel_call(
        functools.partial(rest_kernel, n_other),
        "rest",
        [shape(feats - first, rows)] * n_other,
        [VMEM] * (1 + n_other),
    )(grad_query, *w_other)
    arrived = [shifted(p, "head", r + 1) for part in (products, rest) for r, p in enumerate(part)]
    terms = kernel_call(
        terms_kernel, "terms", [shape(block_rows, 2 * kv_width)] * n_blocks, [VMEM] * 5
    )(probs, dscores, q, *incoming)
    if direct:
        sent = sorted(zip(partners, terms[1:]), key=lambda pair: pair[0])
        all_terms = [terms[0]] + [swapped(x, "seq", r) for r, x in sent]
    else:
        all_terms = [lax.psum_scatter(terms[0], "seq", scatter_dimension=0, tiled=True)]

    own = kernel_call(
        functools.partial(own_kernel, n_head),
        "own",
        shape(feats, rows, dtype=jnp.float32),
        [VMEM, HBM],
        [pltpu.VMEM((feats, width), low), pltpu.SemaphoreType.DMA(())],
    )(grad_query, in_hbm(proj_query))
    grad_key, grad_value = kernel_call(
        term_sum_kernel, "term_sum", [shape(1, held, kv_width)] * 2, [VMEM] * len(all_terms)
    )(*all_terms)
    grad_input = []
    for start, part in ((0, arrived[:n_other]), (first, arrived[n_other:])):
        grad_input = [
            pl.pallas_call(
                functools.partial(input_sum_kernel, n_other, start),
                out_shape=shape(1, feats, rows),
                in_specs=[VMEM] * (1 + n_other) + [HBM] * len(grad_input),
                out_specs=HBM,
                scratch_shapes=[pltpu.VMEM(part[0].shape, low), pltpu.SemaphoreType.DMA(())],
                input_output_aliases={1 + n_other: 0} if grad_input else {},
                compiler_params=pltpu.CompilerParams(vmem_limit_bytes=VMEM_LIMIT),
                name="input_sum",
            )(own, *part, *grad_input)
        ]
    grad_input = grad_input[0]
    return (grad_input, grad_key, grad_value)


def solution(mesh):
    in_specs = (
        P("section", "seq", "head"),
        P("section", "seq", "head"),
        P("section", "seq", "head"),
        P("section", "seq", "head"),
        P("section", None, "head"),
        P(),
        P(),
    )
    out_specs = (
        P("section", "head", "seq"),
        P("section", "seq", "head"),
        P("section", "seq", "head"),
    )
    return jax.shard_map(
        on_device, mesh=mesh, in_specs=in_specs, out_specs=out_specs, check_vma=False
    )
```

```python
import functools
import math

import jax
import jax.numpy as jnp
from jax import lax
from jax.experimental import pallas as pl
from jax.experimental.pallas import tpu as pltpu
from jax.sharding import PartitionSpec as P

HD = 128
MOST_PARTNERS = 4
VMEM_LIMIT = 40 * 1024 * 1024

query_scale = 168.0 ** (-0.5)
exp2_scale = query_scale * math.log2(math.e)


def shifted(block, axis, distance):
    devices = range(lax.axis_size(axis))
    route = [((i - distance) % len(devices), i) for i in devices]
    return lax.ppermute(block, axis, route)


def swapped(block, axis, distance):
    return lax.ppermute(block, axis, [(i, i ^ distance) for i in range(lax.axis_size(axis))])


def dot(left, right, left_dim, right_dim):
    return lax.dot_general(
        left, right, (((left_dim,), (right_dim,)), ((), ())), preferred_element_type=jnp.float32
    )


def in_hbm(x):
    return pltpu.with_memory_space_constraint(x, pltpu.HBM)


def fetch_rows(n_head, shifts, w_ref, outs, sems):
    feats = w_ref.shape[1] // n_head
    head = lax.axis_index("head")
    copies = []
    for i, (shift, out) in enumerate(zip(shifts, outs)):
        start = pl.multiple_of(lax.rem(head + shift, n_head) * feats, 16)
        copies.append(
            pltpu.make_async_copy(w_ref.at[0, pl.ds(start, feats), :], out, sems.at[i])
        )
    for copy in copies:
        copy.start()
    for copy in copies:
        copy.wait()


def second_core():
    return lax.rem(lax.axis_index("section"), 2) == 1


def join_kernel(n_copies, n_head, key_ref, value_ref, w_ref, *refs):
    outs, w_outs, (sems, w_sems) = refs[:n_copies], refs[n_copies:-2], refs[-2:]
    width = key_ref.shape[2]
    pairs = [(key_ref.at[0], outs[0].at[:, :width]), (value_ref.at[0], outs[0].at[:, width:])]
    copies = [pltpu.make_async_copy(a, b, sems.at[i]) for i, (a, b) in enumerate(pairs)]
    for copy in copies:
        copy.start()
    for copy in copies:
        copy.wait()
    for out in outs[1:]:
        out[...] = outs[0][...]

    @pl.when(second_core())
    def _():
        fetch_rows(n_head, range(n_head), w_ref, w_outs, w_sems)


def stage_kernel(n_head, span_ref, prefix_ref, q_ref, w_ref, limit_out, q_out, *refs):
    *w_outs, span, prefix, sems, w_sems = refs
    pairs = [(span_ref, span), (prefix_ref, prefix), (q_ref.at[0], q_out)]
    copies = [pltpu.make_async_copy(a, b, sems.at[i]) for i, (a, b) in enumerate(pairs)]
    for copy in copies:
        copy.start()

    @pl.when(jnp.logical_not(second_core()))
    def _():
        fetch_rows(n_head, range(1, n_head), w_ref, w_outs, w_sems)

    for copy in copies:
        copy.wait()
    live = prefix[span[lax.axis_index("section")]]
    limit_out[...] = jnp.full(limit_out.shape, live, jnp.int32)


def products(early, late, grad_ref, part_refs, start):
    for held, taken in ((early, second_core()), (late, jnp.logical_not(second_core()))):

        @pl.when(taken)
        def _():
            for w_ref, part_ref in zip(held, part_refs):
                block = w_ref[start : start + part_ref.shape[0], :]
                part_ref[...] = dot(block, grad_ref[...], 1, 0).astype(jnp.bfloat16)


def pair_of(rows, g):
    cols = [slice((2 * g + i) * HD, (2 * g + i + 1) * HD) for i in range(2)]
    return jnp.concatenate([rows(c) for c in cols], axis=0)


def cols_of(g, start=0):
    return slice(start + g * HD, start + (g + 1) * HD)


def attention_kernel(partners, n_other, limit_ref, q_ref, *refs):
    n_blocks = 1 + len(partners)
    kv_refs = refs[:n_blocks]
    d_ref, *refs = refs[n_blocks:]
    early, late = refs[:n_other], refs[n_other : 2 * n_other]
    grad_ref, probs_ref, dscores_ref, *part_refs = refs[2 * n_other :]

    held, both = kv_refs[0].shape
    width = both // 2
    seq = lax.axis_index("seq")
    spots = []
    for r in [0, *partners]:
        first = jnp.bitwise_xor(seq, r) * held if partners else 0
        spots.append(first + lax.broadcasted_iota(jnp.int32, (held, 1), 0))
    alive = jnp.concatenate(spots, axis=0) < limit_ref[0:1, 0:1]

    rows = q_ref.shape[0]
    groups = range(width // HD)
    keys = [jnp.concatenate([ref[:, cols_of(g)] for ref in kv_refs], axis=0) for g in groups]
    scores = [dot(keys[g], pair_of(lambda c: q_ref[:, c], g), 1, 1) for g in groups]
    dprobs = []
    for g in groups:
        value = jnp.concatenate([ref[:, cols_of(g, width)] for ref in kv_refs], axis=0)
        dprobs.append(dot(value, pair_of(lambda c: d_ref[0, :, c], g), 1, 1))
    for g in groups:
        masked = jnp.where(alive, scores[g], jnp.float32(-1e30))
        top = jnp.max(masked, axis=0, keepdims=True)
        probs = jnp.exp2((masked - top) * exp2_scale)
        probs = probs * (1.0 / jnp.sum(probs, axis=0, keepdims=True))
        probs_low = probs.astype(jnp.bfloat16)
        delta = jnp.sum(probs_low.astype(jnp.float32) * dprobs[g], axis=0, keepdims=True)
        probs_ref[g] = probs_low
        dscores_ref[g] = (probs * (dprobs[g] - delta)).astype(jnp.bfloat16)
    for g in groups:
        grad_q = (query_scale * dot(keys[g], dscores_ref[g], 0, 0)).astype(jnp.bfloat16)
        for i in range(2):
            spot = (2 * g + i) * HD
            grad_ref[spot : spot + HD, :] = grad_q[:, i * rows : (i + 1) * rows]

    products(early, late, grad_ref, part_refs, 0)


def rest_kernel(n_other, start, grad_ref, *refs):
    early, late = refs[:n_other], refs[n_other : 2 * n_other]
    products(early, late, grad_ref, refs[2 * n_other :], start)


def terms_kernel(probs_ref, dscores_ref, q_ref, d_ref, *term_refs):
    held, both = term_refs[0].shape
    width = both // 2
    for g in range(width // HD):
        grad_k = (query_scale * dot(dscores_ref[g], pair_of(lambda c: q_ref[:, c], g), 1, 0)).astype(jnp.bfloat16)
        grad_v = dot(probs_ref[g], pair_of(lambda c: d_ref[0, :, c], g), 1, 0).astype(jnp.bfloat16)
        for r, ref in enumerate(term_refs):
            block = slice(r * held, (r + 1) * held)
            ref[:, g * HD : (g + 1) * HD] = grad_k[block]
            ref[:, width + g * HD : width + (g + 1) * HD] = grad_v[block]


def own_kernel(n_head, grad_ref, early_ref, w_ref, out_ref, w_held, sems):
    @pl.when(second_core())
    def _():
        out_ref[...] = dot(early_ref[...], grad_ref[...], 1, 0)

    @pl.when(jnp.logical_not(second_core()))
    def _():
        fetch_rows(n_head, [0], w_ref, [w_held], sems)
        out_ref[...] = dot(w_held[...], grad_ref[...], 1, 0)


def input_sum_kernel(n_other, start, own_ref, *refs):
    arrived = refs[:n_other]
    *_, out_ref, held, sem = refs
    at = slice(start, start + held.shape[0])
    total = own_ref[at, :]
    for ref in arrived:
        total = total + ref[...].astype(jnp.float32)
    held[...] = total.astype(jnp.bfloat16)
    copy = pltpu.make_async_copy(held, out_ref.at[0, at, :], sem)
    copy.start()
    copy.wait()


def term_sum_kernel(*refs):
    *terms, key_ref, value_ref = refs
    total = terms[0][...].astype(jnp.float32)
    for ref in terms[1:]:
        total = total + ref[...].astype(jnp.float32)
    low = total.astype(jnp.bfloat16)
    half = low.shape[1] // 2
    key_ref[0] = low[:, :half]
    value_ref[0] = low[:, half:]


VMEM = pl.BlockSpec(memory_space=pltpu.VMEM)
HBM = pl.BlockSpec(memory_space=pltpu.HBM)


def kernel_call(body, name, out_shape, in_specs, scratch=(), limit=VMEM_LIMIT):
    return pl.pallas_call(
        body,
        out_shape=out_shape,
        in_specs=in_specs,
        out_specs=jax.tree.map(lambda _: VMEM, out_shape),
        scratch_shapes=list(scratch),
        compiler_params=pltpu.CompilerParams(vmem_limit_bytes=limit),
        name=name,
    )


def on_device(queries, grad_out, keys, values, proj_query, section_span, span_prefix):
    n_seq, n_head = lax.axis_size("seq"), lax.axis_size("head")
    n_other = n_head - 1
    direct = n_seq <= MOST_PARTNERS and n_seq & (n_seq - 1) == 0
    low = jnp.bfloat16
    _, held, kv_width = keys.shape
    _, rows, width = queries.shape
    feats = proj_query.shape[1] // n_head

    def shape(*dims, dtype=low):
        return jax.ShapeDtypeStruct(dims, dtype)

    first = feats // 16 * 9 // 16 * 16
    partners = sorted(range(1, n_seq), key=lambda r: -r.bit_length()) if direct else []
    n_copies = 1 + len(partners)
    incoming = shifted(grad_out, "section", -1)
    weight_rows = in_hbm(proj_query)
    out = kernel_call(
        functools.partial(join_kernel, n_copies, n_head),
        "join",
        [shape(held, 2 * kv_width)] * n_copies + [shape(feats, width)] * n_head,
        [HBM] * 3,
        [pltpu.SemaphoreType.DMA((2,)), pltpu.SemaphoreType.DMA((n_head,))],
    )(in_hbm(keys), in_hbm(values), weight_rows)
    joined, (early_own, *early) = out[:n_copies], out[n_copies:]
    if direct:
        blocks = [joined[-1]] + [swapped(x, "seq", r) for x, r in zip(joined, partners)]
    else:
        blocks = [lax.all_gather(joined[0], "seq", axis=0, tiled=True)]
    n_blocks, block_rows = len(blocks), blocks[0].shape[0]

    limit, q, *late = kernel_call(
        functools.partial(stage_kernel, n_head),
        "stage",
        [shape(8, HD, dtype=jnp.int32), shape(rows, width)] + [shape(feats, width)] * n_other,
        [HBM] * 4,
        [
            pltpu.SMEM(section_span.shape, jnp.int32),
            pltpu.SMEM(span_prefix.shape, jnp.int32),
            pltpu.SemaphoreType.DMA((3,)),
            pltpu.SemaphoreType.DMA((max(n_other, 1),)),
        ],
    )(*[in_hbm(x) for x in (section_span, span_prefix, queries)], weight_rows)

    prefix = n_blocks * block_rows
    weights = shape(kv_width // HD, prefix, 2 * rows)
    grad_query, probs, dscores, *products = kernel_call(
        functools.partial(attention_kernel, partners, n_other),
        "attention",
        [shape(width, rows), weights, weights] + [shape(first, rows)] * n_other,
        [VMEM] * (3 + n_blocks + 2 * n_other),
    )(limit, q, *blocks, incoming, *early, *late)
    rest = kernel_call(
        functools.partial(rest_kernel, n_other, first),
        "rest",
        [shape(feats - first, rows)] * n_other,
        [VMEM] * (1 + 2 * n_other),
    )(grad_query, *early, *late)
    arrived = [shifted(p, "head", r + 1) for part in (products, rest) for r, p in enumerate(part)]
    terms = kernel_call(
        terms_kernel, "terms", [shape(block_rows, 2 * kv_width)] * n_blocks, [VMEM] * 4
    )(probs, dscores, q, incoming)
    if direct:
        sent = sorted(zip(partners, terms[1:]), key=lambda pair: pair[0])
        all_terms = [terms[0]] + [swapped(x, "seq", r) for r, x in sent]
    else:
        all_terms = [lax.psum_scatter(terms[0], "seq", scatter_dimension=0, tiled=True)]

    own = kernel_call(
        functools.partial(own_kernel, n_head),
        "own",
        shape(feats, rows, dtype=jnp.float32),
        [VMEM, VMEM, HBM],
        [pltpu.VMEM((feats, width), low), pltpu.SemaphoreType.DMA((1,))],
    )(grad_query, early_own, weight_rows)
    grad_key, grad_value = kernel_call(
        term_sum_kernel, "term_sum", [shape(1, held, kv_width)] * 2, [VMEM] * len(all_terms)
    )(*all_terms)
    grad_input = []
    for start, part in ((0, arrived[:n_other]), (first, arrived[n_other:])):
        grad_input = [
            pl.pallas_call(
                functools.partial(input_sum_kernel, n_other, start),
                out_shape=shape(1, feats, rows),
                in_specs=[VMEM] * (1 + n_other) + [HBM] * len(grad_input),
                out_specs=HBM,
                scratch_shapes=[pltpu.VMEM(part[0].shape, low), pltpu.SemaphoreType.DMA(())],
                input_output_aliases={1 + n_other: 0} if grad_input else {},
                compiler_params=pltpu.CompilerParams(vmem_limit_bytes=VMEM_LIMIT),
                name="input_sum",
            )(own, *part, *grad_input)
        ]
    grad_input = grad_input[0]
    return (grad_input, grad_key, grad_value)


def solution(mesh):
    in_specs = (
        P("section", "seq", "head"),
        P("section", "seq", "head"),
        P("section", "seq", "head"),
        P("section", "seq", "head"),
        P("section", None, "head"),
        P(),
        P(),
    )
    out_specs = (
        P("section", "head", "seq"),
        P("section", "seq", "head"),
        P("section", "seq", "head"),
    )
    return jax.shard_map(
        on_device, mesh=mesh, in_specs=in_specs, out_specs=out_specs, check_vma=False
    )
```

```python
import functools
import math

import jax
import jax.numpy as jnp
from jax import lax
from jax.experimental import pallas as pl
from jax.experimental.pallas import tpu as pltpu
from jax.sharding import PartitionSpec as P

HD = 128
MOST_PARTNERS = 4
VMEM_LIMIT = 40 * 1024 * 1024

query_scale = 168.0 ** (-0.5)
exp2_scale = query_scale * math.log2(math.e)


def shifted(block, axis, distance):
    devices = range(lax.axis_size(axis))
    route = [((i - distance) % len(devices), i) for i in devices]
    return lax.ppermute(block, axis, route)


def dot(left, right, left_dim, right_dim):
    return lax.dot_general(
        left, right, (((left_dim,), (right_dim,)), ((), ())), preferred_element_type=jnp.float32
    )


def in_hbm(x):
    return pltpu.with_memory_space_constraint(x, pltpu.HBM)


def join_kernel(n_copies, key_ref, value_ref, grad_ref, *refs):
    *outs, grad_low, grad_high, sems = refs
    width, rows = key_ref.shape[2], grad_low.shape[0]
    pairs = [
        (key_ref.at[0], outs[0].at[:, :width]),
        (value_ref.at[0], outs[0].at[:, width:]),
        (grad_ref.at[0, :rows, :], grad_low),
        (grad_ref.at[0, rows:, :], grad_high),
    ]
    copies = [pltpu.make_async_copy(a, b, sems.at[i]) for i, (a, b) in enumerate(pairs)]
    for copy in copies:
        copy.start()
    for copy in copies[:2]:
        copy.wait()
    for out in outs[1:]:
        out[...] = outs[0][...]
    for copy in copies[2:]:
        copy.wait()


def stage_kernel(n_head, span_ref, prefix_ref, q_ref, w_ref, limit_out, q_out, *refs):
    *other_outs, span, prefix, sems, small_sems = refs
    feats = w_ref.shape[1] // n_head
    head = lax.axis_index("head")
    copies = []
    for r, out in enumerate(other_outs):
        start = pl.multiple_of(lax.rem(head + r + 1, n_head) * feats, 16)
        copies.append((w_ref.at[0, pl.ds(start, feats), :], out))
    copies.append((q_ref.at[0], q_out))
    copies = [pltpu.make_async_copy(a, b, sems.at[i]) for i, (a, b) in enumerate(copies)]
    small = [
        pltpu.make_async_copy(a, b, small_sems.at[i])
        for i, (a, b) in enumerate([(span_ref, span), (prefix_ref, prefix)])
    ]
    for copy in small + copies:
        copy.start()
    for copy in small:
        copy.wait()
    live = prefix[span[lax.axis_index("section")]]
    limit_out[...] = jnp.full(limit_out.shape, live, jnp.int32)
    for copy in copies:
        copy.wait()


def pair_of(refs, g):
    cols = [slice((2 * g + i) * HD, (2 * g + i + 1) * HD) for i in range(2)]
    return jnp.concatenate([ref[:, c] for c in cols for ref in refs], axis=0)


def cols_of(g, start=0):
    return slice(start + g * HD, start + (g + 1) * HD)


def attention_kernel(partners, n_seq, n_other, limit_ref, q_ref, *refs):
    n_blocks = 1 + len(partners)
    kv_refs = refs[:n_blocks]
    d_low, d_high, *refs = refs[n_blocks:]
    w_refs = refs[:n_other]
    grad_ref, probs_ref, dscores_ref, *part_refs = refs[n_other:]

    held, both = kv_refs[0].shape
    width = both // 2
    seq = lax.axis_index("seq")
    spots = []
    for r in [0, *partners]:
        first = lax.rem(seq - r + n_seq, n_seq) * held if partners else 0
        spots.append(first + lax.broadcasted_iota(jnp.int32, (held, 1), 0))
    alive = jnp.concatenate(spots, axis=0) < limit_ref[0:1, 0:1]

    rows = q_ref.shape[0]
    groups = range(width // HD)
    keys = [jnp.concatenate([ref[:, cols_of(g)] for ref in kv_refs], axis=0) for g in groups]
    scores = [dot(keys[g], pair_of((q_ref,), g), 1, 1) for g in groups]
    dprobs = []
    for g in groups:
        value = jnp.concatenate([ref[:, cols_of(g, width)] for ref in kv_refs], axis=0)
        dprobs.append(dot(value, pair_of((d_low, d_high), g), 1, 1))
    for g in groups:
        masked = jnp.where(alive, scores[g], jnp.float32(-1e30))
        top = jnp.max(masked, axis=0, keepdims=True)
        probs = jnp.exp2((masked - top) * exp2_scale)
        probs = probs * (1.0 / jnp.sum(probs, axis=0, keepdims=True))
        probs_low = probs.astype(jnp.bfloat16)
        delta = jnp.sum(probs_low.astype(jnp.float32) * dprobs[g], axis=0, keepdims=True)
        probs_ref[g] = probs_low
        dscores_ref[g] = (probs * (dprobs[g] - delta)).astype(jnp.bfloat16)
    for g in groups:
        grad_q = (query_scale * dot(keys[g], dscores_ref[g], 0, 0)).astype(jnp.bfloat16)
        for i in range(2):
            spot = (2 * g + i) * HD
            grad_ref[spot : spot + HD, :] = grad_q[:, i * rows : (i + 1) * rows]

    for w_ref, part_ref in zip(w_refs, part_refs):
        block = w_ref[: part_ref.shape[0], :]
        part_ref[...] = dot(block, grad_ref[...], 1, 0).astype(jnp.bfloat16)


def rest_kernel(n_other, grad_ref, *refs):
    for w_ref, part_ref in zip(refs[:n_other], refs[n_other:]):
        block = w_ref[w_ref.shape[0] - part_ref.shape[0] :, :]
        part_ref[...] = dot(block, grad_ref[...], 1, 0).astype(jnp.bfloat16)


def terms_kernel(probs_ref, dscores_ref, q_ref, d_low, d_high, *term_refs):
    held, both = term_refs[0].shape
    width = both // 2
    for g in range(width // HD):
        grad_k = (query_scale * dot(dscores_ref[g], pair_of((q_ref,), g), 1, 0)).astype(jnp.bfloat16)
        grad_v = dot(probs_ref[g], pair_of((d_low, d_high), g), 1, 0).astype(jnp.bfloat16)
        for r, ref in enumerate(term_refs):
            block = slice(r * held, (r + 1) * held)
            ref[:, g * HD : (g + 1) * HD] = grad_k[block]
            ref[:, width + g * HD : width + (g + 1) * HD] = grad_v[block]


def own_kernel(n_head, grad_ref, w_ref, out_ref, w_held, sem):
    feats = out_ref.shape[0]
    start = pl.multiple_of(lax.axis_index("head") * feats, 16)
    copy = pltpu.make_async_copy(w_ref.at[0, pl.ds(start, feats), :], w_held, sem)
    copy.start()
    copy.wait()
    out_ref[...] = dot(w_held[...], grad_ref[...], 1, 0)


def input_sum_kernel(n_other, start, own_ref, *refs):
    arrived = refs[:n_other]
    *_, out_ref, held, sem = refs
    at = slice(start, start + held.shape[0])
    total = own_ref[at, :]
    for ref in arrived:
        total = total + ref[...].astype(jnp.float32)
    held[...] = total.astype(jnp.bfloat16)
    copy = pltpu.make_async_copy(held, out_ref.at[0, at, :], sem)
    copy.start()
    copy.wait()


def term_sum_kernel(*refs):
    *terms, key_ref, value_ref = refs
    total = terms[0][...].astype(jnp.float32)
    for ref in terms[1:]:
        total = total + ref[...].astype(jnp.float32)
    low = total.astype(jnp.bfloat16)
    half = low.shape[1] // 2
    key_ref[0] = low[:, :half]
    value_ref[0] = low[:, half:]


VMEM = pl.BlockSpec(memory_space=pltpu.VMEM)
HBM = pl.BlockSpec(memory_space=pltpu.HBM)


def kernel_call(body, name, out_shape, in_specs, scratch=(), limit=VMEM_LIMIT):
    return pl.pallas_call(
        body,
        out_shape=out_shape,
        in_specs=in_specs,
        out_specs=jax.tree.map(lambda _: VMEM, out_shape),
        scratch_shapes=list(scratch),
        compiler_params=pltpu.CompilerParams(vmem_limit_bytes=limit),
        name=name,
    )


def on_device(queries, grad_out, keys, values, proj_query, section_span, span_prefix):
    n_seq, n_head = lax.axis_size("seq"), lax.axis_size("head")
    n_other = n_head - 1
    direct = n_seq <= MOST_PARTNERS
    low = jnp.bfloat16
    _, held, kv_width = keys.shape
    _, rows, width = queries.shape
    feats = proj_query.shape[1] // n_head

    def shape(*dims, dtype=low):
        return jax.ShapeDtypeStruct(dims, dtype)

    first = feats // 16 * 9 // 16 * 16
    partners = list(range(1, n_seq)) if direct else []
    n_copies = 1 + len(partners)
    *joined, grad_low, grad_high = kernel_call(
        functools.partial(join_kernel, n_copies),
        "join",
        [shape(held, 2 * kv_width)] * n_copies + [shape(rows // 2, width)] * 2,
        [HBM] * 3,
        [pltpu.SemaphoreType.DMA((4,))],
    )(*[in_hbm(x) for x in (keys, values, grad_out)])
    if direct:
        blocks = joined[-1:] + [shifted(x, "seq", r) for x, r in zip(joined, partners)]
    else:
        blocks = [lax.all_gather(joined[0], "seq", axis=0, tiled=True)]
    n_blocks, block_rows = len(blocks), blocks[0].shape[0]
    incoming = [shifted(part, "section", -1) for part in (grad_low, grad_high)]

    limit, q, *w_other = kernel_call(
        functools.partial(stage_kernel, n_head),
        "stage",
        [shape(8, HD, dtype=jnp.int32), shape(rows, width)] + [shape(feats, width)] * n_other,
        [HBM] * 4,
        [
            pltpu.SMEM(section_span.shape, jnp.int32),
            pltpu.SMEM(span_prefix.shape, jnp.int32),
            pltpu.SemaphoreType.DMA((1 + n_other,)),
            pltpu.SemaphoreType.DMA((2,)),
        ],
    )(*[in_hbm(x) for x in (section_span, span_prefix, queries, proj_query)])

    prefix = n_blocks * block_rows
    weights = shape(kv_width // HD, prefix, 2 * rows)
    grad_query, probs, dscores, *products = kernel_call(
        functools.partial(attention_kernel, partners, n_seq, n_other),
        "attention",
        [shape(width, rows), weights, weights] + [shape(first, rows)] * n_other,
        [VMEM] * (4 + n_blocks + n_other),
    )(limit, q, *blocks, *incoming, *w_other)
    rest = kernel_call(
        functools.partial(rest_kernel, n_other),
        "rest",
        [shape(feats - first, rows)] * n_other,
        [VMEM] * (1 + n_other),
    )(grad_query, *w_other)
    arrived = [shifted(p, "head", r + 1) for part in (products, rest) for r, p in enumerate(part)]
    terms = kernel_call(
        terms_kernel, "terms", [shape(block_rows, 2 * kv_width)] * n_blocks, [VMEM] * 5
    )(probs, dscores, q, *incoming)
    if direct:
        all_terms = [terms[0]] + [shifted(x, "seq", -r) for x, r in zip(terms[1:], partners)]
    else:
        all_terms = [lax.psum_scatter(terms[0], "seq", scatter_dimension=0, tiled=True)]

    own = kernel_call(
        functools.partial(own_kernel, n_head),
        "own",
        shape(feats, rows, dtype=jnp.float32),
        [VMEM, HBM],
        [pltpu.VMEM((feats, width), low), pltpu.SemaphoreType.DMA(())],
    )(grad_query, in_hbm(proj_query))
    grad_key, grad_value = kernel_call(
        term_sum_kernel, "term_sum", [shape(1, held, kv_width)] * 2, [VMEM] * len(all_terms)
    )(*all_terms)
    grad_input = []
    for start, part in ((0, arrived[:n_other]), (first, arrived[n_other:])):
        grad_input = [
            pl.pallas_call(
                functools.partial(input_sum_kernel, n_other, start),
                out_shape=shape(1, feats, rows),
                in_specs=[VMEM] * (1 + n_other) + [HBM] * len(grad_input),
                out_specs=HBM,
                scratch_shapes=[pltpu.VMEM(part[0].shape, low), pltpu.SemaphoreType.DMA(())],
                input_output_aliases={1 + n_other: 0} if grad_input else {},
                compiler_params=pltpu.CompilerParams(vmem_limit_bytes=VMEM_LIMIT),
                name="input_sum",
            )(own, *part, *grad_input)
        ]
    grad_input = grad_input[0]
    return (grad_input, grad_key, grad_value)


def solution(mesh):
    in_specs = (
        P("section", "seq", "head"),
        P("section", "seq", "head"),
        P("section", "seq", "head"),
        P("section", "seq", "head"),
        P("section", None, "head"),
        P(),
        P(),
    )
    out_specs = (
        P("section", "head", "seq"),
        P("section", "seq", "head"),
        P("section", "seq", "head"),
    )
    return jax.shard_map(
        on_device, mesh=mesh, in_specs=in_specs, out_specs=out_specs, check_vma=False
    )
```

```python
import functools
import math

import jax
import jax.numpy as jnp
from jax import lax
from jax.experimental import pallas as pl
from jax.experimental.pallas import tpu as pltpu
from jax.sharding import PartitionSpec as P

HD = 128
MOST_PARTNERS = 4
STEPS_OF_FOUR = ((1, 3, 0, 2), (3, 2, 1, 0), (2, 0, 3, 1))
VMEM_LIMIT = 40 * 1024 * 1024

query_scale = 168.0 ** (-0.5)
exp2_scale = query_scale * math.log2(math.e)


def shifted(block, axis, distance):
    devices = range(lax.axis_size(axis))
    route = [((i - distance) % len(devices), i) for i in devices]
    return lax.ppermute(block, axis, route)


def seq_steps(n):
    if n == len(STEPS_OF_FOUR) + 1:
        return STEPS_OF_FOUR
    return [[(i + r) % n for i in range(n)] for r in range(1, n)]


def sent(block, step):
    return lax.ppermute(block, "seq", list(enumerate(step)))


def sent_back(block, step):
    return lax.ppermute(block, "seq", [(to, i) for i, to in enumerate(step)])


def dot(left, right, left_dim, right_dim):
    return lax.dot_general(
        left, right, (((left_dim,), (right_dim,)), ((), ())), preferred_element_type=jnp.float32
    )


def in_hbm(x):
    return pltpu.with_memory_space_constraint(x, pltpu.HBM)


def join_kernel(n_copies, key_ref, value_ref, grad_ref, *refs):
    *outs, grad_low, grad_high, sems = refs
    width, rows = key_ref.shape[2], grad_low.shape[0]
    pairs = [
        (key_ref.at[0], outs[0].at[:, :width]),
        (value_ref.at[0], outs[0].at[:, width:]),
        (grad_ref.at[0, :rows, :], grad_low),
        (grad_ref.at[0, rows:, :], grad_high),
    ]
    copies = [pltpu.make_async_copy(a, b, sems.at[i]) for i, (a, b) in enumerate(pairs)]
    for copy in copies:
        copy.start()
    for copy in copies[:2]:
        copy.wait()
    for out in outs[1:]:
        out[...] = outs[0][...]
    for copy in copies[2:]:
        copy.wait()


def stage_kernel(n_head, span_ref, prefix_ref, q_ref, w_ref, limit_out, q_out, *refs):
    *other_outs, span, prefix, sems, small_sems = refs
    feats = w_ref.shape[1] // n_head
    head = lax.axis_index("head")
    copies = []
    for r, out in enumerate(other_outs):
        start = pl.multiple_of(lax.rem(head + r + 1, n_head) * feats, 16)
        copies.append((w_ref.at[0, pl.ds(start, feats), :], out))
    copies.append((q_ref.at[0], q_out))
    copies = [pltpu.make_async_copy(a, b, sems.at[i]) for i, (a, b) in enumerate(copies)]
    small = [
        pltpu.make_async_copy(a, b, small_sems.at[i])
        for i, (a, b) in enumerate([(span_ref, span), (prefix_ref, prefix)])
    ]
    for copy in small + copies:
        copy.start()
    for copy in small:
        copy.wait()
    live = prefix[span[lax.axis_index("section")]]
    limit_out[...] = jnp.full(limit_out.shape, live, jnp.int32)
    for copy in copies:
        copy.wait()


def pair_of(refs, g):
    cols = [slice((2 * g + i) * HD, (2 * g + i + 1) * HD) for i in range(2)]
    return jnp.concatenate([ref[:, c] for c in cols for ref in refs], axis=0)


def cols_of(g, start=0):
    return slice(start + g * HD, start + (g + 1) * HD)


def attention_kernel(partners, n_other, limit_ref, q_ref, *refs):
    n_blocks = 1 + len(partners)
    kv_refs = refs[:n_blocks]
    d_low, d_high, *refs = refs[n_blocks:]
    w_refs = refs[:n_other]
    grad_ref, probs_ref, dscores_ref, *part_refs = refs[n_other:]

    held, both = kv_refs[0].shape
    width = both // 2
    seq = lax.axis_index("seq")
    owners = [seq if partners else 0]
    for step in partners:
        owners.append(sum(jnp.where(seq == to, i, 0) for i, to in enumerate(step)))
    spots = [i * held + lax.broadcasted_iota(jnp.int32, (held, 1), 0) for i in owners]
    alive = jnp.concatenate(spots, axis=0) < limit_ref[0:1, 0:1]

    rows = q_ref.shape[0]
    groups = range(width // HD)
    keys = [jnp.concatenate([ref[:, cols_of(g)] for ref in kv_refs], axis=0) for g in groups]
    scores = [dot(keys[g], pair_of((q_ref,), g), 1, 1) for g in groups]
    dprobs = []
    for g in groups:
        value = jnp.concatenate([ref[:, cols_of(g, width)] for ref in kv_refs], axis=0)
        dprobs.append(dot(value, pair_of((d_low, d_high), g), 1, 1))
    for g in groups:
        masked = jnp.where(alive, scores[g], jnp.float32(-1e30))
        top = jnp.max(masked, axis=0, keepdims=True)
        probs = jnp.exp2((masked - top) * exp2_scale)
        probs = probs * (1.0 / jnp.sum(probs, axis=0, keepdims=True))
        probs_low = probs.astype(jnp.bfloat16)
        delta = jnp.sum(probs_low.astype(jnp.float32) * dprobs[g], axis=0, keepdims=True)
        probs_ref[g] = probs_low
        dscores_ref[g] = (probs * (dprobs[g] - delta)).astype(jnp.bfloat16)
    for g in groups:
        grad_q = (query_scale * dot(keys[g], dscores_ref[g], 0, 0)).astype(jnp.bfloat16)
        for i in range(2):
            spot = (2 * g + i) * HD
            grad_ref[spot : spot + HD, :] = grad_q[:, i * rows : (i + 1) * rows]

    for w_ref, part_ref in zip(w_refs, part_refs):
        block = w_ref[: part_ref.shape[0], :]
        part_ref[...] = dot(block, grad_ref[...], 1, 0).astype(jnp.bfloat16)


def rest_kernel(n_other, grad_ref, *refs):
    for w_ref, part_ref in zip(refs[:n_other], refs[n_other:]):
        block = w_ref[w_ref.shape[0] - part_ref.shape[0] :, :]
        part_ref[...] = dot(block, grad_ref[...], 1, 0).astype(jnp.bfloat16)


def terms_kernel(probs_ref, dscores_ref, q_ref, d_low, d_high, *term_refs):
    held, both = term_refs[0].shape
    width = both // 2
    for g in range(width // HD):
        grad_k = (query_scale * dot(dscores_ref[g], pair_of((q_ref,), g), 1, 0)).astype(jnp.bfloat16)
        grad_v = dot(probs_ref[g], pair_of((d_low, d_high), g), 1, 0).astype(jnp.bfloat16)
        for r, ref in enumerate(term_refs):
            block = slice(r * held, (r + 1) * held)
            ref[:, g * HD : (g + 1) * HD] = grad_k[block]
            ref[:, width + g * HD : width + (g + 1) * HD] = grad_v[block]


def own_kernel(n_head, grad_ref, w_ref, out_ref, w_held, sem):
    feats = out_ref.shape[0]
    start = pl.multiple_of(lax.axis_index("head") * feats, 16)
    copy = pltpu.make_async_copy(w_ref.at[0, pl.ds(start, feats), :], w_held, sem)
    copy.start()
    copy.wait()
    out_ref[...] = dot(w_held[...], grad_ref[...], 1, 0)


def input_sum_kernel(n_other, start, own_ref, *refs):
    arrived = refs[:n_other]
    *_, out_ref, held, sem = refs
    at = slice(start, start + held.shape[0])
    total = own_ref[at, :]
    for ref in arrived:
        total = total + ref[...].astype(jnp.float32)
    held[...] = total.astype(jnp.bfloat16)
    copy = pltpu.make_async_copy(held, out_ref.at[0, at, :], sem)
    copy.start()
    copy.wait()


def term_sum_kernel(*refs):
    *terms, key_ref, value_ref = refs
    total = terms[0][...].astype(jnp.float32)
    for ref in terms[1:]:
        total = total + ref[...].astype(jnp.float32)
    low = total.astype(jnp.bfloat16)
    half = low.shape[1] // 2
    key_ref[0] = low[:, :half]
    value_ref[0] = low[:, half:]


VMEM = pl.BlockSpec(memory_space=pltpu.VMEM)
HBM = pl.BlockSpec(memory_space=pltpu.HBM)


def kernel_call(body, name, out_shape, in_specs, scratch=(), limit=VMEM_LIMIT):
    return pl.pallas_call(
        body,
        out_shape=out_shape,
        in_specs=in_specs,
        out_specs=jax.tree.map(lambda _: VMEM, out_shape),
        scratch_shapes=list(scratch),
        compiler_params=pltpu.CompilerParams(vmem_limit_bytes=limit),
        name=name,
    )


def on_device(queries, grad_out, keys, values, proj_query, section_span, span_prefix):
    n_seq, n_head = lax.axis_size("seq"), lax.axis_size("head")
    n_other = n_head - 1
    direct = n_seq <= MOST_PARTNERS
    low = jnp.bfloat16
    _, held, kv_width = keys.shape
    _, rows, width = queries.shape
    feats = proj_query.shape[1] // n_head

    def shape(*dims, dtype=low):
        return jax.ShapeDtypeStruct(dims, dtype)

    first = feats // 16 * 9 // 16 * 16
    partners = seq_steps(n_seq) if direct else []
    n_copies = 1 + len(partners)
    *joined, grad_low, grad_high = kernel_call(
        functools.partial(join_kernel, n_copies),
        "join",
        [shape(held, 2 * kv_width)] * n_copies + [shape(rows // 2, width)] * 2,
        [HBM] * 3,
        [pltpu.SemaphoreType.DMA((4,))],
    )(*[in_hbm(x) for x in (keys, values, grad_out)])
    if direct:
        blocks = joined[-1:] + [sent(x, step) for x, step in zip(joined, partners)]
    else:
        blocks = [lax.all_gather(joined[0], "seq", axis=0, tiled=True)]
    n_blocks, block_rows = len(blocks), blocks[0].shape[0]
    incoming = [shifted(part, "section", -1) for part in (grad_low, grad_high)]

    limit, q, *w_other = kernel_call(
        functools.partial(stage_kernel, n_head),
        "stage",
        [shape(8, HD, dtype=jnp.int32), shape(rows, width)] + [shape(feats, width)] * n_other,
        [HBM] * 4,
        [
            pltpu.SMEM(section_span.shape, jnp.int32),
            pltpu.SMEM(span_prefix.shape, jnp.int32),
            pltpu.SemaphoreType.DMA((1 + n_other,)),
            pltpu.SemaphoreType.DMA((2,)),
        ],
    )(*[in_hbm(x) for x in (section_span, span_prefix, queries, proj_query)])

    prefix = n_blocks * block_rows
    weights = shape(kv_width // HD, prefix, 2 * rows)
    grad_query, probs, dscores, *products = kernel_call(
        functools.partial(attention_kernel, partners, n_other),
        "attention",
        [shape(width, rows), weights, weights] + [shape(first, rows)] * n_other,
        [VMEM] * (4 + n_blocks + n_other),
    )(limit, q, *blocks, *incoming, *w_other)
    rest = kernel_call(
        functools.partial(rest_kernel, n_other),
        "rest",
        [shape(feats - first, rows)] * n_other,
        [VMEM] * (1 + n_other),
    )(grad_query, *w_other)
    arrived = [shifted(p, "head", r + 1) for part in (products, rest) for r, p in enumerate(part)]
    terms = kernel_call(
        terms_kernel, "terms", [shape(block_rows, 2 * kv_width)] * n_blocks, [VMEM] * 5
    )(probs, dscores, q, *incoming)
    if direct:
        all_terms = [terms[0]] + [sent_back(x, step) for x, step in zip(terms[1:], partners)]
    else:
        all_terms = [lax.psum_scatter(terms[0], "seq", scatter_dimension=0, tiled=True)]

    own = kernel_call(
        functools.partial(own_kernel, n_head),
        "own",
        shape(feats, rows, dtype=jnp.float32),
        [VMEM, HBM],
        [pltpu.VMEM((feats, width), low), pltpu.SemaphoreType.DMA(())],
    )(grad_query, in_hbm(proj_query))
    grad_key, grad_value = kernel_call(
        term_sum_kernel, "term_sum", [shape(1, held, kv_width)] * 2, [VMEM] * len(all_terms)
    )(*all_terms)
    grad_input = []
    for start, part in ((0, arrived[:n_other]), (first, arrived[n_other:])):
        grad_input = [
            pl.pallas_call(
                functools.partial(input_sum_kernel, n_other, start),
                out_shape=shape(1, feats, rows),
                in_specs=[VMEM] * (1 + n_other) + [HBM] * len(grad_input),
                out_specs=HBM,
                scratch_shapes=[pltpu.VMEM(part[0].shape, low), pltpu.SemaphoreType.DMA(())],
                input_output_aliases={1 + n_other: 0} if grad_input else {},
                compiler_params=pltpu.CompilerParams(vmem_limit_bytes=VMEM_LIMIT),
                name="input_sum",
            )(own, *part, *grad_input)
        ]
    grad_input = grad_input[0]
    return (grad_input, grad_key, grad_value)


def solution(mesh):
    in_specs = (
        P("section", "seq", "head"),
        P("section", "seq", "head"),
        P("section", "seq", "head"),
        P("section", "seq", "head"),
        P("section", None, "head"),
        P(),
        P(),
    )
    out_specs = (
        P("section", "head", "seq"),
        P("section", "seq", "head"),
        P("section", "seq", "head"),
    )
    return jax.shard_map(
        on_device, mesh=mesh, in_specs=in_specs, out_specs=out_specs, check_vma=False
    )
```

```python
import functools
import math

import jax
import jax.numpy as jnp
from jax import lax
from jax.experimental import pallas as pl
from jax.experimental.pallas import tpu as pltpu
from jax.sharding import PartitionSpec as P

HD = 128
MOST_PARTNERS = 4
STEPS_OF_FOUR = ((2, 3, 1, 0), (3, 2, 0, 1), (1, 0, 3, 2))
VMEM_LIMIT = 40 * 1024 * 1024

query_scale = 168.0 ** (-0.5)
exp2_scale = query_scale * math.log2(math.e)


def shifted(block, axis, distance):
    devices = range(lax.axis_size(axis))
    route = [((i - distance) % len(devices), i) for i in devices]
    return lax.ppermute(block, axis, route)


def seq_steps(n):
    if n == len(STEPS_OF_FOUR) + 1:
        return STEPS_OF_FOUR
    return [[(i + r) % n for i in range(n)] for r in range(1, n)]


def sent(block, step):
    return lax.ppermute(block, "seq", list(enumerate(step)))


def sent_back(block, step):
    return lax.ppermute(block, "seq", [(to, i) for i, to in enumerate(step)])


def dot(left, right, left_dim, right_dim):
    return lax.dot_general(
        left, right, (((left_dim,), (right_dim,)), ((), ())), preferred_element_type=jnp.float32
    )


def in_hbm(x):
    return pltpu.with_memory_space_constraint(x, pltpu.HBM)


def join_kernel(n_copies, key_ref, value_ref, grad_ref, *refs):
    *outs, grad_low, grad_high, sems = refs
    width, rows = key_ref.shape[2], grad_low.shape[0]
    pairs = [
        (key_ref.at[0], outs[0].at[:, :width]),
        (value_ref.at[0], outs[0].at[:, width:]),
        (grad_ref.at[0, :rows, :], grad_low),
        (grad_ref.at[0, rows:, :], grad_high),
    ]
    copies = [pltpu.make_async_copy(a, b, sems.at[i]) for i, (a, b) in enumerate(pairs)]
    for copy in copies:
        copy.start()
    for copy in copies[:2]:
        copy.wait()
    for out in outs[1:]:
        out[...] = outs[0][...]
    for copy in copies[2:]:
        copy.wait()


def stage_kernel(n_head, span_ref, prefix_ref, q_ref, w_ref, limit_out, q_out, *refs):
    *other_outs, span, prefix, sems, small_sems = refs
    feats = w_ref.shape[1] // n_head
    head = lax.axis_index("head")
    copies = []
    for r, out in enumerate(other_outs):
        start = pl.multiple_of(lax.rem(head + r + 1, n_head) * feats, 16)
        copies.append((w_ref.at[0, pl.ds(start, feats), :], out))
    copies.append((q_ref.at[0], q_out))
    copies = [pltpu.make_async_copy(a, b, sems.at[i]) for i, (a, b) in enumerate(copies)]
    small = [
        pltpu.make_async_copy(a, b, small_sems.at[i])
        for i, (a, b) in enumerate([(span_ref, span), (prefix_ref, prefix)])
    ]
    for copy in small + copies:
        copy.start()
    for copy in small:
        copy.wait()
    live = prefix[span[lax.axis_index("section")]]
    limit_out[...] = jnp.full(limit_out.shape, live, jnp.int32)
    for copy in copies:
        copy.wait()


def pair_of(refs, g):
    cols = [slice((2 * g + i) * HD, (2 * g + i + 1) * HD) for i in range(2)]
    return jnp.concatenate([ref[:, c] for c in cols for ref in refs], axis=0)


def cols_of(g, start=0):
    return slice(start + g * HD, start + (g + 1) * HD)


def attention_kernel(partners, n_other, limit_ref, q_ref, *refs):
    n_blocks = 1 + len(partners)
    kv_refs = refs[:n_blocks]
    d_low, d_high, *refs = refs[n_blocks:]
    w_refs = refs[:n_other]
    grad_ref, probs_ref, dscores_ref, *part_refs = refs[n_other:]

    held, both = kv_refs[0].shape
    width = both // 2
    seq = lax.axis_index("seq")
    owners = [seq if partners else 0]
    for step in partners:
        owners.append(sum(jnp.where(seq == to, i, 0) for i, to in enumerate(step)))
    spots = [i * held + lax.broadcasted_iota(jnp.int32, (held, 1), 0) for i in owners]
    alive = jnp.concatenate(spots, axis=0) < limit_ref[0:1, 0:1]

    rows = q_ref.shape[0]
    groups = range(width // HD)
    keys = [jnp.concatenate([ref[:, cols_of(g)] for ref in kv_refs], axis=0) for g in groups]
    scores = [dot(keys[g], pair_of((q_ref,), g), 1, 1) for g in groups]
    dprobs = []
    for g in groups:
        value = jnp.concatenate([ref[:, cols_of(g, width)] for ref in kv_refs], axis=0)
        dprobs.append(dot(value, pair_of((d_low, d_high), g), 1, 1))
    for g in groups:
        masked = jnp.where(alive, scores[g], jnp.float32(-1e30))
        top = jnp.max(masked, axis=0, keepdims=True)
        probs = jnp.exp2((masked - top) * exp2_scale)
        probs = probs * (1.0 / jnp.sum(probs, axis=0, keepdims=True))
        probs_low = probs.astype(jnp.bfloat16)
        delta = jnp.sum(probs_low.astype(jnp.float32) * dprobs[g], axis=0, keepdims=True)
        probs_ref[g] = probs_low
        dscores_ref[g] = (probs * (dprobs[g] - delta)).astype(jnp.bfloat16)
    for g in groups:
        grad_q = (query_scale * dot(keys[g], dscores_ref[g], 0, 0)).astype(jnp.bfloat16)
        for i in range(2):
            spot = (2 * g + i) * HD
            grad_ref[spot : spot + HD, :] = grad_q[:, i * rows : (i + 1) * rows]

    for w_ref, part_ref in zip(w_refs, part_refs):
        block = w_ref[: part_ref.shape[0], :]
        part_ref[...] = dot(block, grad_ref[...], 1, 0).astype(jnp.bfloat16)


def rest_kernel(n_other, grad_ref, *refs):
    for w_ref, part_ref in zip(refs[:n_other], refs[n_other:]):
        block = w_ref[w_ref.shape[0] - part_ref.shape[0] :, :]
        part_ref[...] = dot(block, grad_ref[...], 1, 0).astype(jnp.bfloat16)


def terms_kernel(probs_ref, dscores_ref, q_ref, d_low, d_high, *term_refs):
    held, both = term_refs[0].shape
    width = both // 2
    for g in range(width // HD):
        grad_k = (query_scale * dot(dscores_ref[g], pair_of((q_ref,), g), 1, 0)).astype(jnp.bfloat16)
        grad_v = dot(probs_ref[g], pair_of((d_low, d_high), g), 1, 0).astype(jnp.bfloat16)
        for r, ref in enumerate(term_refs):
            block = slice(r * held, (r + 1) * held)
            ref[:, g * HD : (g + 1) * HD] = grad_k[block]
            ref[:, width + g * HD : width + (g + 1) * HD] = grad_v[block]


def own_kernel(n_head, grad_ref, w_ref, out_ref, w_held, sem):
    feats = out_ref.shape[0]
    start = pl.multiple_of(lax.axis_index("head") * feats, 16)
    copy = pltpu.make_async_copy(w_ref.at[0, pl.ds(start, feats), :], w_held, sem)
    copy.start()
    copy.wait()
    out_ref[...] = dot(w_held[...], grad_ref[...], 1, 0)


def input_sum_kernel(n_other, start, own_ref, *refs):
    arrived = refs[:n_other]
    *_, out_ref, held, sem = refs
    at = slice(start, start + held.shape[0])
    total = own_ref[at, :]
    for ref in arrived:
        total = total + ref[...].astype(jnp.float32)
    held[...] = total.astype(jnp.bfloat16)
    copy = pltpu.make_async_copy(held, out_ref.at[0, at, :], sem)
    copy.start()
    copy.wait()


def term_sum_kernel(*refs):
    *terms, key_ref, value_ref = refs
    total = terms[0][...].astype(jnp.float32)
    for ref in terms[1:]:
        total = total + ref[...].astype(jnp.float32)
    low = total.astype(jnp.bfloat16)
    half = low.shape[1] // 2
    key_ref[0] = low[:, :half]
    value_ref[0] = low[:, half:]


VMEM = pl.BlockSpec(memory_space=pltpu.VMEM)
HBM = pl.BlockSpec(memory_space=pltpu.HBM)


def kernel_call(body, name, out_shape, in_specs, scratch=(), limit=VMEM_LIMIT):
    return pl.pallas_call(
        body,
        out_shape=out_shape,
        in_specs=in_specs,
        out_specs=jax.tree.map(lambda _: VMEM, out_shape),
        scratch_shapes=list(scratch),
        compiler_params=pltpu.CompilerParams(vmem_limit_bytes=limit),
        name=name,
    )


def on_device(queries, grad_out, keys, values, proj_query, section_span, span_prefix):
    n_seq, n_head = lax.axis_size("seq"), lax.axis_size("head")
    n_other = n_head - 1
    direct = n_seq <= MOST_PARTNERS
    low = jnp.bfloat16
    _, held, kv_width = keys.shape
    _, rows, width = queries.shape
    feats = proj_query.shape[1] // n_head

    def shape(*dims, dtype=low):
        return jax.ShapeDtypeStruct(dims, dtype)

    first = feats // 16 * 9 // 16 * 16
    partners = seq_steps(n_seq) if direct else []
    n_copies = 1 + len(partners)
    *joined, grad_low, grad_high = kernel_call(
        functools.partial(join_kernel, n_copies),
        "join",
        [shape(held, 2 * kv_width)] * n_copies + [shape(rows // 2, width)] * 2,
        [HBM] * 3,
        [pltpu.SemaphoreType.DMA((4,))],
    )(*[in_hbm(x) for x in (keys, values, grad_out)])
    if direct:
        blocks = joined[-1:] + [sent(x, step) for x, step in zip(joined, partners)]
    else:
        blocks = [lax.all_gather(joined[0], "seq", axis=0, tiled=True)]
    n_blocks, block_rows = len(blocks), blocks[0].shape[0]
    incoming = [shifted(part, "section", -1) for part in (grad_low, grad_high)]

    limit, q, *w_other = kernel_call(
        functools.partial(stage_kernel, n_head),
        "stage",
        [shape(8, HD, dtype=jnp.int32), shape(rows, width)] + [shape(feats, width)] * n_other,
        [HBM] * 4,
        [
            pltpu.SMEM(section_span.shape, jnp.int32),
            pltpu.SMEM(span_prefix.shape, jnp.int32),
            pltpu.SemaphoreType.DMA((1 + n_other,)),
            pltpu.SemaphoreType.DMA((2,)),
        ],
    )(*[in_hbm(x) for x in (section_span, span_prefix, queries, proj_query)])

    prefix = n_blocks * block_rows
    weights = shape(kv_width // HD, prefix, 2 * rows)
    grad_query, probs, dscores, *products = kernel_call(
        functools.partial(attention_kernel, partners, n_other),
        "attention",
        [shape(width, rows), weights, weights] + [shape(first, rows)] * n_other,
        [VMEM] * (4 + n_blocks + n_other),
    )(limit, q, *blocks, *incoming, *w_other)
    rest = kernel_call(
        functools.partial(rest_kernel, n_other),
        "rest",
        [shape(feats - first, rows)] * n_other,
        [VMEM] * (1 + n_other),
    )(grad_query, *w_other)
    arrived = [shifted(p, "head", r + 1) for part in (products, rest) for r, p in enumerate(part)]
    terms = kernel_call(
        terms_kernel, "terms", [shape(block_rows, 2 * kv_width)] * n_blocks, [VMEM] * 5
    )(probs, dscores, q, *incoming)
    if direct:
        steps = reversed(list(zip(terms[1:], partners)))
        all_terms = [terms[0]] + [sent_back(x, step) for x, step in steps]
    else:
        all_terms = [lax.psum_scatter(terms[0], "seq", scatter_dimension=0, tiled=True)]

    own = kernel_call(
        functools.partial(own_kernel, n_head),
        "own",
        shape(feats, rows, dtype=jnp.float32),
        [VMEM, HBM],
        [pltpu.VMEM((feats, width), low), pltpu.SemaphoreType.DMA(())],
    )(grad_query, in_hbm(proj_query))
    grad_key, grad_value = kernel_call(
        term_sum_kernel, "term_sum", [shape(1, held, kv_width)] * 2, [VMEM] * len(all_terms)
    )(*all_terms)
    grad_input = []
    for start, part in ((0, arrived[:n_other]), (first, arrived[n_other:])):
        grad_input = [
            pl.pallas_call(
                functools.partial(input_sum_kernel, n_other, start),
                out_shape=shape(1, feats, rows),
                in_specs=[VMEM] * (1 + n_other) + [HBM] * len(grad_input),
                out_specs=HBM,
                scratch_shapes=[pltpu.VMEM(part[0].shape, low), pltpu.SemaphoreType.DMA(())],
                input_output_aliases={1 + n_other: 0} if grad_input else {},
                compiler_params=pltpu.CompilerParams(vmem_limit_bytes=VMEM_LIMIT),
                name="input_sum",
            )(own, *part, *grad_input)
        ]
    grad_input = grad_input[0]
    return (grad_input, grad_key, grad_value)


def solution(mesh):
    in_specs = (
        P("section", "seq", "head"),
        P("section", "seq", "head"),
        P("section", "seq", "head"),
        P("section", "seq", "head"),
        P("section", None, "head"),
        P(),
        P(),
    )
    out_specs = (
        P("section", "head", "seq"),
        P("section", "seq", "head"),
        P("section", "seq", "head"),
    )
    return jax.shard_map(
        on_device, mesh=mesh, in_specs=in_specs, out_specs=out_specs, check_vma=False
    )
```

```python
import functools
import math

import jax
import jax.numpy as jnp
from jax import lax
from jax.experimental import pallas as pl
from jax.experimental.pallas import tpu as pltpu
from jax.sharding import PartitionSpec as P

HD = 128
MOST_PARTNERS = 4
STEPS_OF_FOUR = ((1, 3, 0, 2), (3, 2, 1, 0), (2, 0, 3, 1))
VMEM_LIMIT = 40 * 1024 * 1024

query_scale = 168.0 ** (-0.5)
exp2_scale = query_scale * math.log2(math.e)


def shifted(block, axis, distance):
    devices = range(lax.axis_size(axis))
    route = [((i - distance) % len(devices), i) for i in devices]
    return lax.ppermute(block, axis, route)


def seq_steps(n):
    if n == len(STEPS_OF_FOUR) + 1:
        return STEPS_OF_FOUR
    return [[(i + r) % n for i in range(n)] for r in range(1, n)]


def sent(block, step):
    return lax.ppermute(block, "seq", list(enumerate(step)))


def sent_back(block, step):
    return lax.ppermute(block, "seq", [(to, i) for i, to in enumerate(step)])


def dot(left, right, left_dim, right_dim):
    return lax.dot_general(
        left, right, (((left_dim,), (right_dim,)), ((), ())), preferred_element_type=jnp.float32
    )


def in_hbm(x):
    return pltpu.with_memory_space_constraint(x, pltpu.HBM)


def join_kernel(n_copies, key_ref, value_ref, grad_ref, *refs):
    *outs, grad_low, grad_high, sems = refs
    width, rows = key_ref.shape[2], grad_low.shape[0]
    pairs = [
        (key_ref.at[0], outs[0].at[:, :width]),
        (value_ref.at[0], outs[0].at[:, width:]),
        (grad_ref.at[0, :rows, :], grad_low),
        (grad_ref.at[0, rows:, :], grad_high),
    ]
    copies = [pltpu.make_async_copy(a, b, sems.at[i]) for i, (a, b) in enumerate(pairs)]
    for copy in copies:
        copy.start()
    for copy in copies[:2]:
        copy.wait()
    for out in outs[1:]:
        out[...] = outs[0][...]
    for copy in copies[2:]:
        copy.wait()


def stage_kernel(n_head, span_ref, prefix_ref, q_ref, w_ref, limit_out, q_out, *refs):
    *other_outs, span, prefix, sems, small_sems = refs
    feats = w_ref.shape[1] // n_head
    head = lax.axis_index("head")
    copies = []
    for r, out in enumerate(other_outs):
        start = pl.multiple_of(lax.rem(head + r + 1, n_head) * feats, 16)
        copies.append((w_ref.at[0, pl.ds(start, feats), :], out))
    copies.append((q_ref.at[0], q_out))
    copies = [pltpu.make_async_copy(a, b, sems.at[i]) for i, (a, b) in enumerate(copies)]
    small = [
        pltpu.make_async_copy(a, b, small_sems.at[i])
        for i, (a, b) in enumerate([(span_ref, span), (prefix_ref, prefix)])
    ]
    for copy in small + copies:
        copy.start()
    for copy in small:
        copy.wait()
    live = prefix[span[lax.axis_index("section")]]
    limit_out[...] = jnp.full(limit_out.shape, live, jnp.int32)
    for copy in copies:
        copy.wait()


def pair_of(refs, g):
    cols = [slice((2 * g + i) * HD, (2 * g + i + 1) * HD) for i in range(2)]
    return jnp.concatenate([ref[:, c] for c in cols for ref in refs], axis=0)


def cols_of(g, start=0):
    return slice(start + g * HD, start + (g + 1) * HD)


def attention_kernel(partners, n_other, limit_ref, q_ref, *refs):
    most = 1 + len(partners[:-1])
    kv_refs, (d_low, d_high), refs = refs[:most], refs[most : most + 2], refs[most + 2 :]
    if partners:
        kv_refs, refs = kv_refs + refs[:1], refs[1:]
    w_refs = refs[:n_other]
    grad_ref, probs_ref, dscores_ref, *part_refs = refs[n_other:]

    held, both = kv_refs[0].shape
    width = both // 2
    seq = lax.axis_index("seq")
    owners = [seq if partners else 0]
    for step in partners:
        owners.append(sum(jnp.where(seq == to, i, 0) for i, to in enumerate(step)))
    spots = [i * held + lax.broadcasted_iota(jnp.int32, (held, 1), 0) for i in owners]
    alive = jnp.concatenate(spots, axis=0) < limit_ref[0:1, 0:1]

    rows = q_ref.shape[0]
    groups = range(width // HD)
    keys = [jnp.concatenate([ref[:, cols_of(g)] for ref in kv_refs], axis=0) for g in groups]
    scores = [dot(keys[g], pair_of((q_ref,), g), 1, 1) for g in groups]
    dprobs = []
    for g in groups:
        value = jnp.concatenate([ref[:, cols_of(g, width)] for ref in kv_refs], axis=0)
        dprobs.append(dot(value, pair_of((d_low, d_high), g), 1, 1))
    for g in groups:
        masked = jnp.where(alive, scores[g], jnp.float32(-1e30))
        top = jnp.max(masked, axis=0, keepdims=True)
        probs = jnp.exp2((masked - top) * exp2_scale)
        probs = probs * (1.0 / jnp.sum(probs, axis=0, keepdims=True))
        probs_low = probs.astype(jnp.bfloat16)
        delta = jnp.sum(probs_low.astype(jnp.float32) * dprobs[g], axis=0, keepdims=True)
        probs_ref[g] = probs_low
        dscores_ref[g] = (probs * (dprobs[g] - delta)).astype(jnp.bfloat16)
    for g in groups:
        grad_q = (query_scale * dot(keys[g], dscores_ref[g], 0, 0)).astype(jnp.bfloat16)
        for i in range(2):
            spot = (2 * g + i) * HD
            grad_ref[spot : spot + HD, :] = grad_q[:, i * rows : (i + 1) * rows]

    for w_ref, part_ref in zip(w_refs, part_refs):
        block = w_ref[: part_ref.shape[0], :]
        part_ref[...] = dot(block, grad_ref[...], 1, 0).astype(jnp.bfloat16)


def rest_kernel(n_other, grad_ref, *refs):
    for w_ref, part_ref in zip(refs[:n_other], refs[n_other:]):
        block = w_ref[w_ref.shape[0] - part_ref.shape[0] :, :]
        part_ref[...] = dot(block, grad_ref[...], 1, 0).astype(jnp.bfloat16)


def terms_kernel(probs_ref, dscores_ref, q_ref, d_low, d_high, *term_refs):
    held, both = term_refs[0].shape
    width = both // 2
    for g in range(width // HD):
        grad_k = (query_scale * dot(dscores_ref[g], pair_of((q_ref,), g), 1, 0)).astype(jnp.bfloat16)
        grad_v = dot(probs_ref[g], pair_of((d_low, d_high), g), 1, 0).astype(jnp.bfloat16)
        for r, ref in enumerate(term_refs):
            block = slice(r * held, (r + 1) * held)
            ref[:, g * HD : (g + 1) * HD] = grad_k[block]
            ref[:, width + g * HD : width + (g + 1) * HD] = grad_v[block]


def own_kernel(n_head, grad_ref, w_ref, out_ref, w_held, sem):
    feats = out_ref.shape[0]
    start = pl.multiple_of(lax.axis_index("head") * feats, 16)
    copy = pltpu.make_async_copy(w_ref.at[0, pl.ds(start, feats), :], w_held, sem)
    copy.start()
    copy.wait()
    out_ref[...] = dot(w_held[...], grad_ref[...], 1, 0)


def input_sum_kernel(n_other, start, own_ref, *refs):
    arrived = refs[:n_other]
    *_, out_ref, held, sem = refs
    at = slice(start, start + held.shape[0])
    total = own_ref[at, :]
    for ref in arrived:
        total = total + ref[...].astype(jnp.float32)
    held[...] = total.astype(jnp.bfloat16)
    copy = pltpu.make_async_copy(held, out_ref.at[0, at, :], sem)
    copy.start()
    copy.wait()


def term_sum_kernel(*refs):
    *terms, key_ref, value_ref = refs
    total = terms[0][...].astype(jnp.float32)
    for ref in terms[1:]:
        total = total + ref[...].astype(jnp.float32)
    low = total.astype(jnp.bfloat16)
    half = low.shape[1] // 2
    key_ref[0] = low[:, :half]
    value_ref[0] = low[:, half:]


VMEM = pl.BlockSpec(memory_space=pltpu.VMEM)
HBM = pl.BlockSpec(memory_space=pltpu.HBM)


def kernel_call(body, name, out_shape, in_specs, scratch=(), limit=VMEM_LIMIT):
    return pl.pallas_call(
        body,
        out_shape=out_shape,
        in_specs=in_specs,
        out_specs=jax.tree.map(lambda _: VMEM, out_shape),
        scratch_shapes=list(scratch),
        compiler_params=pltpu.CompilerParams(vmem_limit_bytes=limit),
        name=name,
    )


def on_device(queries, grad_out, keys, values, proj_query, section_span, span_prefix):
    n_seq, n_head = lax.axis_size("seq"), lax.axis_size("head")
    n_other = n_head - 1
    direct = n_seq <= MOST_PARTNERS
    low = jnp.bfloat16
    _, held, kv_width = keys.shape
    _, rows, width = queries.shape
    feats = proj_query.shape[1] // n_head

    def shape(*dims, dtype=low):
        return jax.ShapeDtypeStruct(dims, dtype)

    first = feats // 16 * 9 // 16 * 16
    partners = seq_steps(n_seq) if direct else []
    n_copies = 1 + len(partners)
    *joined, grad_low, grad_high = kernel_call(
        functools.partial(join_kernel, n_copies),
        "join",
        [shape(held, 2 * kv_width)] * n_copies + [shape(rows // 2, width)] * 2,
        [HBM] * 3,
        [pltpu.SemaphoreType.DMA((4,))],
    )(*[in_hbm(x) for x in (keys, values, grad_out)])
    if direct:
        blocks = joined[-1:] + [sent(x, step) for x, step in zip(joined, partners[:-1])]
    else:
        blocks = [lax.all_gather(joined[0], "seq", axis=0, tiled=True)]
    incoming = [shifted(part, "section", -1) for part in (grad_low, grad_high)]
    last = [sent(joined[len(partners) - 1], step) for step in partners[-1:]]
    n_blocks, block_rows = len(blocks) + len(last), blocks[0].shape[0]

    limit, q, *w_other = kernel_call(
        functools.partial(stage_kernel, n_head),
        "stage",
        [shape(8, HD, dtype=jnp.int32), shape(rows, width)] + [shape(feats, width)] * n_other,
        [HBM] * 4,
        [
            pltpu.SMEM(section_span.shape, jnp.int32),
            pltpu.SMEM(span_prefix.shape, jnp.int32),
            pltpu.SemaphoreType.DMA((1 + n_other,)),
            pltpu.SemaphoreType.DMA((2,)),
        ],
    )(*[in_hbm(x) for x in (section_span, span_prefix, queries, proj_query)])

    prefix = n_blocks * block_rows
    weights = shape(kv_width // HD, prefix, 2 * rows)
    grad_query, probs, dscores, *products = kernel_call(
        functools.partial(attention_kernel, partners, n_other),
        "attention",
        [shape(width, rows), weights, weights] + [shape(first, rows)] * n_other,
        [VMEM] * (4 + n_blocks + n_other),
    )(limit, q, *blocks, *incoming, *last, *w_other)
    rest = kernel_call(
        functools.partial(rest_kernel, n_other),
        "rest",
        [shape(feats - first, rows)] * n_other,
        [VMEM] * (1 + n_other),
    )(grad_query, *w_other)
    arrived = [shifted(p, "head", r + 1) for part in (products, rest) for r, p in enumerate(part)]
    terms = kernel_call(
        terms_kernel, "terms", [shape(block_rows, 2 * kv_width)] * n_blocks, [VMEM] * 5
    )(probs, dscores, q, *incoming)
    if direct:
        all_terms = [terms[0]] + [sent_back(x, step) for x, step in zip(terms[1:], partners)]
    else:
        all_terms = [lax.psum_scatter(terms[0], "seq", scatter_dimension=0, tiled=True)]

    own = kernel_call(
        functools.partial(own_kernel, n_head),
        "own",
        shape(feats, rows, dtype=jnp.float32),
        [VMEM, HBM],
        [pltpu.VMEM((feats, width), low), pltpu.SemaphoreType.DMA(())],
    )(grad_query, in_hbm(proj_query))
    grad_key, grad_value = kernel_call(
        term_sum_kernel, "term_sum", [shape(1, held, kv_width)] * 2, [VMEM] * len(all_terms)
    )(*all_terms)
    grad_input = []
    for start, part in ((0, arrived[:n_other]), (first, arrived[n_other:])):
        grad_input = [
            pl.pallas_call(
                functools.partial(input_sum_kernel, n_other, start),
                out_shape=shape(1, feats, rows),
                in_specs=[VMEM] * (1 + n_other) + [HBM] * len(grad_input),
                out_specs=HBM,
                scratch_shapes=[pltpu.VMEM(part[0].shape, low), pltpu.SemaphoreType.DMA(())],
                input_output_aliases={1 + n_other: 0} if grad_input else {},
                compiler_params=pltpu.CompilerParams(vmem_limit_bytes=VMEM_LIMIT),
                name="input_sum",
            )(own, *part, *grad_input)
        ]
    grad_input = grad_input[0]
    return (grad_input, grad_key, grad_value)


def solution(mesh):
    in_specs = (
        P("section", "seq", "head"),
        P("section", "seq", "head"),
        P("section", "seq", "head"),
        P("section", "seq", "head"),
        P("section", None, "head"),
        P(),
        P(),
    )
    out_specs = (
        P("section", "head", "seq"),
        P("section", "seq", "head"),
        P("section", "seq", "head"),
    )
    return jax.shard_map(
        on_device, mesh=mesh, in_specs=in_specs, out_specs=out_specs, check_vma=False
    )
```

```python
import functools
import math

import jax
import jax.numpy as jnp
from jax import lax
from jax.experimental import pallas as pl
from jax.experimental.pallas import tpu as pltpu
from jax.sharding import PartitionSpec as P

HD = 128
MOST_PARTNERS = 4
STEPS_OF_FOUR = ((1, 3, 0, 2), (2, 0, 3, 1), (3, 2, 1, 0))
VMEM_LIMIT = 40 * 1024 * 1024

query_scale = 168.0 ** (-0.5)
exp2_scale = query_scale * math.log2(math.e)


def shifted(block, axis, distance):
    devices = range(lax.axis_size(axis))
    route = [((i - distance) % len(devices), i) for i in devices]
    return lax.ppermute(block, axis, route)


def seq_steps(n):
    if n == len(STEPS_OF_FOUR) + 1:
        return STEPS_OF_FOUR
    return [[(i + r) % n for i in range(n)] for r in range(1, n)]


def sent(block, step):
    return lax.ppermute(block, "seq", list(enumerate(step)))


def sent_back(block, step):
    return lax.ppermute(block, "seq", [(to, i) for i, to in enumerate(step)])


def dot(left, right, left_dim, right_dim):
    return lax.dot_general(
        left, right, (((left_dim,), (right_dim,)), ((), ())), preferred_element_type=jnp.float32
    )


def in_hbm(x):
    return pltpu.with_memory_space_constraint(x, pltpu.HBM)


def join_kernel(n_copies, key_ref, value_ref, grad_ref, *refs):
    *outs, grad_low, grad_high, sems = refs
    width, rows = key_ref.shape[2], grad_low.shape[0]
    pairs = [
        (key_ref.at[0], outs[0].at[:, :width]),
        (value_ref.at[0], outs[0].at[:, width:]),
        (grad_ref.at[0, :rows, :], grad_low),
        (grad_ref.at[0, rows:, :], grad_high),
    ]
    copies = [pltpu.make_async_copy(a, b, sems.at[i]) for i, (a, b) in enumerate(pairs)]
    for copy in copies:
        copy.start()
    for copy in copies[:2]:
        copy.wait()
    for out in outs[1:]:
        out[...] = outs[0][...]
    for copy in copies[2:]:
        copy.wait()


def stage_kernel(n_head, span_ref, prefix_ref, q_ref, w_ref, limit_out, q_out, *refs):
    *other_outs, span, prefix, sems, small_sems = refs
    feats = w_ref.shape[1] // n_head
    head = lax.axis_index("head")
    copies = []
    for r, out in enumerate(other_outs):
        start = pl.multiple_of(lax.rem(head + r + 1, n_head) * feats, 16)
        copies.append((w_ref.at[0, pl.ds(start, feats), :], out))
    copies.append((q_ref.at[0], q_out))
    copies = [pltpu.make_async_copy(a, b, sems.at[i]) for i, (a, b) in enumerate(copies)]
    small = [
        pltpu.make_async_copy(a, b, small_sems.at[i])
        for i, (a, b) in enumerate([(span_ref, span), (prefix_ref, prefix)])
    ]
    for copy in small + copies:
        copy.start()
    for copy in small:
        copy.wait()
    live = prefix[span[lax.axis_index("section")]]
    limit_out[...] = jnp.full(limit_out.shape, live, jnp.int32)
    for copy in copies:
        copy.wait()


def pair_of(refs, g):
    cols = [slice((2 * g + i) * HD, (2 * g + i + 1) * HD) for i in range(2)]
    return jnp.concatenate([ref[:, c] for c in cols for ref in refs], axis=0)


def cols_of(g, start=0):
    return slice(start + g * HD, start + (g + 1) * HD)


def attention_kernel(partners, n_other, limit_ref, q_ref, *refs):
    most = 1 + len(partners[:-1])
    kv_refs, (d_low, d_high), refs = refs[:most], refs[most : most + 2], refs[most + 2 :]
    if partners:
        kv_refs, refs = kv_refs + refs[:1], refs[1:]
    w_refs = refs[:n_other]
    grad_ref, probs_ref, dscores_ref, *part_refs = refs[n_other:]

    held, both = kv_refs[0].shape
    width = both // 2
    seq = lax.axis_index("seq")
    owners = [seq if partners else 0]
    for step in partners:
        owners.append(sum(jnp.where(seq == to, i, 0) for i, to in enumerate(step)))
    spots = [i * held + lax.broadcasted_iota(jnp.int32, (held, 1), 0) for i in owners]
    alive = jnp.concatenate(spots, axis=0) < limit_ref[0:1, 0:1]

    rows = q_ref.shape[0]
    groups = range(width // HD)
    keys = [jnp.concatenate([ref[:, cols_of(g)] for ref in kv_refs], axis=0) for g in groups]
    scores = [dot(keys[g], pair_of((q_ref,), g), 1, 1) for g in groups]
    dprobs = []
    for g in groups:
        value = jnp.concatenate([ref[:, cols_of(g, width)] for ref in kv_refs], axis=0)
        dprobs.append(dot(value, pair_of((d_low, d_high), g), 1, 1))
    for g in groups:
        masked = jnp.where(alive, scores[g], jnp.float32(-1e30))
        top = jnp.max(masked, axis=0, keepdims=True)
        probs = jnp.exp2((masked - top) * exp2_scale)
        probs = probs * (1.0 / jnp.sum(probs, axis=0, keepdims=True))
        probs_low = probs.astype(jnp.bfloat16)
        delta = jnp.sum(probs_low.astype(jnp.float32) * dprobs[g], axis=0, keepdims=True)
        probs_ref[g] = probs_low
        dscores_ref[g] = (probs * (dprobs[g] - delta)).astype(jnp.bfloat16)
    for g in groups:
        grad_q = (query_scale * dot(keys[g], dscores_ref[g], 0, 0)).astype(jnp.bfloat16)
        for i in range(2):
            spot = (2 * g + i) * HD
            grad_ref[spot : spot + HD, :] = grad_q[:, i * rows : (i + 1) * rows]

    for w_ref, part_ref in zip(w_refs, part_refs):
        block = w_ref[: part_ref.shape[0], :]
        part_ref[...] = dot(block, grad_ref[...], 1, 0).astype(jnp.bfloat16)


def rest_kernel(n_other, grad_ref, *refs):
    for w_ref, part_ref in zip(refs[:n_other], refs[n_other:]):
        block = w_ref[w_ref.shape[0] - part_ref.shape[0] :, :]
        part_ref[...] = dot(block, grad_ref[...], 1, 0).astype(jnp.bfloat16)


def terms_kernel(probs_ref, dscores_ref, q_ref, d_low, d_high, *term_refs):
    held, both = term_refs[0].shape
    width = both // 2
    for g in range(width // HD):
        grad_k = (query_scale * dot(dscores_ref[g], pair_of((q_ref,), g), 1, 0)).astype(jnp.bfloat16)
        grad_v = dot(probs_ref[g], pair_of((d_low, d_high), g), 1, 0).astype(jnp.bfloat16)
        for r, ref in enumerate(term_refs):
            block = slice(r * held, (r + 1) * held)
            ref[:, g * HD : (g + 1) * HD] = grad_k[block]
            ref[:, width + g * HD : width + (g + 1) * HD] = grad_v[block]


def own_kernel(n_head, grad_ref, w_ref, out_ref, w_held, sem):
    feats = out_ref.shape[0]
    start = pl.multiple_of(lax.axis_index("head") * feats, 16)
    copy = pltpu.make_async_copy(w_ref.at[0, pl.ds(start, feats), :], w_held, sem)
    copy.start()
    copy.wait()
    out_ref[...] = dot(w_held[...], grad_ref[...], 1, 0)


def input_sum_kernel(n_other, start, own_ref, *refs):
    arrived = refs[:n_other]
    *_, out_ref, held, sem = refs
    at = slice(start, start + held.shape[0])
    total = own_ref[at, :]
    for ref in arrived:
        total = total + ref[...].astype(jnp.float32)
    held[...] = total.astype(jnp.bfloat16)
    copy = pltpu.make_async_copy(held, out_ref.at[0, at, :], sem)
    copy.start()
    copy.wait()


def term_sum_kernel(*refs):
    *terms, key_ref, value_ref = refs
    total = terms[0][...].astype(jnp.float32)
    for ref in terms[1:]:
        total = total + ref[...].astype(jnp.float32)
    low = total.astype(jnp.bfloat16)
    half = low.shape[1] // 2
    key_ref[0] = low[:, :half]
    value_ref[0] = low[:, half:]


VMEM = pl.BlockSpec(memory_space=pltpu.VMEM)
HBM = pl.BlockSpec(memory_space=pltpu.HBM)


def kernel_call(body, name, out_shape, in_specs, scratch=(), limit=VMEM_LIMIT):
    return pl.pallas_call(
        body,
        out_shape=out_shape,
        in_specs=in_specs,
        out_specs=jax.tree.map(lambda _: VMEM, out_shape),
        scratch_shapes=list(scratch),
        compiler_params=pltpu.CompilerParams(vmem_limit_bytes=limit),
        name=name,
    )


def on_device(queries, grad_out, keys, values, proj_query, section_span, span_prefix):
    n_seq, n_head = lax.axis_size("seq"), lax.axis_size("head")
    n_other = n_head - 1
    direct = n_seq <= MOST_PARTNERS
    low = jnp.bfloat16
    _, held, kv_width = keys.shape
    _, rows, width = queries.shape
    feats = proj_query.shape[1] // n_head

    def shape(*dims, dtype=low):
        return jax.ShapeDtypeStruct(dims, dtype)

    first = feats // 16 * 9 // 16 * 16
    partners = seq_steps(n_seq) if direct else []
    n_copies = 1 + len(partners)
    *joined, grad_low, grad_high = kernel_call(
        functools.partial(join_kernel, n_copies),
        "join",
        [shape(held, 2 * kv_width)] * n_copies + [shape(rows // 2, width)] * 2,
        [HBM] * 3,
        [pltpu.SemaphoreType.DMA((4,))],
    )(*[in_hbm(x) for x in (keys, values, grad_out)])
    if direct:
        blocks = joined[-1:] + [sent(x, step) for x, step in zip(joined, partners[:-1])]
    else:
        blocks = [lax.all_gather(joined[0], "seq", axis=0, tiled=True)]
    incoming = [shifted(part, "section", -1) for part in (grad_low, grad_high)]
    last = [sent(joined[len(partners) - 1], step) for step in partners[-1:]]
    n_blocks, block_rows = len(blocks) + len(last), blocks[0].shape[0]

    limit, q, *w_other = kernel_call(
        functools.partial(stage_kernel, n_head),
        "stage",
        [shape(8, HD, dtype=jnp.int32), shape(rows, width)] + [shape(feats, width)] * n_other,
        [HBM] * 4,
        [
            pltpu.SMEM(section_span.shape, jnp.int32),
            pltpu.SMEM(span_prefix.shape, jnp.int32),
            pltpu.SemaphoreType.DMA((1 + n_other,)),
            pltpu.SemaphoreType.DMA((2,)),
        ],
    )(*[in_hbm(x) for x in (section_span, span_prefix, queries, proj_query)])

    prefix = n_blocks * block_rows
    weights = shape(kv_width // HD, prefix, 2 * rows)
    grad_query, probs, dscores, *products = kernel_call(
        functools.partial(attention_kernel, partners, n_other),
        "attention",
        [shape(width, rows), weights, weights] + [shape(first, rows)] * n_other,
        [VMEM] * (4 + n_blocks + n_other),
    )(limit, q, *blocks, *incoming, *last, *w_other)
    rest = kernel_call(
        functools.partial(rest_kernel, n_other),
        "rest",
        [shape(feats - first, rows)] * n_other,
        [VMEM] * (1 + n_other),
    )(grad_query, *w_other)
    arrived = [shifted(p, "head", r + 1) for part in (products, rest) for r, p in enumerate(part)]
    terms = kernel_call(
        terms_kernel, "terms", [shape(block_rows, 2 * kv_width)] * n_blocks, [VMEM] * 5
    )(probs, dscores, q, *incoming)
    if direct:
        all_terms = [terms[0]] + [sent_back(x, step) for x, step in zip(terms[1:], partners)]
    else:
        all_terms = [lax.psum_scatter(terms[0], "seq", scatter_dimension=0, tiled=True)]

    own = kernel_call(
        functools.partial(own_kernel, n_head),
        "own",
        shape(feats, rows, dtype=jnp.float32),
        [VMEM, HBM],
        [pltpu.VMEM((feats, width), low), pltpu.SemaphoreType.DMA(())],
    )(grad_query, in_hbm(proj_query))
    grad_key, grad_value = kernel_call(
        term_sum_kernel, "term_sum", [shape(1, held, kv_width)] * 2, [VMEM] * len(all_terms)
    )(*all_terms)
    grad_input = []
    for start, part in ((0, arrived[:n_other]), (first, arrived[n_other:])):
        grad_input = [
            pl.pallas_call(
                functools.partial(input_sum_kernel, n_other, start),
                out_shape=shape(1, feats, rows),
                in_specs=[VMEM] * (1 + n_other) + [HBM] * len(grad_input),
                out_specs=HBM,
                scratch_shapes=[pltpu.VMEM(part[0].shape, low), pltpu.SemaphoreType.DMA(())],
                input_output_aliases={1 + n_other: 0} if grad_input else {},
                compiler_params=pltpu.CompilerParams(vmem_limit_bytes=VMEM_LIMIT),
                name="input_sum",
            )(own, *part, *grad_input)
        ]
    grad_input = grad_input[0]
    return (grad_input, grad_key, grad_value)


def solution(mesh):
    in_specs = (
        P("section", "seq", "head"),
        P("section", "seq", "head"),
        P("section", "seq", "head"),
        P("section", "seq", "head"),
        P("section", None, "head"),
        P(),
        P(),
    )
    out_specs = (
        P("section", "head", "seq"),
        P("section", "seq", "head"),
        P("section", "seq", "head"),
    )
    return jax.shard_map(
        on_device, mesh=mesh, in_specs=in_specs, out_specs=out_specs, check_vma=False
    )
```

```python
import functools
import math

import jax
import jax.numpy as jnp
from jax import lax
from jax.experimental import pallas as pl
from jax.experimental.pallas import tpu as pltpu
from jax.sharding import PartitionSpec as P

HD = 128
MOST_PARTNERS = 4
VMEM_LIMIT = 40 * 1024 * 1024

query_scale = 168.0 ** (-0.5)
exp2_scale = query_scale * math.log2(math.e)


def shifted(block, axis, distance):
    devices = range(lax.axis_size(axis))
    route = [((i - distance) % len(devices), i) for i in devices]
    return lax.ppermute(block, axis, route)


def swapped(block, axis, distance):
    return lax.ppermute(block, axis, [(i, i ^ distance) for i in range(lax.axis_size(axis))])


def dot(left, right, left_dim, right_dim):
    return lax.dot_general(
        left, right, (((left_dim,), (right_dim,)), ((), ())), preferred_element_type=jnp.float32
    )


def in_hbm(x):
    return pltpu.with_memory_space_constraint(x, pltpu.HBM)


def join_kernel(n_copies, key_ref, value_ref, grad_ref, *refs):
    *outs, grad_low, grad_high, sems = refs
    width, rows = key_ref.shape[2], grad_low.shape[0]
    pairs = [
        (key_ref.at[0], outs[0].at[:, :width]),
        (value_ref.at[0], outs[0].at[:, width:]),
        (grad_ref.at[0, :rows, :], grad_low),
        (grad_ref.at[0, rows:, :], grad_high),
    ]
    copies = [pltpu.make_async_copy(a, b, sems.at[i]) for i, (a, b) in enumerate(pairs)]
    for copy in copies:
        copy.start()
    for copy in copies[:2]:
        copy.wait()
    for out in outs[1:]:
        out[...] = outs[0][...]
    for copy in copies[2:]:
        copy.wait()


def stage_kernel(n_head, span_ref, prefix_ref, q_ref, w_ref, limit_out, q_out, *refs):
    *other_outs, span, prefix, sems, small_sems = refs
    feats = w_ref.shape[1] // n_head
    head = lax.axis_index("head")
    copies = []
    for r, out in enumerate(other_outs):
        start = pl.multiple_of(lax.rem(head + r + 1, n_head) * feats, 16)
        copies.append((w_ref.at[0, pl.ds(start, feats), :], out))
    copies.append((q_ref.at[0], q_out))
    copies = [pltpu.make_async_copy(a, b, sems.at[i]) for i, (a, b) in enumerate(copies)]
    small = [
        pltpu.make_async_copy(a, b, small_sems.at[i])
        for i, (a, b) in enumerate([(span_ref, span), (prefix_ref, prefix)])
    ]
    for copy in small + copies:
        copy.start()
    for copy in small:
        copy.wait()
    live = prefix[span[lax.axis_index("section")]]
    limit_out[...] = jnp.full(limit_out.shape, live, jnp.int32)
    for copy in copies:
        copy.wait()


def pair_of(refs, g):
    cols = [slice((2 * g + i) * HD, (2 * g + i + 1) * HD) for i in range(2)]
    return jnp.concatenate([ref[:, c] for c in cols for ref in refs], axis=0)


def cols_of(g, start=0):
    return slice(start + g * HD, start + (g + 1) * HD)


def attention_kernel(partners, n_other, limit_ref, q_ref, *refs):
    n_blocks = 1 + len(partners)
    kv_refs = refs[:n_blocks]
    d_low, d_high, *refs = refs[n_blocks:]
    w_refs = refs[:n_other]
    grad_ref, probs_ref, dscores_ref, *part_refs = refs[n_other:]

    held, both = kv_refs[0].shape
    width = both // 2
    seq = lax.axis_index("seq")
    spots = []
    for r in [0, *partners]:
        first = jnp.bitwise_xor(seq, r) * held if partners else 0
        spots.append(first + lax.broadcasted_iota(jnp.int32, (held, 1), 0))
    alive = jnp.concatenate(spots, axis=0) < limit_ref[0:1, 0:1]

    rows = q_ref.shape[0]
    groups = range(width // HD)
    keys = [jnp.concatenate([ref[:, cols_of(g)] for ref in kv_refs], axis=0) for g in groups]
    scores = [dot(keys[g], pair_of((q_ref,), g), 1, 1) for g in groups]
    dprobs = []
    for g in groups:
        value = jnp.concatenate([ref[:, cols_of(g, width)] for ref in kv_refs], axis=0)
        dprobs.append(dot(value, pair_of((d_low, d_high), g), 1, 1))
    for g in groups:
        masked = jnp.where(alive, scores[g], jnp.float32(-1e30))
        top = jnp.max(masked, axis=0, keepdims=True)
        probs = jnp.exp2((masked - top) * exp2_scale)
        probs = probs * (1.0 / jnp.sum(probs, axis=0, keepdims=True))
        probs_low = probs.astype(jnp.bfloat16)
        delta = jnp.sum(probs_low.astype(jnp.float32) * dprobs[g], axis=0, keepdims=True)
        probs_ref[g] = probs_low
        dscores_ref[g] = (probs * (dprobs[g] - delta)).astype(jnp.bfloat16)
    for g in groups:
        grad_q = (query_scale * dot(keys[g], dscores_ref[g], 0, 0)).astype(jnp.bfloat16)
        for i in range(2):
            spot = (2 * g + i) * HD
            grad_ref[spot : spot + HD, :] = grad_q[:, i * rows : (i + 1) * rows]

    for w_ref, part_ref in zip(w_refs, part_refs):
        block = w_ref[: part_ref.shape[0], :]
        part_ref[...] = dot(block, grad_ref[...], 1, 0).astype(jnp.bfloat16)


def rest_kernel(n_other, grad_ref, *refs):
    for w_ref, part_ref in zip(refs[:n_other], refs[n_other:]):
        block = w_ref[w_ref.shape[0] - part_ref.shape[0] :, :]
        part_ref[...] = dot(block, grad_ref[...], 1, 0).astype(jnp.bfloat16)


def terms_kernel(probs_ref, dscores_ref, q_ref, d_low, d_high, *term_refs):
    held, both = term_refs[0].shape
    width = both // 2
    for g in range(width // HD):
        grad_k = (query_scale * dot(dscores_ref[g], pair_of((q_ref,), g), 1, 0)).astype(jnp.bfloat16)
        grad_v = dot(probs_ref[g], pair_of((d_low, d_high), g), 1, 0).astype(jnp.bfloat16)
        for r, ref in enumerate(term_refs):
            block = slice(r * held, (r + 1) * held)
            ref[:, g * HD : (g + 1) * HD] = grad_k[block]
            ref[:, width + g * HD : width + (g + 1) * HD] = grad_v[block]


def own_kernel(n_head, grad_ref, w_ref, out_ref, w_held, sem):
    feats = out_ref.shape[0]
    start = pl.multiple_of(lax.axis_index("head") * feats, 16)
    copy = pltpu.make_async_copy(w_ref.at[0, pl.ds(start, feats), :], w_held, sem)
    copy.start()
    copy.wait()
    out_ref[...] = dot(w_held[...], grad_ref[...], 1, 0)


def input_sum_kernel(n_other, start, own_ref, *refs):
    arrived = refs[:n_other]
    *_, out_ref, held, sem = refs
    at = slice(start, start + held.shape[0])
    total = own_ref[at, :]
    for ref in arrived:
        total = total + ref[...].astype(jnp.float32)
    held[...] = total.astype(jnp.bfloat16)
    copy = pltpu.make_async_copy(held, out_ref.at[0, at, :], sem)
    copy.start()
    copy.wait()


def term_sum_kernel(*refs):
    *terms, key_ref, value_ref = refs
    total = terms[0][...].astype(jnp.float32)
    for ref in terms[1:]:
        total = total + ref[...].astype(jnp.float32)
    low = total.astype(jnp.bfloat16)
    half = low.shape[1] // 2
    key_ref[0] = low[:, :half]
    value_ref[0] = low[:, half:]


VMEM = pl.BlockSpec(memory_space=pltpu.VMEM)
HBM = pl.BlockSpec(memory_space=pltpu.HBM)


def kernel_call(body, name, out_shape, in_specs, scratch=(), limit=VMEM_LIMIT):
    return pl.pallas_call(
        body,
        out_shape=out_shape,
        in_specs=in_specs,
        out_specs=jax.tree.map(lambda _: VMEM, out_shape),
        scratch_shapes=list(scratch),
        compiler_params=pltpu.CompilerParams(vmem_limit_bytes=limit),
        name=name,
    )


def on_device(queries, grad_out, keys, values, proj_query, section_span, span_prefix):
    n_seq, n_head = lax.axis_size("seq"), lax.axis_size("head")
    n_other = n_head - 1
    direct = n_seq <= MOST_PARTNERS and n_seq & (n_seq - 1) == 0
    low = jnp.bfloat16
    _, held, kv_width = keys.shape
    _, rows, width = queries.shape
    feats = proj_query.shape[1] // n_head

    def shape(*dims, dtype=low):
        return jax.ShapeDtypeStruct(dims, dtype)

    first = feats // 16 * 17 // 32 * 16
    partners = list(range(1, n_seq)) if direct else []
    n_copies = 1 + len(partners)
    *joined, grad_low, grad_high = kernel_call(
        functools.partial(join_kernel, n_copies),
        "join",
        [shape(held, 2 * kv_width)] * n_copies + [shape(rows // 2, width)] * 2,
        [HBM] * 3,
        [pltpu.SemaphoreType.DMA((4,))],
    )(*[in_hbm(x) for x in (keys, values, grad_out)])
    if direct:
        blocks = joined[-1:] + [swapped(x, "seq", r) for x, r in zip(joined, partners)]
    else:
        blocks = [lax.all_gather(joined[0], "seq", axis=0, tiled=True)]
    n_blocks, block_rows = len(blocks), blocks[0].shape[0]
    incoming = [shifted(part, "section", -1) for part in (grad_low, grad_high)]

    limit, q, *w_other = kernel_call(
        functools.partial(stage_kernel, n_head),
        "stage",
        [shape(8, HD, dtype=jnp.int32), shape(rows, width)] + [shape(feats, width)] * n_other,
        [HBM] * 4,
        [
            pltpu.SMEM(section_span.shape, jnp.int32),
            pltpu.SMEM(span_prefix.shape, jnp.int32),
            pltpu.SemaphoreType.DMA((1 + n_other,)),
            pltpu.SemaphoreType.DMA((2,)),
        ],
    )(*[in_hbm(x) for x in (section_span, span_prefix, queries, proj_query)])

    prefix = n_blocks * block_rows
    weights = shape(kv_width // HD, prefix, 2 * rows)
    grad_query, probs, dscores, *products = kernel_call(
        functools.partial(attention_kernel, partners, n_other),
        "attention",
        [shape(width, rows), weights, weights] + [shape(first, rows)] * n_other,
        [VMEM] * (4 + n_blocks + n_other),
    )(limit, q, *blocks, *incoming, *w_other)
    rest = kernel_call(
        functools.partial(rest_kernel, n_other),
        "rest",
        [shape(feats - first, rows)] * n_other,
        [VMEM] * (1 + n_other),
    )(grad_query, *w_other)
    arrived = [shifted(p, "head", r + 1) for part in (products, rest) for r, p in enumerate(part)]
    terms = kernel_call(
        terms_kernel, "terms", [shape(block_rows, 2 * kv_width)] * n_blocks, [VMEM] * 5
    )(probs, dscores, q, *incoming)
    if direct:
        sent = sorted(zip(partners, terms[1:]), key=lambda pair: -pair[0])
        all_terms = [terms[0]] + [swapped(x, "seq", r) for r, x in sent]
    else:
        all_terms = [lax.psum_scatter(terms[0], "seq", scatter_dimension=0, tiled=True)]

    own = kernel_call(
        functools.partial(own_kernel, n_head),
        "own",
        shape(feats, rows, dtype=jnp.float32),
        [VMEM, HBM],
        [pltpu.VMEM((feats, width), low), pltpu.SemaphoreType.DMA(())],
    )(grad_query, in_hbm(proj_query))
    grad_key, grad_value = kernel_call(
        term_sum_kernel, "term_sum", [shape(1, held, kv_width)] * 2, [VMEM] * len(all_terms)
    )(*all_terms)
    grad_input = []
    for start, part in ((0, arrived[:n_other]), (first, arrived[n_other:])):
        grad_input = [
            pl.pallas_call(
                functools.partial(input_sum_kernel, n_other, start),
                out_shape=shape(1, feats, rows),
                in_specs=[VMEM] * (1 + n_other) + [HBM] * len(grad_input),
                out_specs=HBM,
                scratch_shapes=[pltpu.VMEM(part[0].shape, low), pltpu.SemaphoreType.DMA(())],
                input_output_aliases={1 + n_other: 0} if grad_input else {},
                compiler_params=pltpu.CompilerParams(vmem_limit_bytes=VMEM_LIMIT),
                name="input_sum",
            )(own, *part, *grad_input)
        ]
    grad_input = grad_input[0]
    return (grad_input, grad_key, grad_value)


def solution(mesh):
    in_specs = (
        P("section", "seq", "head"),
        P("section", "seq", "head"),
        P("section", "seq", "head"),
        P("section", "seq", "head"),
        P("section", None, "head"),
        P(),
        P(),
    )
    out_specs = (
        P("section", "head", "seq"),
        P("section", "seq", "head"),
        P("section", "seq", "head"),
    )
    return jax.shard_map(
        on_device, mesh=mesh, in_specs=in_specs, out_specs=out_specs, check_vma=False
    )
```

```python
import functools
import math

import jax
import jax.numpy as jnp
from jax import lax
from jax.experimental import pallas as pl
from jax.experimental.pallas import tpu as pltpu
from jax.sharding import PartitionSpec as P

HD = 128
MOST_PARTNERS = 4
VMEM_LIMIT = 40 * 1024 * 1024

query_scale = 168.0 ** (-0.5)
exp2_scale = query_scale * math.log2(math.e)


def shifted(block, axis, distance):
    devices = range(lax.axis_size(axis))
    route = [((i - distance) % len(devices), i) for i in devices]
    return lax.ppermute(block, axis, route)


def swapped(block, axis, distance):
    return lax.ppermute(block, axis, [(i, i ^ distance) for i in range(lax.axis_size(axis))])


def dot(left, right, left_dim, right_dim):
    return lax.dot_general(
        left, right, (((left_dim,), (right_dim,)), ((), ())), preferred_element_type=jnp.float32
    )


def in_hbm(x):
    return pltpu.with_memory_space_constraint(x, pltpu.HBM)


def fetch_rows(n_head, shifts, w_ref, outs, sems):
    feats = w_ref.shape[1] // n_head
    head = lax.axis_index("head")
    copies = []
    for i, (shift, out) in enumerate(zip(shifts, outs)):
        start = pl.multiple_of(lax.rem(head + shift, n_head) * feats, 16)
        copies.append(
            pltpu.make_async_copy(w_ref.at[0, pl.ds(start, feats), :], out, sems.at[i])
        )
    for copy in copies:
        copy.start()
    for copy in copies:
        copy.wait()


def second_core():
    return lax.rem(lax.axis_index("section"), 2) == 1


def join_kernel(n_copies, n_head, key_ref, value_ref, grad_ref, w_ref, *refs):
    outs, (grad_low, grad_high), refs = refs[:n_copies], refs[n_copies : n_copies + 2], refs[n_copies + 2 :]
    *early, sems, w_sems = refs
    width, rows = key_ref.shape[2], grad_low.shape[0]
    pairs = [
        (key_ref.at[0], outs[0].at[:, :width]),
        (value_ref.at[0], outs[0].at[:, width:]),
        (grad_ref.at[0, :rows, :], grad_low),
        (grad_ref.at[0, rows:, :], grad_high),
    ]
    copies = [pltpu.make_async_copy(a, b, sems.at[i]) for i, (a, b) in enumerate(pairs)]
    for copy in copies:
        copy.start()
    for copy in copies[:2]:
        copy.wait()
    for out in outs[1:]:
        out[...] = outs[0][...]

    @pl.when(jnp.logical_not(second_core()))
    def _():
        fetch_rows(n_head, range(1, n_head), w_ref, early, w_sems)

    for copy in copies[2:]:
        copy.wait()


def stage_kernel(n_head, span_ref, prefix_ref, q_ref, w_ref, limit_out, q_out, *refs):
    *late, span, prefix, sems, w_sems = refs
    pairs = [(span_ref, span), (prefix_ref, prefix), (q_ref.at[0], q_out)]
    copies = [pltpu.make_async_copy(a, b, sems.at[i]) for i, (a, b) in enumerate(pairs)]
    for copy in copies:
        copy.start()

    @pl.when(second_core())
    def _():
        fetch_rows(n_head, range(1, n_head), w_ref, late, w_sems)

    for copy in copies:
        copy.wait()
    live = prefix[span[lax.axis_index("section")]]
    limit_out[...] = jnp.full(limit_out.shape, live, jnp.int32)


def products(early, late, grad_ref, part_refs, start):
    for held, taken in ((early, jnp.logical_not(second_core())), (late, second_core())):

        @pl.when(taken)
        def _():
            for w_ref, part_ref in zip(held, part_refs):
                block = w_ref[start : start + part_ref.shape[0], :]
                part_ref[...] = dot(block, grad_ref[...], 1, 0).astype(jnp.bfloat16)


def pair_of(refs, g):
    cols = [slice((2 * g + i) * HD, (2 * g + i + 1) * HD) for i in range(2)]
    return jnp.concatenate([ref[:, c] for c in cols for ref in refs], axis=0)


def cols_of(g, start=0):
    return slice(start + g * HD, start + (g + 1) * HD)


def attention_kernel(partners, n_other, limit_ref, q_ref, *refs):
    n_blocks = 1 + len(partners)
    kv_refs = refs[:n_blocks]
    d_low, d_high, *refs = refs[n_blocks:]
    early, late = refs[:n_other], refs[n_other : 2 * n_other]
    grad_ref, probs_ref, dscores_ref, *part_refs = refs[2 * n_other :]

    held, both = kv_refs[0].shape
    width = both // 2
    seq = lax.axis_index("seq")
    spots = []
    for r in [0, *partners]:
        first = jnp.bitwise_xor(seq, r) * held if partners else 0
        spots.append(first + lax.broadcasted_iota(jnp.int32, (held, 1), 0))
    alive = jnp.concatenate(spots, axis=0) < limit_ref[0:1, 0:1]

    rows = q_ref.shape[0]
    groups = range(width // HD)
    keys = [jnp.concatenate([ref[:, cols_of(g)] for ref in kv_refs], axis=0) for g in groups]
    scores = [dot(keys[g], pair_of((q_ref,), g), 1, 1) for g in groups]
    dprobs = []
    for g in groups:
        value = jnp.concatenate([ref[:, cols_of(g, width)] for ref in kv_refs], axis=0)
        dprobs.append(dot(value, pair_of((d_low, d_high), g), 1, 1))
    for g in groups:
        masked = jnp.where(alive, scores[g], jnp.float32(-1e30))
        top = jnp.max(masked, axis=0, keepdims=True)
        probs = jnp.exp2((masked - top) * exp2_scale)
        probs = probs * (1.0 / jnp.sum(probs, axis=0, keepdims=True))
        probs_low = probs.astype(jnp.bfloat16)
        delta = jnp.sum(probs_low.astype(jnp.float32) * dprobs[g], axis=0, keepdims=True)
        probs_ref[g] = probs_low
        dscores_ref[g] = (probs * (dprobs[g] - delta)).astype(jnp.bfloat16)
    for g in groups:
        grad_q = (query_scale * dot(keys[g], dscores_ref[g], 0, 0)).astype(jnp.bfloat16)
        for i in range(2):
            spot = (2 * g + i) * HD
            grad_ref[spot : spot + HD, :] = grad_q[:, i * rows : (i + 1) * rows]

    products(early, late, grad_ref, part_refs, 0)


def rest_kernel(n_other, start, grad_ref, *refs):
    early, late = refs[:n_other], refs[n_other : 2 * n_other]
    products(early, late, grad_ref, refs[2 * n_other :], start)


def terms_kernel(probs_ref, dscores_ref, q_ref, d_low, d_high, *term_refs):
    held, both = term_refs[0].shape
    width = both // 2
    for g in range(width // HD):
        grad_k = (query_scale * dot(dscores_ref[g], pair_of((q_ref,), g), 1, 0)).astype(jnp.bfloat16)
        grad_v = dot(probs_ref[g], pair_of((d_low, d_high), g), 1, 0).astype(jnp.bfloat16)
        for r, ref in enumerate(term_refs):
            block = slice(r * held, (r + 1) * held)
            ref[:, g * HD : (g + 1) * HD] = grad_k[block]
            ref[:, width + g * HD : width + (g + 1) * HD] = grad_v[block]


def own_kernel(n_head, grad_ref, w_ref, out_ref, w_held, sem):
    feats = out_ref.shape[0]
    start = pl.multiple_of(lax.axis_index("head") * feats, 16)
    copy = pltpu.make_async_copy(w_ref.at[0, pl.ds(start, feats), :], w_held, sem)
    copy.start()
    copy.wait()
    out_ref[...] = dot(w_held[...], grad_ref[...], 1, 0)


def input_sum_kernel(n_other, start, own_ref, *refs):
    arrived = refs[:n_other]
    *_, out_ref, held, sem = refs
    at = slice(start, start + held.shape[0])
    total = own_ref[at, :]
    for ref in arrived:
        total = total + ref[...].astype(jnp.float32)
    held[...] = total.astype(jnp.bfloat16)
    copy = pltpu.make_async_copy(held, out_ref.at[0, at, :], sem)
    copy.start()
    copy.wait()


def term_sum_kernel(*refs):
    *terms, key_ref, value_ref = refs
    total = terms[0][...].astype(jnp.float32)
    for ref in terms[1:]:
        total = total + ref[...].astype(jnp.float32)
    low = total.astype(jnp.bfloat16)
    half = low.shape[1] // 2
    key_ref[0] = low[:, :half]
    value_ref[0] = low[:, half:]


VMEM = pl.BlockSpec(memory_space=pltpu.VMEM)
HBM = pl.BlockSpec(memory_space=pltpu.HBM)


def kernel_call(body, name, out_shape, in_specs, scratch=(), limit=VMEM_LIMIT):
    return pl.pallas_call(
        body,
        out_shape=out_shape,
        in_specs=in_specs,
        out_specs=jax.tree.map(lambda _: VMEM, out_shape),
        scratch_shapes=list(scratch),
        compiler_params=pltpu.CompilerParams(vmem_limit_bytes=limit),
        name=name,
    )


def on_device(queries, grad_out, keys, values, proj_query, section_span, span_prefix):
    n_seq, n_head = lax.axis_size("seq"), lax.axis_size("head")
    n_other = n_head - 1
    direct = n_seq <= MOST_PARTNERS and n_seq & (n_seq - 1) == 0
    low = jnp.bfloat16
    _, held, kv_width = keys.shape
    _, rows, width = queries.shape
    feats = proj_query.shape[1] // n_head

    def shape(*dims, dtype=low):
        return jax.ShapeDtypeStruct(dims, dtype)

    first = feats // 16 * 17 // 32 * 16
    partners = list(range(1, n_seq)) if direct else []
    n_copies = 1 + len(partners)
    weight_rows = in_hbm(proj_query)
    out = kernel_call(
        functools.partial(join_kernel, n_copies, n_head),
        "join",
        [shape(held, 2 * kv_width)] * n_copies
        + [shape(rows // 2, width)] * 2
        + [shape(feats, width)] * n_other,
        [HBM] * 4,
        [pltpu.SemaphoreType.DMA((4,)), pltpu.SemaphoreType.DMA((max(n_other, 1),))],
    )(in_hbm(keys), in_hbm(values), in_hbm(grad_out), weight_rows)
    joined, (grad_low, grad_high, *early) = list(out[:n_copies]), out[n_copies:]
    if direct:
        blocks = joined[-1:] + [swapped(x, "seq", r) for x, r in zip(joined, partners)]
    else:
        blocks = [lax.all_gather(joined[0], "seq", axis=0, tiled=True)]
    n_blocks, block_rows = len(blocks), blocks[0].shape[0]
    incoming = [shifted(part, "section", -1) for part in (grad_low, grad_high)]

    limit, q, *late = kernel_call(
        functools.partial(stage_kernel, n_head),
        "stage",
        [shape(8, HD, dtype=jnp.int32), shape(rows, width)] + [shape(feats, width)] * n_other,
        [HBM] * 4,
        [
            pltpu.SMEM(section_span.shape, jnp.int32),
            pltpu.SMEM(span_prefix.shape, jnp.int32),
            pltpu.SemaphoreType.DMA((3,)),
            pltpu.SemaphoreType.DMA((max(n_other, 1),)),
        ],
    )(*[in_hbm(x) for x in (section_span, span_prefix, queries)], weight_rows)

    prefix = n_blocks * block_rows
    weights = shape(kv_width // HD, prefix, 2 * rows)
    grad_query, probs, dscores, *products = kernel_call(
        functools.partial(attention_kernel, partners, n_other),
        "attention",
        [shape(width, rows), weights, weights] + [shape(first, rows)] * n_other,
        [VMEM] * (4 + n_blocks + 2 * n_other),
    )(limit, q, *blocks, *incoming, *early, *late)
    rest = kernel_call(
        functools.partial(rest_kernel, n_other, first),
        "rest",
        [shape(feats - first, rows)] * n_other,
        [VMEM] * (1 + 2 * n_other),
    )(grad_query, *early, *late)
    arrived = [shifted(p, "head", r + 1) for part in (products, rest) for r, p in enumerate(part)]
    terms = kernel_call(
        terms_kernel, "terms", [shape(block_rows, 2 * kv_width)] * n_blocks, [VMEM] * 5
    )(probs, dscores, q, *incoming)
    if direct:
        sent = sorted(zip(partners, terms[1:]), key=lambda pair: -pair[0])
        all_terms = [terms[0]] + [swapped(x, "seq", r) for r, x in sent]
    else:
        all_terms = [lax.psum_scatter(terms[0], "seq", scatter_dimension=0, tiled=True)]

    own = kernel_call(
        functools.partial(own_kernel, n_head),
        "own",
        shape(feats, rows, dtype=jnp.float32),
        [VMEM, HBM],
        [pltpu.VMEM((feats, width), low), pltpu.SemaphoreType.DMA(())],
    )(grad_query, in_hbm(proj_query))
    grad_key, grad_value = kernel_call(
        term_sum_kernel, "term_sum", [shape(1, held, kv_width)] * 2, [VMEM] * len(all_terms)
    )(*all_terms)
    grad_input = []
    for start, part in ((0, arrived[:n_other]), (first, arrived[n_other:])):
        grad_input = [
            pl.pallas_call(
                functools.partial(input_sum_kernel, n_other, start),
                out_shape=shape(1, feats, rows),
                in_specs=[VMEM] * (1 + n_other) + [HBM] * len(grad_input),
                out_specs=HBM,
                scratch_shapes=[pltpu.VMEM(part[0].shape, low), pltpu.SemaphoreType.DMA(())],
                input_output_aliases={1 + n_other: 0} if grad_input else {},
                compiler_params=pltpu.CompilerParams(vmem_limit_bytes=VMEM_LIMIT),
                name="input_sum",
            )(own, *part, *grad_input)
        ]
    grad_input = grad_input[0]
    return (grad_input, grad_key, grad_value)


def solution(mesh):
    in_specs = (
        P("section", "seq", "head"),
        P("section", "seq", "head"),
        P("section", "seq", "head"),
        P("section", "seq", "head"),
        P("section", None, "head"),
        P(),
        P(),
    )
    out_specs = (
        P("section", "head", "seq"),
        P("section", "seq", "head"),
        P("section", "seq", "head"),
    )
    return jax.shard_map(
        on_device, mesh=mesh, in_specs=in_specs, out_specs=out_specs, check_vma=False
    )
```

```python
import functools
import math

import jax
import jax.numpy as jnp
from jax import lax
from jax.experimental import pallas as pl
from jax.experimental.pallas import tpu as pltpu
from jax.sharding import PartitionSpec as P

HD = 128
MOST_PARTNERS = 4
STEPS_OF_FOUR = ((1, 3, 0, 2), (3, 2, 1, 0), (2, 0, 3, 1))
VMEM_LIMIT = 40 * 1024 * 1024

query_scale = 168.0 ** (-0.5)
exp2_scale = query_scale * math.log2(math.e)


def shifted(block, axis, distance):
    devices = range(lax.axis_size(axis))
    route = [((i - distance) % len(devices), i) for i in devices]
    return lax.ppermute(block, axis, route)


def seq_steps(n):
    if n == len(STEPS_OF_FOUR) + 1:
        return STEPS_OF_FOUR
    return [[(i + r) % n for i in range(n)] for r in range(1, n)]


def sent(block, step):
    return lax.ppermute(block, "seq", list(enumerate(step)))


def sent_back(block, step):
    return lax.ppermute(block, "seq", [(to, i) for i, to in enumerate(step)])


def dot(left, right, left_dim, right_dim):
    return lax.dot_general(
        left, right, (((left_dim,), (right_dim,)), ((), ())), preferred_element_type=jnp.float32
    )


def in_hbm(x):
    return pltpu.with_memory_space_constraint(x, pltpu.HBM)


def join_kernel(n_copies, key_ref, value_ref, grad_ref, *refs):
    *outs, grad_low, grad_high, sems = refs
    width, rows = key_ref.shape[2], grad_low.shape[0]
    pairs = [
        (key_ref.at[0], outs[0].at[:, :width]),
        (value_ref.at[0], outs[0].at[:, width:]),
        (grad_ref.at[0, :rows, :], grad_low),
        (grad_ref.at[0, rows:, :], grad_high),
    ]
    copies = [pltpu.make_async_copy(a, b, sems.at[i]) for i, (a, b) in enumerate(pairs)]
    for copy in copies:
        copy.start()
    for copy in copies[:2]:
        copy.wait()
    for out in outs[1:]:
        out[...] = outs[0][...]
    for copy in copies[2:]:
        copy.wait()


def stage_kernel(n_head, span_ref, prefix_ref, q_ref, w_ref, limit_out, q_out, *refs):
    *other_outs, span, prefix, sems, small_sems = refs
    feats = w_ref.shape[1] // n_head
    head = lax.axis_index("head")
    copies = []
    for r, out in enumerate(other_outs):
        start = pl.multiple_of(lax.rem(head + r + 1, n_head) * feats, 16)
        copies.append((w_ref.at[0, pl.ds(start, feats), :], out))
    copies.append((q_ref.at[0], q_out))
    copies = [pltpu.make_async_copy(a, b, sems.at[i]) for i, (a, b) in enumerate(copies)]
    small = [
        pltpu.make_async_copy(a, b, small_sems.at[i])
        for i, (a, b) in enumerate([(span_ref, span), (prefix_ref, prefix)])
    ]
    for copy in small + copies:
        copy.start()
    for copy in small:
        copy.wait()
    live = prefix[span[lax.axis_index("section")]]
    limit_out[...] = jnp.full(limit_out.shape, live, jnp.int32)
    for copy in copies:
        copy.wait()


def pair_of(refs, g):
    cols = [slice((2 * g + i) * HD, (2 * g + i + 1) * HD) for i in range(2)]
    return jnp.concatenate([ref[:, c] for c in cols for ref in refs], axis=0)


def cols_of(g, start=0):
    return slice(start + g * HD, start + (g + 1) * HD)


def attention_kernel(partners, n_other, limit_ref, q_ref, *refs):
    most = 1 + len(partners[:1])
    kv_refs, (d_low, d_high), refs = refs[:most], refs[most : most + 2], refs[most + 2 :]
    kv_refs, refs = kv_refs + refs[: len(partners[1:])], refs[len(partners[1:]) :]
    w_refs = refs[:n_other]
    grad_ref, probs_ref, dscores_ref, *part_refs = refs[n_other:]

    held, both = kv_refs[0].shape
    width = both // 2
    seq = lax.axis_index("seq")
    owners = [seq if partners else 0]
    for step in partners:
        owners.append(sum(jnp.where(seq == to, i, 0) for i, to in enumerate(step)))
    spots = [i * held + lax.broadcasted_iota(jnp.int32, (held, 1), 0) for i in owners]
    alive = jnp.concatenate(spots, axis=0) < limit_ref[0:1, 0:1]

    rows = q_ref.shape[0]
    groups = range(width // HD)
    keys = [jnp.concatenate([ref[:, cols_of(g)] for ref in kv_refs], axis=0) for g in groups]
    scores = [dot(keys[g], pair_of((q_ref,), g), 1, 1) for g in groups]
    dprobs = []
    for g in groups:
        value = jnp.concatenate([ref[:, cols_of(g, width)] for ref in kv_refs], axis=0)
        dprobs.append(dot(value, pair_of((d_low, d_high), g), 1, 1))
    for g in groups:
        masked = jnp.where(alive, scores[g], jnp.float32(-1e30))
        top = jnp.max(masked, axis=0, keepdims=True)
        probs = jnp.exp2((masked - top) * exp2_scale)
        probs = probs * (1.0 / jnp.sum(probs, axis=0, keepdims=True))
        probs_low = probs.astype(jnp.bfloat16)
        delta = jnp.sum(probs_low.astype(jnp.float32) * dprobs[g], axis=0, keepdims=True)
        probs_ref[g] = probs_low
        dscores_ref[g] = (probs * (dprobs[g] - delta)).astype(jnp.bfloat16)
    for g in groups:
        grad_q = (query_scale * dot(keys[g], dscores_ref[g], 0, 0)).astype(jnp.bfloat16)
        for i in range(2):
            spot = (2 * g + i) * HD
            grad_ref[spot : spot + HD, :] = grad_q[:, i * rows : (i + 1) * rows]

    for w_ref, part_ref in zip(w_refs, part_refs):
        block = w_ref[: part_ref.shape[0], :]
        part_ref[...] = dot(block, grad_ref[...], 1, 0).astype(jnp.bfloat16)


def rest_kernel(n_other, grad_ref, *refs):
    for w_ref, part_ref in zip(refs[:n_other], refs[n_other:]):
        block = w_ref[w_ref.shape[0] - part_ref.shape[0] :, :]
        part_ref[...] = dot(block, grad_ref[...], 1, 0).astype(jnp.bfloat16)


def terms_kernel(probs_ref, dscores_ref, q_ref, d_low, d_high, *term_refs):
    held, both = term_refs[0].shape
    width = both // 2
    for g in range(width // HD):
        grad_k = (query_scale * dot(dscores_ref[g], pair_of((q_ref,), g), 1, 0)).astype(jnp.bfloat16)
        grad_v = dot(probs_ref[g], pair_of((d_low, d_high), g), 1, 0).astype(jnp.bfloat16)
        for r, ref in enumerate(term_refs):
            block = slice(r * held, (r + 1) * held)
            ref[:, g * HD : (g + 1) * HD] = grad_k[block]
            ref[:, width + g * HD : width + (g + 1) * HD] = grad_v[block]


def own_kernel(n_head, grad_ref, w_ref, out_ref, w_held, sem):
    feats = out_ref.shape[0]
    start = pl.multiple_of(lax.axis_index("head") * feats, 16)
    copy = pltpu.make_async_copy(w_ref.at[0, pl.ds(start, feats), :], w_held, sem)
    copy.start()
    copy.wait()
    out_ref[...] = dot(w_held[...], grad_ref[...], 1, 0)


def input_sum_kernel(n_other, start, own_ref, *refs):
    arrived = refs[:n_other]
    *_, out_ref, held, sem = refs
    at = slice(start, start + held.shape[0])
    total = own_ref[at, :]
    for ref in arrived:
        total = total + ref[...].astype(jnp.float32)
    held[...] = total.astype(jnp.bfloat16)
    copy = pltpu.make_async_copy(held, out_ref.at[0, at, :], sem)
    copy.start()
    copy.wait()


def term_sum_kernel(*refs):
    *terms, key_ref, value_ref = refs
    total = terms[0][...].astype(jnp.float32)
    for ref in terms[1:]:
        total = total + ref[...].astype(jnp.float32)
    low = total.astype(jnp.bfloat16)
    half = low.shape[1] // 2
    key_ref[0] = low[:, :half]
    value_ref[0] = low[:, half:]


VMEM = pl.BlockSpec(memory_space=pltpu.VMEM)
HBM = pl.BlockSpec(memory_space=pltpu.HBM)


def kernel_call(body, name, out_shape, in_specs, scratch=(), limit=VMEM_LIMIT):
    return pl.pallas_call(
        body,
        out_shape=out_shape,
        in_specs=in_specs,
        out_specs=jax.tree.map(lambda _: VMEM, out_shape),
        scratch_shapes=list(scratch),
        compiler_params=pltpu.CompilerParams(vmem_limit_bytes=limit),
        name=name,
    )


def on_device(queries, grad_out, keys, values, proj_query, section_span, span_prefix):
    n_seq, n_head = lax.axis_size("seq"), lax.axis_size("head")
    n_other = n_head - 1
    direct = n_seq <= MOST_PARTNERS
    low = jnp.bfloat16
    _, held, kv_width = keys.shape
    _, rows, width = queries.shape
    feats = proj_query.shape[1] // n_head

    def shape(*dims, dtype=low):
        return jax.ShapeDtypeStruct(dims, dtype)

    first = feats // 16 * 17 // 32 * 16
    partners = seq_steps(n_seq) if direct else []
    n_copies = 1 + len(partners)
    *joined, grad_low, grad_high = kernel_call(
        functools.partial(join_kernel, n_copies),
        "join",
        [shape(held, 2 * kv_width)] * n_copies + [shape(rows // 2, width)] * 2,
        [HBM] * 3,
        [pltpu.SemaphoreType.DMA((4,))],
    )(*[in_hbm(x) for x in (keys, values, grad_out)])
    if direct:
        blocks = joined[-1:] + [sent(x, step) for x, step in zip(joined, partners[:1])]
    else:
        blocks = [lax.all_gather(joined[0], "seq", axis=0, tiled=True)]
    incoming = [shifted(part, "section", -1) for part in (grad_low, grad_high)]
    last = [sent(x, step) for x, step in zip(joined[1:], partners[1:])]
    n_blocks, block_rows = len(blocks) + len(last), blocks[0].shape[0]

    limit, q, *w_other = kernel_call(
        functools.partial(stage_kernel, n_head),
        "stage",
        [shape(8, HD, dtype=jnp.int32), shape(rows, width)] + [shape(feats, width)] * n_other,
        [HBM] * 4,
        [
            pltpu.SMEM(section_span.shape, jnp.int32),
            pltpu.SMEM(span_prefix.shape, jnp.int32),
            pltpu.SemaphoreType.DMA((1 + n_other,)),
            pltpu.SemaphoreType.DMA((2,)),
        ],
    )(*[in_hbm(x) for x in (section_span, span_prefix, queries, proj_query)])

    prefix = n_blocks * block_rows
    weights = shape(kv_width // HD, prefix, 2 * rows)
    grad_query, probs, dscores, *products = kernel_call(
        functools.partial(attention_kernel, partners, n_other),
        "attention",
        [shape(width, rows), weights, weights] + [shape(first, rows)] * n_other,
        [VMEM] * (4 + n_blocks + n_other),
    )(limit, q, *blocks, *incoming, *last, *w_other)
    rest = kernel_call(
        functools.partial(rest_kernel, n_other),
        "rest",
        [shape(feats - first, rows)] * n_other,
        [VMEM] * (1 + n_other),
    )(grad_query, *w_other)
    arrived = [shifted(p, "head", r + 1) for part in (products, rest) for r, p in enumerate(part)]
    terms = kernel_call(
        terms_kernel, "terms", [shape(block_rows, 2 * kv_width)] * n_blocks, [VMEM] * 5
    )(probs, dscores, q, *incoming)
    if direct:
        all_terms = [terms[0]] + [sent_back(x, step) for x, step in zip(terms[1:], partners)]
    else:
        all_terms = [lax.psum_scatter(terms[0], "seq", scatter_dimension=0, tiled=True)]

    own = kernel_call(
        functools.partial(own_kernel, n_head),
        "own",
        shape(feats, rows, dtype=jnp.float32),
        [VMEM, HBM],
        [pltpu.VMEM((feats, width), low), pltpu.SemaphoreType.DMA(())],
    )(grad_query, in_hbm(proj_query))
    grad_key, grad_value = kernel_call(
        term_sum_kernel, "term_sum", [shape(1, held, kv_width)] * 2, [VMEM] * len(all_terms)
    )(*all_terms)
    grad_input = []
    for start, part in ((0, arrived[:n_other]), (first, arrived[n_other:])):
        grad_input = [
            pl.pallas_call(
                functools.partial(input_sum_kernel, n_other, start),
                out_shape=shape(1, feats, rows),
                in_specs=[VMEM] * (1 + n_other) + [HBM] * len(grad_input),
                out_specs=HBM,
                scratch_shapes=[pltpu.VMEM(part[0].shape, low), pltpu.SemaphoreType.DMA(())],
                input_output_aliases={1 + n_other: 0} if grad_input else {},
                compiler_params=pltpu.CompilerParams(vmem_limit_bytes=VMEM_LIMIT),
                name="input_sum",
            )(own, *part, *grad_input)
        ]
    grad_input = grad_input[0]
    return (grad_input, grad_key, grad_value)


def solution(mesh):
    in_specs = (
        P("section", "seq", "head"),
        P("section", "seq", "head"),
        P("section", "seq", "head"),
        P("section", "seq", "head"),
        P("section", None, "head"),
        P(),
        P(),
    )
    out_specs = (
        P("section", "head", "seq"),
        P("section", "seq", "head"),
        P("section", "seq", "head"),
    )
    return jax.shard_map(
        on_device, mesh=mesh, in_specs=in_specs, out_specs=out_specs, check_vma=False
    )
```

```python
import functools
import math

import jax
import jax.numpy as jnp
from jax import lax
from jax.experimental import pallas as pl
from jax.experimental.pallas import tpu as pltpu
from jax.sharding import PartitionSpec as P

HD = 128
MOST_PARTNERS = 4
VMEM_LIMIT = 40 * 1024 * 1024

query_scale = 168.0 ** (-0.5)
exp2_scale = query_scale * math.log2(math.e)


def shifted(block, axis, distance):
    devices = range(lax.axis_size(axis))
    route = [((i - distance) % len(devices), i) for i in devices]
    return lax.ppermute(block, axis, route)


def swapped(block, axis, distance):
    return lax.ppermute(block, axis, [(i, i ^ distance) for i in range(lax.axis_size(axis))])


def dot(left, right, left_dim, right_dim):
    return lax.dot_general(
        left, right, (((left_dim,), (right_dim,)), ((), ())), preferred_element_type=jnp.float32
    )


def in_hbm(x):
    return pltpu.with_memory_space_constraint(x, pltpu.HBM)


def join_kernel(n_copies, key_ref, value_ref, grad_ref, *refs):
    *outs, grad_low, grad_high, sems = refs
    width, rows = key_ref.shape[2], grad_low.shape[0]
    pairs = [
        (key_ref.at[0], outs[0].at[:, :width]),
        (value_ref.at[0], outs[0].at[:, width:]),
        (grad_ref.at[0, :rows, :], grad_low),
        (grad_ref.at[0, rows:, :], grad_high),
    ]
    copies = [pltpu.make_async_copy(a, b, sems.at[i]) for i, (a, b) in enumerate(pairs)]
    for copy in copies:
        copy.start()
    for copy in copies[:2]:
        copy.wait()
    for out in outs[1:]:
        out[...] = outs[0][...]
    for copy in copies[2:]:
        copy.wait()


def stage_kernel(n_head, span_ref, prefix_ref, q_ref, w_ref, limit_out, q_out, *refs):
    *other_outs, span, prefix, sems, small_sems = refs
    feats = w_ref.shape[1] // n_head
    head = lax.axis_index("head")
    copies = []
    for r, out in enumerate(other_outs):
        start = pl.multiple_of(lax.rem(head + r + 1, n_head) * feats, 16)
        copies.append((w_ref.at[0, pl.ds(start, feats), :], out))
    copies.append((q_ref.at[0], q_out))
    copies = [pltpu.make_async_copy(a, b, sems.at[i]) for i, (a, b) in enumerate(copies)]
    small = [
        pltpu.make_async_copy(a, b, small_sems.at[i])
        for i, (a, b) in enumerate([(span_ref, span), (prefix_ref, prefix)])
    ]
    for copy in small + copies:
        copy.start()
    for copy in small:
        copy.wait()
    live = prefix[span[lax.axis_index("section")]]
    limit_out[...] = jnp.full(limit_out.shape, live, jnp.int32)
    for copy in copies:
        copy.wait()


def pair_of(refs, g):
    cols = [slice((2 * g + i) * HD, (2 * g + i + 1) * HD) for i in range(2)]
    return jnp.concatenate([ref[:, c] for c in cols for ref in refs], axis=0)


def cols_of(g, start=0):
    return slice(start + g * HD, start + (g + 1) * HD)


def attention_kernel(partners, n_other, limit_ref, q_ref, *refs):
    n_blocks = 1 + len(partners)
    kv_refs = refs[:n_blocks]
    d_low, d_high, *refs = refs[n_blocks:]
    w_refs = refs[:n_other]
    grad_ref, probs_ref, dscores_ref, *part_refs = refs[n_other:]

    held, both = kv_refs[0].shape
    width = both // 2
    seq = lax.axis_index("seq")
    spots = []
    for r in [0, *partners]:
        first = jnp.bitwise_xor(seq, r) * held if partners else 0
        spots.append(first + lax.broadcasted_iota(jnp.int32, (held, 1), 0))
    alive = jnp.concatenate(spots, axis=0) < limit_ref[0:1, 0:1]

    rows = q_ref.shape[0]
    groups = range(width // HD)
    keys = [jnp.concatenate([ref[:, cols_of(g)] for ref in kv_refs], axis=0) for g in groups]
    scores = [dot(keys[g], pair_of((q_ref,), g), 1, 1) for g in groups]
    dprobs = []
    for g in groups:
        value = jnp.concatenate([ref[:, cols_of(g, width)] for ref in kv_refs], axis=0)
        dprobs.append(dot(value, pair_of((d_low, d_high), g), 1, 1))
    for g in groups:
        masked = jnp.where(alive, scores[g], jnp.float32(-1e30))
        top = jnp.max(masked, axis=0, keepdims=True)
        probs = jnp.exp2((masked - top) * exp2_scale)
        probs = probs * (1.0 / jnp.sum(probs, axis=0, keepdims=True))
        probs_low = probs.astype(jnp.bfloat16)
        delta = jnp.sum(probs_low.astype(jnp.float32) * dprobs[g], axis=0, keepdims=True)
        probs_ref[g] = probs_low
        dscores_ref[g] = (probs * (dprobs[g] - delta)).astype(jnp.bfloat16)
    for g in groups:
        grad_q = (query_scale * dot(keys[g], dscores_ref[g], 0, 0)).astype(jnp.bfloat16)
        for i in range(2):
            spot = (2 * g + i) * HD
            grad_ref[spot : spot + HD, :] = grad_q[:, i * rows : (i + 1) * rows]

    for w_ref, part_ref in zip(w_refs, part_refs):
        block = w_ref[: part_ref.shape[0], :]
        part_ref[...] = dot(block, grad_ref[...], 1, 0).astype(jnp.bfloat16)


def rest_kernel(n_other, grad_ref, *refs):
    for w_ref, part_ref in zip(refs[:n_other], refs[n_other:]):
        block = w_ref[w_ref.shape[0] - part_ref.shape[0] :, :]
        part_ref[...] = dot(block, grad_ref[...], 1, 0).astype(jnp.bfloat16)


def terms_kernel(probs_ref, dscores_ref, q_ref, d_low, d_high, *term_refs):
    held, both = term_refs[0].shape
    width = both // 2
    for g in range(width // HD):
        grad_k = (query_scale * dot(dscores_ref[g], pair_of((q_ref,), g), 1, 0)).astype(jnp.bfloat16)
        grad_v = dot(probs_ref[g], pair_of((d_low, d_high), g), 1, 0).astype(jnp.bfloat16)
        for r, ref in enumerate(term_refs):
            block = slice(r * held, (r + 1) * held)
            ref[:, g * HD : (g + 1) * HD] = grad_k[block]
            ref[:, width + g * HD : width + (g + 1) * HD] = grad_v[block]


def own_kernel(n_head, grad_ref, w_ref, out_ref, w_held, sem):
    feats = out_ref.shape[0]
    start = pl.multiple_of(lax.axis_index("head") * feats, 16)
    copy = pltpu.make_async_copy(w_ref.at[0, pl.ds(start, feats), :], w_held, sem)
    copy.start()
    copy.wait()
    out_ref[...] = dot(w_held[...], grad_ref[...], 1, 0)


def input_sum_kernel(n_other, start, own_ref, *refs):
    arrived = refs[:n_other]
    *_, out_ref, held, sems = refs
    count = held.shape[0]
    middle = count // 32 * 16
    copies = []
    for i, (low, high) in enumerate(((0, middle), (middle, count))):
        at = slice(start + low, start + high)
        total = own_ref[at, :]
        for ref in arrived:
            total = total + ref[low:high, :].astype(jnp.float32)
        held[low:high, :] = total.astype(jnp.bfloat16)
        copy = pltpu.make_async_copy(held.at[low:high, :], out_ref.at[0, at, :], sems.at[i])
        copy.start()
        copies.append(copy)
    for copy in copies:
        copy.wait()


def term_sum_kernel(*refs):
    *terms, key_ref, value_ref = refs
    total = terms[0][...].astype(jnp.float32)
    for ref in terms[1:]:
        total = total + ref[...].astype(jnp.float32)
    low = total.astype(jnp.bfloat16)
    half = low.shape[1] // 2
    key_ref[0] = low[:, :half]
    value_ref[0] = low[:, half:]


VMEM = pl.BlockSpec(memory_space=pltpu.VMEM)
HBM = pl.BlockSpec(memory_space=pltpu.HBM)


def kernel_call(body, name, out_shape, in_specs, scratch=(), limit=VMEM_LIMIT):
    return pl.pallas_call(
        body,
        out_shape=out_shape,
        in_specs=in_specs,
        out_specs=jax.tree.map(lambda _: VMEM, out_shape),
        scratch_shapes=list(scratch),
        compiler_params=pltpu.CompilerParams(vmem_limit_bytes=limit),
        name=name,
    )


def on_device(queries, grad_out, keys, values, proj_query, section_span, span_prefix):
    n_seq, n_head = lax.axis_size("seq"), lax.axis_size("head")
    n_other = n_head - 1
    direct = n_seq <= MOST_PARTNERS and n_seq & (n_seq - 1) == 0
    low = jnp.bfloat16
    _, held, kv_width = keys.shape
    _, rows, width = queries.shape
    feats = proj_query.shape[1] // n_head

    def shape(*dims, dtype=low):
        return jax.ShapeDtypeStruct(dims, dtype)

    first = feats // 16 * 17 // 32 * 16
    partners = list(range(1, n_seq)) if direct else []
    n_copies = 1 + len(partners)
    *joined, grad_low, grad_high = kernel_call(
        functools.partial(join_kernel, n_copies),
        "join",
        [shape(held, 2 * kv_width)] * n_copies + [shape(rows // 2, width)] * 2,
        [HBM] * 3,
        [pltpu.SemaphoreType.DMA((4,))],
    )(*[in_hbm(x) for x in (keys, values, grad_out)])
    if direct:
        blocks = joined[-1:] + [swapped(x, "seq", r) for x, r in zip(joined, partners)]
    else:
        blocks = [lax.all_gather(joined[0], "seq", axis=0, tiled=True)]
    n_blocks, block_rows = len(blocks), blocks[0].shape[0]
    incoming = [shifted(part, "section", -1) for part in (grad_low, grad_high)]

    limit, q, *w_other = kernel_call(
        functools.partial(stage_kernel, n_head),
        "stage",
        [shape(8, HD, dtype=jnp.int32), shape(rows, width)] + [shape(feats, width)] * n_other,
        [HBM] * 4,
        [
            pltpu.SMEM(section_span.shape, jnp.int32),
            pltpu.SMEM(span_prefix.shape, jnp.int32),
            pltpu.SemaphoreType.DMA((1 + n_other,)),
            pltpu.SemaphoreType.DMA((2,)),
        ],
    )(*[in_hbm(x) for x in (section_span, span_prefix, queries, proj_query)])

    prefix = n_blocks * block_rows
    weights = shape(kv_width // HD, prefix, 2 * rows)
    grad_query, probs, dscores, *products = kernel_call(
        functools.partial(attention_kernel, partners, n_other),
        "attention",
        [shape(width, rows), weights, weights] + [shape(first, rows)] * n_other,
        [VMEM] * (4 + n_blocks + n_other),
    )(limit, q, *blocks, *incoming, *w_other)
    rest = kernel_call(
        functools.partial(rest_kernel, n_other),
        "rest",
        [shape(feats - first, rows)] * n_other,
        [VMEM] * (1 + n_other),
    )(grad_query, *w_other)
    arrived = [shifted(p, "head", r + 1) for part in (products, rest) for r, p in enumerate(part)]
    terms = kernel_call(
        terms_kernel, "terms", [shape(block_rows, 2 * kv_width)] * n_blocks, [VMEM] * 5
    )(probs, dscores, q, *incoming)
    if direct:
        sent = sorted(zip(partners, terms[1:]), key=lambda pair: -pair[0].bit_length())
        all_terms = [terms[0]] + [swapped(x, "seq", r) for r, x in sent]
    else:
        all_terms = [lax.psum_scatter(terms[0], "seq", scatter_dimension=0, tiled=True)]

    own = kernel_call(
        functools.partial(own_kernel, n_head),
        "own",
        shape(feats, rows, dtype=jnp.float32),
        [VMEM, HBM],
        [pltpu.VMEM((feats, width), low), pltpu.SemaphoreType.DMA(())],
    )(grad_query, in_hbm(proj_query))
    grad_key, grad_value = kernel_call(
        term_sum_kernel, "term_sum", [shape(1, held, kv_width)] * 2, [VMEM] * len(all_terms)
    )(*all_terms)
    grad_input = []
    for start, part in ((0, arrived[:n_other]), (first, arrived[n_other:])):
        grad_input = [
            pl.pallas_call(
                functools.partial(input_sum_kernel, n_other, start),
                out_shape=shape(1, feats, rows),
                in_specs=[VMEM] * (1 + n_other) + [HBM] * len(grad_input),
                out_specs=HBM,
                scratch_shapes=[pltpu.VMEM(part[0].shape, low), pltpu.SemaphoreType.DMA((2,))],
                input_output_aliases={1 + n_other: 0} if grad_input else {},
                compiler_params=pltpu.CompilerParams(vmem_limit_bytes=VMEM_LIMIT),
                name="input_sum",
            )(own, *part, *grad_input)
        ]
    grad_input = grad_input[0]
    return (grad_input, grad_key, grad_value)


def solution(mesh):
    in_specs = (
        P("section", "seq", "head"),
        P("section", "seq", "head"),
        P("section", "seq", "head"),
        P("section", "seq", "head"),
        P("section", None, "head"),
        P(),
        P(),
    )
    out_specs = (
        P("section", "head", "seq"),
        P("section", "seq", "head"),
        P("section", "seq", "head"),
    )
    return jax.shard_map(
        on_device, mesh=mesh, in_specs=in_specs, out_specs=out_specs, check_vma=False
    )
```

```python
import functools
import math

import jax
import jax.numpy as jnp
from jax import lax
from jax.experimental import pallas as pl
from jax.experimental.pallas import tpu as pltpu
from jax.sharding import PartitionSpec as P

HD = 128
MOST_PARTNERS = 4
VMEM_LIMIT = 40 * 1024 * 1024

query_scale = 168.0 ** (-0.5)
exp2_scale = query_scale * math.log2(math.e)


def shifted(block, axis, distance):
    devices = range(lax.axis_size(axis))
    route = [((i - distance) % len(devices), i) for i in devices]
    return lax.ppermute(block, axis, route)


def swapped(block, axis, distance):
    return lax.ppermute(block, axis, [(i, i ^ distance) for i in range(lax.axis_size(axis))])


def dot(left, right, left_dim, right_dim):
    return lax.dot_general(
        left, right, (((left_dim,), (right_dim,)), ((), ())), preferred_element_type=jnp.float32
    )


def in_hbm(x):
    return pltpu.with_memory_space_constraint(x, pltpu.HBM)


def join_kernel(n_copies, key_ref, value_ref, grad_ref, *refs):
    *outs, grad_low, grad_high, sems = refs
    width, rows = key_ref.shape[2], grad_low.shape[0]
    pairs = [
        (key_ref.at[0], outs[0].at[:, :width]),
        (value_ref.at[0], outs[0].at[:, width:]),
        (grad_ref.at[0, :rows, :], grad_low),
        (grad_ref.at[0, rows:, :], grad_high),
    ]
    copies = [pltpu.make_async_copy(a, b, sems.at[i]) for i, (a, b) in enumerate(pairs)]
    for copy in copies:
        copy.start()
    for copy in copies[:2]:
        copy.wait()
    for out in outs[1:]:
        out[...] = outs[0][...]
    for copy in copies[2:]:
        copy.wait()


def stage_kernel(n_head, span_ref, prefix_ref, q_ref, w_ref, limit_out, q_out, *refs):
    *other_outs, span, prefix, sems, small_sems = refs
    feats = w_ref.shape[1] // n_head
    head = lax.axis_index("head")
    copies = []
    for r, out in enumerate(other_outs):
        start = pl.multiple_of(lax.rem(head + r + 1, n_head) * feats, 16)
        copies.append((w_ref.at[0, pl.ds(start, feats), :], out))
    copies.append((q_ref.at[0], q_out))
    copies = [pltpu.make_async_copy(a, b, sems.at[i]) for i, (a, b) in enumerate(copies)]
    small = [
        pltpu.make_async_copy(a, b, small_sems.at[i])
        for i, (a, b) in enumerate([(span_ref, span), (prefix_ref, prefix)])
    ]
    for copy in small + copies:
        copy.start()
    for copy in small:
        copy.wait()
    live = prefix[span[lax.axis_index("section")]]
    limit_out[...] = jnp.full(limit_out.shape, live, jnp.int32)
    for copy in copies:
        copy.wait()


def pair_of(refs, g):
    cols = [slice((2 * g + i) * HD, (2 * g + i + 1) * HD) for i in range(2)]
    return jnp.concatenate([ref[:, c] for c in cols for ref in refs], axis=0)


def cols_of(g, start=0):
    return slice(start + g * HD, start + (g + 1) * HD)


def attention_kernel(partners, n_other, limit_ref, q_ref, *refs):
    n_blocks = 1 + len(partners)
    kv_refs = refs[:n_blocks]
    d_low, d_high, *refs = refs[n_blocks:]
    w_refs = refs[:n_other]
    grad_ref, probs_ref, dscores_ref, *part_refs = refs[n_other:]

    held, both = kv_refs[0].shape
    width = both // 2
    seq = lax.axis_index("seq")
    spots = []
    for r in [0, *partners]:
        first = jnp.bitwise_xor(seq, r) * held if partners else 0
        spots.append(first + lax.broadcasted_iota(jnp.int32, (held, 1), 0))
    alive = jnp.concatenate(spots, axis=0) < limit_ref[0:1, 0:1]

    rows = q_ref.shape[0]
    groups = range(width // HD)
    keys = [jnp.concatenate([ref[:, cols_of(g)] for ref in kv_refs], axis=0) for g in groups]
    scores = [dot(keys[g], pair_of((q_ref,), g), 1, 1) for g in groups]
    dprobs = []
    for g in groups:
        value = jnp.concatenate([ref[:, cols_of(g, width)] for ref in kv_refs], axis=0)
        dprobs.append(dot(value, pair_of((d_low, d_high), g), 1, 1))
    for g in groups:
        masked = jnp.where(alive, scores[g], jnp.float32(-1e30))
        top = jnp.max(masked, axis=0, keepdims=True)
        probs = jnp.exp2((masked - top) * exp2_scale)
        probs = probs * (1.0 / jnp.sum(probs, axis=0, keepdims=True))
        probs_low = probs.astype(jnp.bfloat16)
        delta = jnp.sum(probs_low.astype(jnp.float32) * dprobs[g], axis=0, keepdims=True)
        probs_ref[g] = probs_low
        dscores_ref[g] = (probs * (dprobs[g] - delta)).astype(jnp.bfloat16)
    for g in groups:
        grad_q = (query_scale * dot(keys[g], dscores_ref[g], 0, 0)).astype(jnp.bfloat16)
        for i in range(2):
            spot = (2 * g + i) * HD
            grad_ref[spot : spot + HD, :] = grad_q[:, i * rows : (i + 1) * rows]

    for w_ref, part_ref in zip(w_refs, part_refs):
        block = w_ref[: part_ref.shape[0], :]
        part_ref[...] = dot(block, grad_ref[...], 1, 0).astype(jnp.bfloat16)


def rest_kernel(n_other, start, grad_ref, *refs):
    w_refs, part_refs = refs[:n_other], refs[n_other:]
    while part_refs:
        count = part_refs[0].shape[0]
        for w_ref, part_ref in zip(w_refs, part_refs):
            block = w_ref[start : start + count, :]
            part_ref[...] = dot(block, grad_ref[...], 1, 0).astype(jnp.bfloat16)
        start, part_refs = start + count, part_refs[n_other:]


def terms_kernel(probs_ref, dscores_ref, q_ref, d_low, d_high, *term_refs):
    held, both = term_refs[0].shape
    width = both // 2
    for g in range(width // HD):
        grad_k = (query_scale * dot(dscores_ref[g], pair_of((q_ref,), g), 1, 0)).astype(jnp.bfloat16)
        grad_v = dot(probs_ref[g], pair_of((d_low, d_high), g), 1, 0).astype(jnp.bfloat16)
        for r, ref in enumerate(term_refs):
            block = slice(r * held, (r + 1) * held)
            ref[:, g * HD : (g + 1) * HD] = grad_k[block]
            ref[:, width + g * HD : width + (g + 1) * HD] = grad_v[block]


def own_kernel(n_head, grad_ref, w_ref, out_ref, w_held, sem):
    feats = out_ref.shape[0]
    start = pl.multiple_of(lax.axis_index("head") * feats, 16)
    copy = pltpu.make_async_copy(w_ref.at[0, pl.ds(start, feats), :], w_held, sem)
    copy.start()
    copy.wait()
    out_ref[...] = dot(w_held[...], grad_ref[...], 1, 0)


def input_sum_kernel(n_other, start, own_ref, *refs):
    arrived = refs[:n_other]
    *_, out_ref, held, sems = refs
    count = held.shape[0]
    middle = count // 32 * 16
    copies = []
    for i, (low, high) in enumerate(((0, middle), (middle, count))):
        at = slice(start + low, start + high)
        total = own_ref[at, :]
        for ref in arrived:
            total = total + ref[low:high, :].astype(jnp.float32)
        held[low:high, :] = total.astype(jnp.bfloat16)
        copy = pltpu.make_async_copy(held.at[low:high, :], out_ref.at[0, at, :], sems.at[i])
        copy.start()
        copies.append(copy)
    for copy in copies:
        copy.wait()


def term_sum_kernel(*refs):
    *terms, key_ref, value_ref = refs
    total = terms[0][...].astype(jnp.float32)
    for ref in terms[1:]:
        total = total + ref[...].astype(jnp.float32)
    low = total.astype(jnp.bfloat16)
    half = low.shape[1] // 2
    key_ref[0] = low[:, :half]
    value_ref[0] = low[:, half:]


VMEM = pl.BlockSpec(memory_space=pltpu.VMEM)
HBM = pl.BlockSpec(memory_space=pltpu.HBM)


def kernel_call(body, name, out_shape, in_specs, scratch=(), limit=VMEM_LIMIT):
    return pl.pallas_call(
        body,
        out_shape=out_shape,
        in_specs=in_specs,
        out_specs=jax.tree.map(lambda _: VMEM, out_shape),
        scratch_shapes=list(scratch),
        compiler_params=pltpu.CompilerParams(vmem_limit_bytes=limit),
        name=name,
    )


def on_device(queries, grad_out, keys, values, proj_query, section_span, span_prefix):
    n_seq, n_head = lax.axis_size("seq"), lax.axis_size("head")
    n_other = n_head - 1
    direct = n_seq <= MOST_PARTNERS and n_seq & (n_seq - 1) == 0
    low = jnp.bfloat16
    _, held, kv_width = keys.shape
    _, rows, width = queries.shape
    feats = proj_query.shape[1] // n_head

    def shape(*dims, dtype=low):
        return jax.ShapeDtypeStruct(dims, dtype)

    first = feats // 16 * 35 // 100 * 16
    second = (feats - first) // 32 * 16
    parts = [first, feats - first - second, second]
    partners = list(range(1, n_seq)) if direct else []
    n_copies = 1 + len(partners)
    *joined, grad_low, grad_high = kernel_call(
        functools.partial(join_kernel, n_copies),
        "join",
        [shape(held, 2 * kv_width)] * n_copies + [shape(rows // 2, width)] * 2,
        [HBM] * 3,
        [pltpu.SemaphoreType.DMA((4,))],
    )(*[in_hbm(x) for x in (keys, values, grad_out)])
    if direct:
        blocks = joined[-1:] + [swapped(x, "seq", r) for x, r in zip(joined, partners)]
    else:
        blocks = [lax.all_gather(joined[0], "seq", axis=0, tiled=True)]
    n_blocks, block_rows = len(blocks), blocks[0].shape[0]
    incoming = [shifted(part, "section", -1) for part in (grad_low, grad_high)]

    limit, q, *w_other = kernel_call(
        functools.partial(stage_kernel, n_head),
        "stage",
        [shape(8, HD, dtype=jnp.int32), shape(rows, width)] + [shape(feats, width)] * n_other,
        [HBM] * 4,
        [
            pltpu.SMEM(section_span.shape, jnp.int32),
            pltpu.SMEM(span_prefix.shape, jnp.int32),
            pltpu.SemaphoreType.DMA((1 + n_other,)),
            pltpu.SemaphoreType.DMA((2,)),
        ],
    )(*[in_hbm(x) for x in (section_span, span_prefix, queries, proj_query)])

    prefix = n_blocks * block_rows
    weights = shape(kv_width // HD, prefix, 2 * rows)
    grad_query, probs, dscores, *products = kernel_call(
        functools.partial(attention_kernel, partners, n_other),
        "attention",
        [shape(width, rows), weights, weights] + [shape(first, rows)] * n_other,
        [VMEM] * (4 + n_blocks + n_other),
    )(limit, q, *blocks, *incoming, *w_other)
    rest = kernel_call(
        functools.partial(rest_kernel, n_other, first),
        "rest",
        [shape(count, rows) for count in parts[1:] for _ in range(n_other)],
        [VMEM] * (1 + n_other),
    )(grad_query, *w_other)
    products = [*products, *rest]
    arrived = [shifted(p, "head", i % n_other + 1) for i, p in enumerate(products)]
    terms = kernel_call(
        terms_kernel, "terms", [shape(block_rows, 2 * kv_width)] * n_blocks, [VMEM] * 5
    )(probs, dscores, q, *incoming)
    if direct:
        sent = sorted(zip(partners, terms[1:]), key=lambda pair: -pair[0].bit_length())
        all_terms = [terms[0]] + [swapped(x, "seq", r) for r, x in sent]
    else:
        all_terms = [lax.psum_scatter(terms[0], "seq", scatter_dimension=0, tiled=True)]

    own = kernel_call(
        functools.partial(own_kernel, n_head),
        "own",
        shape(feats, rows, dtype=jnp.float32),
        [VMEM, HBM],
        [pltpu.VMEM((feats, width), low), pltpu.SemaphoreType.DMA(())],
    )(grad_query, in_hbm(proj_query))
    grad_key, grad_value = kernel_call(
        term_sum_kernel, "term_sum", [shape(1, held, kv_width)] * 2, [VMEM] * len(all_terms)
    )(*all_terms)
    grad_input = []
    for i in range(len(parts)):
        start, part = sum(parts[:i]), arrived[i * n_other : (i + 1) * n_other]
        grad_input = [
            pl.pallas_call(
                functools.partial(input_sum_kernel, n_other, start),
                out_shape=shape(1, feats, rows),
                in_specs=[VMEM] * (1 + n_other) + [HBM] * len(grad_input),
                out_specs=HBM,
                scratch_shapes=[pltpu.VMEM(part[0].shape, low), pltpu.SemaphoreType.DMA((2,))],
                input_output_aliases={1 + n_other: 0} if grad_input else {},
                compiler_params=pltpu.CompilerParams(vmem_limit_bytes=VMEM_LIMIT),
                name="input_sum",
            )(own, *part, *grad_input)
        ]
    grad_input = grad_input[0]
    return (grad_input, grad_key, grad_value)


def solution(mesh):
    in_specs = (
        P("section", "seq", "head"),
        P("section", "seq", "head"),
        P("section", "seq", "head"),
        P("section", "seq", "head"),
        P("section", None, "head"),
        P(),
        P(),
    )
    out_specs = (
        P("section", "head", "seq"),
        P("section", "seq", "head"),
        P("section", "seq", "head"),
    )
    return jax.shard_map(
        on_device, mesh=mesh, in_specs=in_specs, out_specs=out_specs, check_vma=False
    )
```

```python
import functools
import math

import jax
import jax.numpy as jnp
from jax import lax
from jax.experimental import pallas as pl
from jax.experimental.pallas import tpu as pltpu
from jax.sharding import PartitionSpec as P

HD = 128
MOST_PARTNERS = 4
VMEM_LIMIT = 40 * 1024 * 1024

query_scale = 168.0 ** (-0.5)
exp2_scale = query_scale * math.log2(math.e)


def shifted(block, axis, distance):
    devices = range(lax.axis_size(axis))
    route = [((i - distance) % len(devices), i) for i in devices]
    return lax.ppermute(block, axis, route)


def swapped(block, axis, distance):
    return lax.ppermute(block, axis, [(i, i ^ distance) for i in range(lax.axis_size(axis))])


def dot(left, right, left_dim, right_dim):
    return lax.dot_general(
        left, right, (((left_dim,), (right_dim,)), ((), ())), preferred_element_type=jnp.float32
    )


def in_hbm(x):
    return pltpu.with_memory_space_constraint(x, pltpu.HBM)


def join_kernel(n_copies, key_ref, value_ref, grad_ref, *refs):
    *outs, grad_low, grad_high, sems = refs
    width, rows = key_ref.shape[2], grad_low.shape[0]
    pairs = [
        (key_ref.at[0], outs[0].at[:, :width]),
        (value_ref.at[0], outs[0].at[:, width:]),
        (grad_ref.at[0, :rows, :], grad_low),
        (grad_ref.at[0, rows:, :], grad_high),
    ]
    copies = [pltpu.make_async_copy(a, b, sems.at[i]) for i, (a, b) in enumerate(pairs)]
    for copy in copies:
        copy.start()
    for copy in copies[:2]:
        copy.wait()
    for out in outs[1:]:
        out[...] = outs[0][...]
    for copy in copies[2:]:
        copy.wait()


def stage_kernel(n_head, span_ref, prefix_ref, q_ref, w_ref, limit_out, q_out, *refs):
    *other_outs, span, prefix, sems, small_sems = refs
    feats = w_ref.shape[1] // n_head
    head = lax.axis_index("head")
    copies = []
    for r, out in enumerate(other_outs):
        start = pl.multiple_of(lax.rem(head + r + 1, n_head) * feats, 16)
        copies.append((w_ref.at[0, pl.ds(start, feats), :], out))
    copies.append((q_ref.at[0], q_out))
    copies = [pltpu.make_async_copy(a, b, sems.at[i]) for i, (a, b) in enumerate(copies)]
    small = [
        pltpu.make_async_copy(a, b, small_sems.at[i])
        for i, (a, b) in enumerate([(span_ref, span), (prefix_ref, prefix)])
    ]
    for copy in small + copies:
        copy.start()
    for copy in small:
        copy.wait()
    live = prefix[span[lax.axis_index("section")]]
    limit_out[...] = jnp.full(limit_out.shape, live, jnp.int32)
    for copy in copies:
        copy.wait()


def pair_of(refs, g):
    cols = [slice((2 * g + i) * HD, (2 * g + i + 1) * HD) for i in range(2)]
    return jnp.concatenate([ref[:, c] for c in cols for ref in refs], axis=0)


def cols_of(g, start=0):
    return slice(start + g * HD, start + (g + 1) * HD)


def attention_kernel(partners, n_other, limit_ref, q_ref, *refs):
    n_blocks = 1 + len(partners)
    kv_refs = refs[:n_blocks]
    d_low, d_high, *refs = refs[n_blocks:]
    w_refs = refs[:n_other]
    grad_ref, probs_ref, dscores_ref, *part_refs = refs[n_other:]

    held, both = kv_refs[0].shape
    width = both // 2
    seq = lax.axis_index("seq")
    spots = []
    for r in [0, *partners]:
        first = jnp.bitwise_xor(seq, r) * held if partners else 0
        spots.append(first + lax.broadcasted_iota(jnp.int32, (held, 1), 0))
    alive = jnp.concatenate(spots, axis=0) < limit_ref[0:1, 0:1]

    rows = q_ref.shape[0]
    groups = range(width // HD)
    keys = [jnp.concatenate([ref[:, cols_of(g)] for ref in kv_refs], axis=0) for g in groups]
    scores = [dot(keys[g], pair_of((q_ref,), g), 1, 1) for g in groups]
    dprobs = []
    for g in groups:
        value = jnp.concatenate([ref[:, cols_of(g, width)] for ref in kv_refs], axis=0)
        dprobs.append(dot(value, pair_of((d_low, d_high), g), 1, 1))
    for g in groups:
        masked = jnp.where(alive, scores[g], jnp.float32(-1e30))
        top = jnp.max(masked, axis=0, keepdims=True)
        probs = jnp.exp2((masked - top) * exp2_scale)
        probs = probs * (1.0 / jnp.sum(probs, axis=0, keepdims=True))
        probs_low = probs.astype(jnp.bfloat16)
        delta = jnp.sum(probs_low.astype(jnp.float32) * dprobs[g], axis=0, keepdims=True)
        probs_ref[g] = probs_low
        dscores_ref[g] = (probs * (dprobs[g] - delta)).astype(jnp.bfloat16)
    for g in groups:
        grad_q = (query_scale * dot(keys[g], dscores_ref[g], 0, 0)).astype(jnp.bfloat16)
        for i in range(2):
            spot = (2 * g + i) * HD
            grad_ref[spot : spot + HD, :] = grad_q[:, i * rows : (i + 1) * rows]

    for w_ref, part_ref in zip(w_refs, part_refs):
        block = w_ref[: part_ref.shape[0], :]
        part_ref[...] = dot(block, grad_ref[...], 1, 0).astype(jnp.bfloat16)


def terms_kernel(probs_ref, dscores_ref, q_ref, d_low, d_high, *term_refs):
    held, both = term_refs[0].shape
    width = both // 2
    for g in range(width // HD):
        grad_k = (query_scale * dot(dscores_ref[g], pair_of((q_ref,), g), 1, 0)).astype(jnp.bfloat16)
        grad_v = dot(probs_ref[g], pair_of((d_low, d_high), g), 1, 0).astype(jnp.bfloat16)
        for r, ref in enumerate(term_refs):
            block = slice(r * held, (r + 1) * held)
            ref[:, g * HD : (g + 1) * HD] = grad_k[block]
            ref[:, width + g * HD : width + (g + 1) * HD] = grad_v[block]


def own_kernel(n_head, grad_ref, w_ref, out_ref, w_held, sem):
    feats = out_ref.shape[0]
    start = pl.multiple_of(lax.axis_index("head") * feats, 16)
    copy = pltpu.make_async_copy(w_ref.at[0, pl.ds(start, feats), :], w_held, sem)
    copy.start()
    copy.wait()
    out_ref[...] = dot(w_held[...], grad_ref[...], 1, 0)


def input_sum_kernel(n_other, start, own_ref, *refs):
    arrived = refs[:n_other]
    *_, out_ref, held, sems = refs
    count = held.shape[0]
    middle = count // 32 * 16
    copies = []
    for i, (low, high) in enumerate(((0, middle), (middle, count))):
        at = slice(start + low, start + high)
        total = own_ref[at, :]
        for ref in arrived:
            total = total + ref[low:high, :].astype(jnp.float32)
        held[low:high, :] = total.astype(jnp.bfloat16)
        copy = pltpu.make_async_copy(held.at[low:high, :], out_ref.at[0, at, :], sems.at[i])
        copy.start()
        copies.append(copy)
    for copy in copies:
        copy.wait()


def term_sum_kernel(*refs):
    *terms, key_ref, value_ref = refs
    total = terms[0][...].astype(jnp.float32)
    for ref in terms[1:]:
        total = total + ref[...].astype(jnp.float32)
    low = total.astype(jnp.bfloat16)
    half = low.shape[1] // 2
    key_ref[0] = low[:, :half]
    value_ref[0] = low[:, half:]


VMEM = pl.BlockSpec(memory_space=pltpu.VMEM)
HBM = pl.BlockSpec(memory_space=pltpu.HBM)


def kernel_call(body, name, out_shape, in_specs, scratch=(), limit=VMEM_LIMIT):
    return pl.pallas_call(
        body,
        out_shape=out_shape,
        in_specs=in_specs,
        out_specs=jax.tree.map(lambda _: VMEM, out_shape),
        scratch_shapes=list(scratch),
        compiler_params=pltpu.CompilerParams(vmem_limit_bytes=limit),
        name=name,
    )


def on_device(queries, grad_out, keys, values, proj_query, section_span, span_prefix):
    n_seq, n_head = lax.axis_size("seq"), lax.axis_size("head")
    n_other = n_head - 1
    direct = n_seq <= MOST_PARTNERS and n_seq & (n_seq - 1) == 0
    low = jnp.bfloat16
    _, held, kv_width = keys.shape
    _, rows, width = queries.shape
    feats = proj_query.shape[1] // n_head

    def shape(*dims, dtype=low):
        return jax.ShapeDtypeStruct(dims, dtype)

    partners = list(range(1, n_seq)) if direct else []
    n_copies = 1 + len(partners)
    *joined, grad_low, grad_high = kernel_call(
        functools.partial(join_kernel, n_copies),
        "join",
        [shape(held, 2 * kv_width)] * n_copies + [shape(rows // 2, width)] * 2,
        [HBM] * 3,
        [pltpu.SemaphoreType.DMA((4,))],
    )(*[in_hbm(x) for x in (keys, values, grad_out)])
    if direct:
        blocks = joined[-1:] + [swapped(x, "seq", r) for x, r in zip(joined, partners)]
    else:
        blocks = [lax.all_gather(joined[0], "seq", axis=0, tiled=True)]
    n_blocks, block_rows = len(blocks), blocks[0].shape[0]
    incoming = [shifted(part, "section", -1) for part in (grad_low, grad_high)]

    limit, q, *w_other = kernel_call(
        functools.partial(stage_kernel, n_head),
        "stage",
        [shape(8, HD, dtype=jnp.int32), shape(rows, width)] + [shape(feats, width)] * n_other,
        [HBM] * 4,
        [
            pltpu.SMEM(section_span.shape, jnp.int32),
            pltpu.SMEM(span_prefix.shape, jnp.int32),
            pltpu.SemaphoreType.DMA((1 + n_other,)),
            pltpu.SemaphoreType.DMA((2,)),
        ],
    )(*[in_hbm(x) for x in (section_span, span_prefix, queries, proj_query)])

    prefix = n_blocks * block_rows
    weights = shape(kv_width // HD, prefix, 2 * rows)
    grad_query, probs, dscores, *products = kernel_call(
        functools.partial(attention_kernel, partners, n_other),
        "attention",
        [shape(width, rows), weights, weights] + [shape(feats, rows)] * n_other,
        [VMEM] * (4 + n_blocks + n_other),
    )(limit, q, *blocks, *incoming, *w_other)
    arrived = [shifted(part, "head", r + 1) for r, part in enumerate(products)]
    terms = kernel_call(
        terms_kernel, "terms", [shape(block_rows, 2 * kv_width)] * n_blocks, [VMEM] * 5
    )(probs, dscores, q, *incoming)
    if direct:
        sent = sorted(zip(partners, terms[1:]), key=lambda pair: -pair[0].bit_length())
        all_terms = [terms[0]] + [swapped(x, "seq", r) for r, x in sent]
    else:
        all_terms = [lax.psum_scatter(terms[0], "seq", scatter_dimension=0, tiled=True)]

    own = kernel_call(
        functools.partial(own_kernel, n_head),
        "own",
        shape(feats, rows, dtype=jnp.float32),
        [VMEM, HBM],
        [pltpu.VMEM((feats, width), low), pltpu.SemaphoreType.DMA(())],
    )(grad_query, in_hbm(proj_query))
    grad_key, grad_value = kernel_call(
        term_sum_kernel, "term_sum", [shape(1, held, kv_width)] * 2, [VMEM] * len(all_terms)
    )(*all_terms)
    grad_input = pl.pallas_call(
        functools.partial(input_sum_kernel, n_other, 0),
        out_shape=shape(1, feats, rows),
        in_specs=[VMEM] * (1 + n_other),
        out_specs=HBM,
        scratch_shapes=[pltpu.VMEM((feats, rows), low), pltpu.SemaphoreType.DMA((2,))],
        compiler_params=pltpu.CompilerParams(vmem_limit_bytes=VMEM_LIMIT),
        name="input_sum",
    )(own, *arrived)
    return (grad_input, grad_key, grad_value)


def solution(mesh):
    in_specs = (
        P("section", "seq", "head"),
        P("section", "seq", "head"),
        P("section", "seq", "head"),
        P("section", "seq", "head"),
        P("section", None, "head"),
        P(),
        P(),
    )
    out_specs = (
        P("section", "head", "seq"),
        P("section", "seq", "head"),
        P("section", "seq", "head"),
    )
    return jax.shard_map(
        on_device, mesh=mesh, in_specs=in_specs, out_specs=out_specs, check_vma=False
    )
```

```python
import functools
import math

import jax
import jax.numpy as jnp
from jax import lax
from jax.experimental import pallas as pl
from jax.experimental.pallas import tpu as pltpu
from jax.sharding import PartitionSpec as P

HD = 128
MOST_PARTNERS = 4
VMEM_LIMIT = 40 * 1024 * 1024

query_scale = 168.0 ** (-0.5)
exp2_scale = query_scale * math.log2(math.e)


def shifted(block, axis, distance):
    devices = range(lax.axis_size(axis))
    route = [((i - distance) % len(devices), i) for i in devices]
    return lax.ppermute(block, axis, route)


def swapped(block, axis, distance):
    return lax.ppermute(block, axis, [(i, i ^ distance) for i in range(lax.axis_size(axis))])


def dot(left, right, left_dim, right_dim):
    return lax.dot_general(
        left, right, (((left_dim,), (right_dim,)), ((), ())), preferred_element_type=jnp.float32
    )


def in_hbm(x):
    return pltpu.with_memory_space_constraint(x, pltpu.HBM)


def join_kernel(n_copies, key_ref, value_ref, grad_ref, *refs):
    *outs, grad_low, grad_high, sems = refs
    width, rows = key_ref.shape[2], grad_low.shape[0]
    pairs = [
        (key_ref.at[0], outs[0].at[:, :width]),
        (value_ref.at[0], outs[0].at[:, width:]),
        (grad_ref.at[0, :rows, :], grad_low),
        (grad_ref.at[0, rows:, :], grad_high),
    ]
    copies = [pltpu.make_async_copy(a, b, sems.at[i]) for i, (a, b) in enumerate(pairs)]
    for copy in copies:
        copy.start()
    for copy in copies[:2]:
        copy.wait()
    for out in outs[1:]:
        out[...] = outs[0][...]
    for copy in copies[2:]:
        copy.wait()


def stage_kernel(n_head, span_ref, prefix_ref, q_ref, w_ref, limit_out, q_out, *refs):
    *other_outs, span, prefix, sems, small_sems = refs
    feats = w_ref.shape[1] // n_head
    head = lax.axis_index("head")
    copies = []
    for r, out in enumerate(other_outs):
        start = pl.multiple_of(lax.rem(head + r + 1, n_head) * feats, 16)
        copies.append((w_ref.at[0, pl.ds(start, feats), :], out))
    copies.append((q_ref.at[0], q_out))
    copies = [pltpu.make_async_copy(a, b, sems.at[i]) for i, (a, b) in enumerate(copies)]
    small = [
        pltpu.make_async_copy(a, b, small_sems.at[i])
        for i, (a, b) in enumerate([(span_ref, span), (prefix_ref, prefix)])
    ]
    for copy in small + copies:
        copy.start()
    for copy in small:
        copy.wait()
    live = prefix[span[lax.axis_index("section")]]
    limit_out[...] = jnp.full(limit_out.shape, live, jnp.int32)
    for copy in copies:
        copy.wait()


def pair_of(refs, g):
    cols = [slice((2 * g + i) * HD, (2 * g + i + 1) * HD) for i in range(2)]
    return jnp.concatenate([ref[:, c] for c in cols for ref in refs], axis=0)


def cols_of(g, start=0):
    return slice(start + g * HD, start + (g + 1) * HD)


def attention_kernel(partners, n_other, limit_ref, q_ref, *refs):
    most = 1 + len(partners[:-1])
    kv_refs, (d_low, d_high), refs = refs[:most], refs[most : most + 2], refs[most + 2 :]
    if partners:
        kv_refs, refs = kv_refs + refs[:1], refs[1:]
    w_refs = refs[:n_other]
    grad_ref, probs_ref, dscores_ref, *part_refs = refs[n_other:]

    held, both = kv_refs[0].shape
    width = both // 2
    seq = lax.axis_index("seq")
    spots = []
    for r in [0, *partners]:
        first = jnp.bitwise_xor(seq, r) * held if partners else 0
        spots.append(first + lax.broadcasted_iota(jnp.int32, (held, 1), 0))
    alive = jnp.concatenate(spots, axis=0) < limit_ref[0:1, 0:1]

    rows = q_ref.shape[0]
    groups = range(width // HD)
    keys = [jnp.concatenate([ref[:, cols_of(g)] for ref in kv_refs], axis=0) for g in groups]
    scores = [dot(keys[g], pair_of((q_ref,), g), 1, 1) for g in groups]
    dprobs = []
    for g in groups:
        value = jnp.concatenate([ref[:, cols_of(g, width)] for ref in kv_refs], axis=0)
        dprobs.append(dot(value, pair_of((d_low, d_high), g), 1, 1))
    for g in groups:
        masked = jnp.where(alive, scores[g], jnp.float32(-1e30))
        top = jnp.max(masked, axis=0, keepdims=True)
        probs = jnp.exp2((masked - top) * exp2_scale)
        probs = probs * (1.0 / jnp.sum(probs, axis=0, keepdims=True))
        probs_low = probs.astype(jnp.bfloat16)
        delta = jnp.sum(probs_low.astype(jnp.float32) * dprobs[g], axis=0, keepdims=True)
        probs_ref[g] = probs_low
        dscores_ref[g] = (probs * (dprobs[g] - delta)).astype(jnp.bfloat16)
    for g in groups:
        grad_q = (query_scale * dot(keys[g], dscores_ref[g], 0, 0)).astype(jnp.bfloat16)
        for i in range(2):
            spot = (2 * g + i) * HD
            grad_ref[spot : spot + HD, :] = grad_q[:, i * rows : (i + 1) * rows]

    for w_ref, part_ref in zip(w_refs, part_refs):
        block = w_ref[: part_ref.shape[0], :]
        part_ref[...] = dot(block, grad_ref[...], 1, 0).astype(jnp.bfloat16)


def rest_kernel(n_other, grad_ref, *refs):
    for w_ref, part_ref in zip(refs[:n_other], refs[n_other:]):
        block = w_ref[w_ref.shape[0] - part_ref.shape[0] :, :]
        part_ref[...] = dot(block, grad_ref[...], 1, 0).astype(jnp.bfloat16)


def terms_kernel(probs_ref, dscores_ref, q_ref, d_low, d_high, *term_refs):
    held, both = term_refs[0].shape
    width = both // 2
    for g in range(width // HD):
        grad_k = (query_scale * dot(dscores_ref[g], pair_of((q_ref,), g), 1, 0)).astype(jnp.bfloat16)
        grad_v = dot(probs_ref[g], pair_of((d_low, d_high), g), 1, 0).astype(jnp.bfloat16)
        for r, ref in enumerate(term_refs):
            block = slice(r * held, (r + 1) * held)
            ref[:, g * HD : (g + 1) * HD] = grad_k[block]
            ref[:, width + g * HD : width + (g + 1) * HD] = grad_v[block]


def own_kernel(n_head, grad_ref, w_ref, out_ref, w_held, sem):
    feats = out_ref.shape[0]
    start = pl.multiple_of(lax.axis_index("head") * feats, 16)
    copy = pltpu.make_async_copy(w_ref.at[0, pl.ds(start, feats), :], w_held, sem)
    copy.start()
    copy.wait()
    out_ref[...] = dot(w_held[...], grad_ref[...], 1, 0)


def input_sum_kernel(n_other, start, own_ref, *refs):
    arrived = refs[:n_other]
    *_, out_ref, held, sem = refs
    at = slice(start, start + held.shape[0])
    total = own_ref[at, :]
    for ref in arrived:
        total = total + ref[...].astype(jnp.float32)
    held[...] = total.astype(jnp.bfloat16)
    copy = pltpu.make_async_copy(held, out_ref.at[0, at, :], sem)
    copy.start()
    copy.wait()


def term_sum_kernel(*refs):
    *terms, key_ref, value_ref = refs
    total = terms[0][...].astype(jnp.float32)
    for ref in terms[1:]:
        total = total + ref[...].astype(jnp.float32)
    low = total.astype(jnp.bfloat16)
    half = low.shape[1] // 2
    key_ref[0] = low[:, :half]
    value_ref[0] = low[:, half:]


VMEM = pl.BlockSpec(memory_space=pltpu.VMEM)
HBM = pl.BlockSpec(memory_space=pltpu.HBM)


def kernel_call(body, name, out_shape, in_specs, scratch=(), limit=VMEM_LIMIT):
    return pl.pallas_call(
        body,
        out_shape=out_shape,
        in_specs=in_specs,
        out_specs=jax.tree.map(lambda _: VMEM, out_shape),
        scratch_shapes=list(scratch),
        compiler_params=pltpu.CompilerParams(vmem_limit_bytes=limit),
        name=name,
    )


def on_device(queries, grad_out, keys, values, proj_query, section_span, span_prefix):
    n_seq, n_head = lax.axis_size("seq"), lax.axis_size("head")
    n_other = n_head - 1
    direct = n_seq <= MOST_PARTNERS and n_seq & (n_seq - 1) == 0
    low = jnp.bfloat16
    _, held, kv_width = keys.shape
    _, rows, width = queries.shape
    feats = proj_query.shape[1] // n_head

    def shape(*dims, dtype=low):
        return jax.ShapeDtypeStruct(dims, dtype)

    first = feats // 16 * 17 // 32 * 16
    partners = list(range(1, n_seq)) if direct else []
    n_copies = 1 + len(partners)
    *joined, grad_low, grad_high = kernel_call(
        functools.partial(join_kernel, n_copies),
        "join",
        [shape(held, 2 * kv_width)] * n_copies + [shape(rows // 2, width)] * 2,
        [HBM] * 3,
        [pltpu.SemaphoreType.DMA((4,))],
    )(*[in_hbm(x) for x in (keys, values, grad_out)])
    if direct:
        blocks = joined[-1:] + [swapped(x, "seq", r) for x, r in zip(joined, partners[:-1])]
    else:
        blocks = [lax.all_gather(joined[0], "seq", axis=0, tiled=True)]
    incoming = [shifted(part, "section", -1) for part in (grad_low, grad_high)]
    last = [swapped(joined[len(partners) - 1], "seq", r) for r in partners[-1:]]
    n_blocks, block_rows = len(blocks) + len(last), blocks[0].shape[0]

    limit, q, *w_other = kernel_call(
        functools.partial(stage_kernel, n_head),
        "stage",
        [shape(8, HD, dtype=jnp.int32), shape(rows, width)] + [shape(feats, width)] * n_other,
        [HBM] * 4,
        [
            pltpu.SMEM(section_span.shape, jnp.int32),
            pltpu.SMEM(span_prefix.shape, jnp.int32),
            pltpu.SemaphoreType.DMA((1 + n_other,)),
            pltpu.SemaphoreType.DMA((2,)),
        ],
    )(*[in_hbm(x) for x in (section_span, span_prefix, queries, proj_query)])

    prefix = n_blocks * block_rows
    weights = shape(kv_width // HD, prefix, 2 * rows)
    grad_query, probs, dscores, *products = kernel_call(
        functools.partial(attention_kernel, partners, n_other),
        "attention",
        [shape(width, rows), weights, weights] + [shape(first, rows)] * n_other,
        [VMEM] * (4 + n_blocks + n_other),
    )(limit, q, *blocks, *incoming, *last, *w_other)
    rest = kernel_call(
        functools.partial(rest_kernel, n_other),
        "rest",
        [shape(feats - first, rows)] * n_other,
        [VMEM] * (1 + n_other),
    )(grad_query, *w_other)
    arrived = [shifted(p, "head", r + 1) for part in (products, rest) for r, p in enumerate(part)]
    terms = kernel_call(
        terms_kernel, "terms", [shape(block_rows, 2 * kv_width)] * n_blocks, [VMEM] * 5
    )(probs, dscores, q, *incoming)
    if direct:
        sent = sorted(zip(partners, terms[1:]), key=lambda pair: -pair[0])
        all_terms = [terms[0]] + [swapped(x, "seq", r) for r, x in sent]
    else:
        all_terms = [lax.psum_scatter(terms[0], "seq", scatter_dimension=0, tiled=True)]

    own = kernel_call(
        functools.partial(own_kernel, n_head),
        "own",
        shape(feats, rows, dtype=jnp.float32),
        [VMEM, HBM],
        [pltpu.VMEM((feats, width), low), pltpu.SemaphoreType.DMA(())],
    )(grad_query, in_hbm(proj_query))
    grad_key, grad_value = kernel_call(
        term_sum_kernel, "term_sum", [shape(1, held, kv_width)] * 2, [VMEM] * len(all_terms)
    )(*all_terms)
    grad_input = []
    for start, part in ((0, arrived[:n_other]), (first, arrived[n_other:])):
        grad_input = [
            pl.pallas_call(
                functools.partial(input_sum_kernel, n_other, start),
                out_shape=shape(1, feats, rows),
                in_specs=[VMEM] * (1 + n_other) + [HBM] * len(grad_input),
                out_specs=HBM,
                scratch_shapes=[pltpu.VMEM(part[0].shape, low), pltpu.SemaphoreType.DMA(())],
                input_output_aliases={1 + n_other: 0} if grad_input else {},
                compiler_params=pltpu.CompilerParams(vmem_limit_bytes=VMEM_LIMIT),
                name="input_sum",
            )(own, *part, *grad_input)
        ]
    grad_input = grad_input[0]
    return (grad_input, grad_key, grad_value)


def solution(mesh):
    in_specs = (
        P("section", "seq", "head"),
        P("section", "seq", "head"),
        P("section", "seq", "head"),
        P("section", "seq", "head"),
        P("section", None, "head"),
        P(),
        P(),
    )
    out_specs = (
        P("section", "head", "seq"),
        P("section", "seq", "head"),
        P("section", "seq", "head"),
    )
    return jax.shard_map(
        on_device, mesh=mesh, in_specs=in_specs, out_specs=out_specs, check_vma=False
    )
```
